32 devices in a mesh: section: 4 (over y, x), dp: 8 (over z, core).
Axes of the slice: x: 2, y: 2, z: 4, core: 2. Of those that a mesh axis runs over, the one named last changes fastest.
Arguments:
- inputs: bfloat16 [32, 1024, 512], P('dp'), may hold values from -6 to 6
- cotangent: bfloat16 [32, 1024, 512], P('dp'), may hold values from -6 to 6
- query_counts: int32 [32], P('dp'), may hold values from 1 to 128, as said below
- section_weight: bfloat16 [4, 512, 2048], P('section', 'dp')
- section_bias: bfloat16 [4, 1536], P('section', 'dp')
- section_norm: bfloat16 [4, 2, 512], P('section', None, 'dp')
Outputs:
- activations: bfloat16 [4, 32, 1024, 512], P('section', 'dp')
- input_grads: bfloat16 [4, 32, 1024, 512], P('section', 'dp')
- weight_grads: float32 [4, 512, 2048], P('section', 'dp')
- bias_grads: float32 [4, 1536], P('section', 'dp')
- norm_grads: float32 [4, 2, 512], P('section', None, 'dp')
The draws below stay inside these ranges and needn't reach their ends.
Inputs may be any that keep to these rules, and one draw needn't show every extreme that they name: `query_counts`: live queries of each neighbourhood; some neighbourhood has 128 and some has 1.
All inputs are finite; a program needn't handle non-finite values.
Results may differ from the reference program's by a relative error of at most 0.024.
Values may be sent and summed in bfloat16 or wider, within the bound.
A program may use at most 128 MiB of HBM per device.

```python
import math
import jax
import jax.numpy as jnp
from jax import lax

D = 512
HEADS = 4
HEAD = 128
FF = 1024
CTX = 896
QMAX = 128
NB = 32


def draw_query_counts(key, part):
    key = jax.random.fold_in(key, 11)
    first_key, second_key, third_key = jax.random.split(key, 3)
    counts = jax.random.randint(first_key, (NB,), 1, QMAX + 1, dtype=jnp.int32)
    top_slot = jax.random.randint(second_key, (), 0, NB, dtype=jnp.int32)
    offset = jax.random.randint(third_key, (), 1, NB, dtype=jnp.int32)
    bottom_slot = (top_slot + offset) % NB
    index_all = jnp.arange(NB, dtype=jnp.int32)
    counts = jnp.where(index_all == top_slot, QMAX, counts)
    counts = jnp.where(index_all == bottom_slot, 1, counts)
    return counts


def draw_section_weight(key, part):
    key = jax.random.fold_in(key, 23)
    samples = jax.random.normal(key, (4, D, 4 * D), jnp.float32)
    column = jnp.arange(4 * D)
    attend_scale = jnp.where(column < D, 1.5, jnp.where(column < 3 * D, 1.0, 10.0)) / math.sqrt(D)
    feed_scale = jnp.where(column < FF, 1.0 / math.sqrt(D), 1.5 / math.sqrt(FF))
    section_index = jnp.arange(4)[:, None]
    scales = jnp.where(section_index % 2 == 0, attend_scale[None, :], feed_scale[None, :])
    return (samples * scales[:, None, :]).astype(jnp.bfloat16)


def draw_section_bias(key, part):
    key = jax.random.fold_in(key, 37)
    samples = jax.random.normal(key, (4, 3 * D), jnp.float32)
    column = jnp.arange(3 * D)
    attend_scale = jnp.where((column >= D) & (column < 2 * D), 0.02, 0.2)
    section_index = jnp.arange(4)[:, None]
    scales = jnp.where(section_index % 2 == 0, attend_scale[None, :], 0.2)
    return (samples * scales).astype(jnp.bfloat16)


def draw_section_norm(key, part):
    key = jax.random.fold_in(key, 41)
    gain_key, shift_key = jax.random.split(key)
    gains = 0.8 + 0.4 * jax.random.uniform(gain_key, (4, D), jnp.float32)
    shifts = 0.2 * jax.random.normal(shift_key, (4, D), jnp.float32)
    return jnp.stack([gains, shifts], axis=1).astype(jnp.bfloat16)


def block_levels(rng, extent, cuts, smallest, top_value):
    gain = 1.0
    for dim, shards_of in cuts:
        heights = jax.random.uniform(jax.random.fold_in(jax.random.fold_in(rng, 6), dim), (shards_of,), jnp.float32, smallest / len(cuts), top_value / len(cuts))
        gain = gain * jnp.repeat(jnp.exp(heights), extent[dim] // shards_of).reshape((-1,) + (1,) * (len(extent) - 1 - dim))
    return gain


def gaussian(rng, shape, deviation, most, cuts=(), held_as=jnp.bfloat16):
    gain = block_levels(rng, shape, cuts, -0.22, 0.18) if cuts else 1.0
    entries = jax.random.normal(rng, shape, jnp.float32) * deviation * gain
    return jnp.minimum(jnp.maximum(entries, -most), most).astype(held_as)


def setup_inputs(seed: int = 0) -> dict:
    splits = jax.random.split(jax.random.key(seed), 7)
    inputs = gaussian(splits[0], (NB, CTX + QMAX, D), 1.0, 6.0, ((0, 8),))
    cotangent = gaussian(splits[1], (NB, CTX + QMAX, D), 1.0, 6.0, ((0, 8),))
    query_counts = draw_query_counts(jax.random.fold_in(splits[6], 71), 0)
    section_weight = draw_section_weight(jax.random.fold_in(splits[6], 71), 0)
    section_bias = draw_section_bias(jax.random.fold_in(splits[6], 71), 0)
    section_norm = draw_section_norm(jax.random.fold_in(splits[6], 71), 0)
    return {"inputs": inputs, "cotangent": cotangent, "query_counts": query_counts, "section_weight": section_weight, "section_bias": section_bias, "section_norm": section_norm}


@jax.custom_vjp
def low(v):
    return lax.optimization_barrier(v.astype(jnp.bfloat16)).astype(jnp.float32)

@jax.custom_vjp
def low_back(v):
    return v

def low_keep(v):
    return (low(v), None)

def low_pass(kept, grad):
    return (grad,)

def back_keep(v):
    return (v, None)

def back_low(kept, grad):
    return (low(grad),)
low.defvjp(low_keep, low_pass)
low_back.defvjp(back_keep, back_low)
highest_precision = lax.Precision.HIGHEST
epsilon = 1e-05

def matmul(first_operand, second_operand):
    return jnp.einsum('vjy,yu->vju', first_operand, second_operand, precision=highest_precision)

def layer_norm(residual, gain_row, shift_row):
    center = residual - lax.optimization_barrier(jnp.mean(residual, axis=-1, keepdims=True))
    inverse = lax.rsqrt(lax.optimization_barrier(jnp.mean(center * center, axis=-1, keepdims=True)) + epsilon)
    return center * inverse * gain_row + shift_row

def attend_section(hidden, weight, biases, norm_par):
    groups = hidden.shape[0]
    rows_all = hidden.shape[1]
    zero_part = jnp.zeros((D,), jnp.float32)
    proj_bias = jnp.concatenate([biases[:D], zero_part, biases[D:2 * D]])
    packed = low(low_back(matmul(hidden, weight[:, :3 * D]) + proj_bias))
    queries = packed[:, :, :D].reshape(groups, rows_all, HEADS, HEAD)
    key_heads = packed[:, :CTX, D:2 * D].reshape(groups, CTX, HEADS, HEAD)
    value_heads = packed[:, :CTX, 2 * D:].reshape(groups, CTX, HEADS, HEAD)
    scores = jnp.einsum('nihe,nlhe->nhil', queries, key_heads, precision=highest_precision) * (1.0 / math.sqrt(HEAD))
    scores = low_back(scores)
    attn_probs = jax.nn.softmax(scores, axis=-1)
    attended = jnp.einsum('nhil,nlhe->nihe', low(attn_probs), value_heads, precision=highest_precision)
    attended = low(low_back(attended.reshape(groups, rows_all, D)))
    branch = low_back(matmul(attended, weight[:, 3 * D:]) + biases[2 * D:])
    return layer_norm(hidden + branch, norm_par[0], norm_par[1])

def feedforward_section(hidden, weight, biases, norm_par):
    pre_act = low_back(matmul(hidden, weight[:, :FF]) + biases[:FF])
    activated = low(jax.nn.gelu(pre_act, approximate=False))
    down = jnp.einsum('nif,df->nid', activated, weight[:, FF:], precision=highest_precision)
    branch = low_back(down + biases[FF:])
    return layer_norm(hidden + branch, norm_par[0], norm_par[1])

def forward(inputs_f, probes, weight, biases, norm_par):
    hidden = inputs_f + probes[0]
    outputs = []
    result = hidden
    for section_num in range(4):
        if section_num % 2 == 0:
            result = attend_section(hidden, weight[section_num], biases[section_num], norm_par[section_num])
        else:
            result = feedforward_section(hidden, weight[section_num], biases[section_num], norm_par[section_num])
        result = low(low_back(result))
        outputs.append(result)
        if section_num < 3:
            hidden = result + probes[section_num + 1]
    return (result, jnp.stack(outputs))

def reference(inputs, cotangent, query_counts, section_weight, section_bias, section_norm):
    weight = section_weight.astype(jnp.float32)
    biases = section_bias.astype(jnp.float32)
    norm_par = section_norm.astype(jnp.float32)
    total_hoods = inputs.shape[0]
    rows_all = inputs.shape[1]
    group_size = 2
    live_rows = (jnp.arange(rows_all, dtype=jnp.int32)[None, :] < CTX + query_counts[:, None]).astype(jnp.float32)
    shaped_in = inputs.reshape(total_hoods // group_size, group_size, rows_all, D)
    shaped_ct = cotangent.reshape(total_hoods // group_size, group_size, rows_all, D)
    shaped_live = live_rows.reshape(total_hoods // group_size, group_size, rows_all)

    def one_group(running, block_in):
        group_in, group_ct, group_live = block_in
        probes = jnp.zeros((4,) + group_in.shape, jnp.float32)
        final_out, pullback, stacked = jax.vjp(forward, group_in.astype(jnp.float32), probes, weight, biases, norm_par, has_aux=True)
        seed_ct = group_ct.astype(jnp.float32) * group_live[:, :, None]
        gradients = pullback(seed_ct)
        running = (running[0] + gradients[2], running[1] + gradients[3], running[2] + gradients[4])
        shown_acts = (stacked * group_live[None, :, :, None]).astype(jnp.bfloat16)
        return (running, (shown_acts, gradients[1].astype(jnp.bfloat16)))
    start_state = (jnp.zeros(weight.shape, jnp.float32), jnp.zeros(biases.shape, jnp.float32), jnp.zeros(norm_par.shape, jnp.float32))
    running, (acts_all, grads_all) = lax.scan(one_group, start_state, (shaped_in, shaped_ct, shaped_live))
    activations = jnp.moveaxis(acts_all, 1, 0).reshape(4, total_hoods, rows_all, D)
    input_grads = jnp.moveaxis(grads_all, 1, 0).reshape(4, total_hoods, rows_all, D)
    return (activations, input_grads, running[0], running[1], running[2])
```

```python
import functools
import math

import jax
import jax.numpy as jnp
from jax import lax
from jax.experimental import pallas as pl
from jax.experimental.pallas import tpu as pltpu
from jax.sharding import PartitionSpec as P

D = 512
HEADS = 4
HEAD = 128
FF = 1024
CTX = 896
ROWS = 1024
SECTIONS = 4
TILE = 256
F32 = jnp.float32
BF = jnp.bfloat16
LOG2E = math.log2(math.e)
MESH = pl.DeviceIdType.MESH
MIB = 1 << 20


def dot(a, b):
    return lax.dot_general(a, b, (((1,), (0,)), ((), ())), preferred_element_type=F32)


def dot_t(a, b):
    return lax.dot_general(a, b, (((1,), (1,)), ((), ())), preferred_element_type=F32)


def t_dot(a, b):
    return lax.dot_general(a, b, (((0,), (0,)), ((), ())), preferred_element_type=F32)


def colsum(x):
    return jnp.sum(x, axis=0, keepdims=True)


def rows_loop(total, step, body):
    def one(i, carry):
        body(pl.multiple_of(i * step, step))
        return carry

    lax.fori_loop(0, total // step, one, 0)


LANE_RSTD = 0
LANE_NORMAL = 8
LANE_INNER = 16


def norm_forward(res, par):
    mean = jnp.mean(res, axis=-1, keepdims=True)
    center = res - mean
    inverse = lax.rsqrt(jnp.mean(center * center, axis=-1, keepdims=True) + 1e-5)
    normed = center * inverse
    return normed * par[3:4, :] + par[4:5, :], normed, inverse


def norm_backward(gy, normed, inverse, par):
    u = gy * par[3:4, :]
    m1 = jnp.mean(u, axis=-1, keepdims=True)
    m2 = jnp.mean(u * normed, axis=-1, keepdims=True)
    return inverse * (u - m1 - normed * m2)


def live_rows(count, begin, n):
    ids = lax.broadcasted_iota(jnp.int32, (n, 1), 0) + begin
    return jnp.where(ids < CTX + count, 1.0, 0.0).astype(F32)


def gelu_parts(z):
    t = 1.0 / (1.0 + (0.3275911 / math.sqrt(2.0)) * jnp.abs(z))
    e = jnp.exp2(z * z * (-0.5 * LOG2E))
    a = [0.254829592, -0.284496736, 1.421413741, -1.453152027, 1.061405429]
    a = [0.5 * v for v in a]
    tail = t * (a[0] + t * (a[1] + t * (a[2] + t * (a[3] + t * a[4])))) * e
    phi = jnp.where(z >= 0, 1.0 - tail, tail)
    return z * phi, phi + z * e * (1.0 / math.sqrt(2 * math.pi))


def finish_forward(j, res, par, count, begin, normed, stat, y):
    rows = pl.ds(begin, TILE)
    out, unit, inverse = norm_forward(res, par)
    y[rows, :] = (out * live_rows(count, begin, TILE)).astype(BF)
    normed[rows, :] = unit.astype(BF)
    stat[rows, LANE_RSTD + j : LANE_RSTD + j + 1] = inverse


def attend_forward(j, h, w, par, count, qkv, probs, att, stat, normed, y):
    factor = LOG2E / math.sqrt(HEAD)
    lane = LANE_NORMAL + 2 * j

    def project(r):
        rows = pl.ds(r, 512)
        x = h[rows, :]
        qkv[rows, 0:D] = ((dot(x, w[:, 0:D]) + par[0:1, :]) * factor).astype(BF)
        qkv[rows, D : 2 * D] = dot(x, w[:, D : 2 * D]).astype(BF)
        qkv[rows, 2 * D : 3 * D] = (dot(x, w[:, 2 * D : 3 * D]) + par[1:2, :]).astype(BF)

    rows_loop(ROWS, 512, project)

    def heads(r):
        rows = pl.ds(r, TILE)
        for hd in range(HEADS):
            c = hd * HEAD
            s = dot_t(qkv[rows, c : c + HEAD], qkv[0:CTX, D + c : D + c + HEAD])
            e = jnp.exp2(s - jnp.max(s, axis=-1, keepdims=True))
            normal = 1.0 / jnp.sum(e, axis=-1, keepdims=True)
            low = e.astype(BF)
            probs[hd, rows, :] = low
            stat[rows, lane + hd : lane + hd + 1] = normal
            o = dot(low, qkv[0:CTX, 2 * D + c : 2 * D + c + HEAD])
            att[rows, c : c + HEAD] = (o * normal).astype(BF)

    rows_loop(ROWS, TILE, heads)

    def project_out(r):
        rows = pl.ds(r, TILE)
        res = dot(att[rows, :], w[:, 3 * D : 4 * D]) + par[2:3, :] + h[rows, :].astype(F32)
        finish_forward(j, res, par, count, r, normed, stat, y)

    rows_loop(ROWS, TILE, project_out)


def feed_forward(j, h, w, par, count, act, slope, stat, normed, y):
    def body(r):
        rows = pl.ds(r, TILE)
        x = h[rows, :]
        for k in range(2):
            c = k * 512
            g, dg = gelu_parts(dot(x, w[:, c : c + 512]) + par[k : k + 1, :])
            act[rows, c : c + 512] = g.astype(BF)
            slope[rows, c : c + 512] = dg.astype(BF)
        res = dot_t(act[rows, :], w[:, FF:]) + par[2:3, :] + x.astype(F32)
        finish_forward(j, res, par, count, r, normed, stat, y)

    rows_loop(ROWS, TILE, body)


def start_backward(j, r, gy, par, normed, stat, gb, small):
    rows = pl.ds(r, TILE)
    unit = normed[rows, :].astype(F32)
    gres = norm_backward(gy, unit, stat[rows, LANE_RSTD + j : LANE_RSTD + j + 1], par)
    small[3:4, :] += colsum(gy * unit)
    small[4:5, :] += colsum(gy)
    low = gres.astype(BF)
    gb[rows, :] = low
    small[2:3, :] += colsum(low.astype(F32))
    return gres, low


def feed_backward(j, gy_of, w, par, act, slope, stat, normed, gb, ig, small):
    small[...] = jnp.zeros(small.shape, F32)

    def body(r):
        rows = pl.ds(r, TILE)
        gres, low = start_backward(j, r, gy_of(r), par, normed, stat, gb, small)
        for k in range(2):
            c = k * 512
            ga = dot(low, w[:, FF + c : FF + c + 512])
            gp = (ga * slope[rows, c : c + 512].astype(F32)).astype(BF)
            slope[rows, c : c + 512] = gp
            small[k : k + 1, :] += colsum(gp.astype(F32))
        ig[rows, :] = (gres + dot_t(slope[rows, :], w[:, 0:FF])).astype(BF)

    rows_loop(ROWS, TILE, body)


def feed_weights(h, act, gpre, gb, flip, dw):
    flip[...] = h[...].T
    for c in range(0, FF, 512):
        dw[:, c : c + 512] = dot(flip[...], gpre[:, c : c + 512]).astype(BF)
    flip[...] = gb[...].T
    for c in range(0, FF, 512):
        dw[:, FF + c : FF + c + 512] = dot(flip[...], act[:, c : c + 512]).astype(BF)


def attend_backward(j, gy_of, w, par, qkv, probs, att, stat, normed, gb, gatt, gqkv, gkv, gres_ref, ig, small):
    lane = LANE_NORMAL + 2 * j
    small[...] = jnp.zeros(small.shape, F32)

    def body(r):
        rows = pl.ds(r, TILE)
        gres, low = start_backward(j, r, gy_of(r), par, normed, stat, gb, small)
        gres_ref[rows, :] = gres
        ga = dot_t(low, w[:, 3 * D : 4 * D])
        a = att[rows, :].astype(F32)
        for hd in range(HEADS):
            c = hd * HEAD
            g = ga[:, c : c + HEAD] * stat[rows, lane + hd : lane + hd + 1]
            gatt[rows, c : c + HEAD] = g.astype(BF)
            stat[rows, LANE_INNER + hd : LANE_INNER + hd + 1] = jnp.sum(
                g * a[:, c : c + HEAD], axis=-1, keepdims=True
            )

    rows_loop(ROWS, TILE, body)
    gkv[...] = jnp.zeros(gkv.shape, F32)

    def heads(r):
        rows = pl.ds(r, TILE)
        for hd in range(HEADS):
            c = hd * HEAD
            ga = gatt[rows, c : c + HEAD]
            gp = dot_t(ga, qkv[0:CTX, 2 * D + c : 2 * D + c + HEAD])
            low = probs[hd, rows, :]
            inner = stat[rows, LANE_INNER + hd : LANE_INNER + hd + 1]
            gs = (low.astype(F32) * (gp - inner)).astype(BF)
            gkv[HEADS + hd, :, :] += t_dot(ga, low)
            gkv[hd, :, :] += t_dot(qkv[rows, c : c + HEAD], gs)
            gq = dot(gs, qkv[0:CTX, D + c : D + c + HEAD])
            gqkv[rows, c : c + HEAD] = (gq * (1.0 / math.sqrt(HEAD))).astype(BF)

    rows_loop(ROWS, TILE, heads)
    for hd in range(HEADS):
        c = hd * HEAD
        gqkv[0:CTX, D + c : D + c + HEAD] = (gkv[hd, :, :] * (1.0 / LOG2E)).T.astype(BF)
        gqkv[0:CTX, 2 * D + c : 2 * D + c + HEAD] = gkv[HEADS + hd, :, :].T.astype(BF)
    gqkv[CTX:ROWS, D : 3 * D] = jnp.zeros((ROWS - CTX, 2 * D), BF)

    def project(r):
        rows = pl.ds(r, TILE)
        ig[rows, :] = (gres_ref[rows, :] + dot_t(gqkv[rows, :], w[:, 0 : 3 * D])).astype(BF)
        small[0:1, :] += colsum(gqkv[rows, 0:D].astype(F32))
        small[1:2, :] += colsum(gqkv[rows, 2 * D : 3 * D].astype(F32))

    rows_loop(ROWS, TILE, project)


def attend_weights(h, att, gqkv, gb, flip, dw):
    flip[...] = h[...].T
    for c in range(0, 3 * D, 512):
        dw[:, c : c + 512] = dot(flip[...], gqkv[:, c : c + 512]).astype(BF)
    flip[...] = att[...].T
    dw[:, 3 * D :] = dot(flip[...], gb[...]).astype(BF)


def vm(*shape, dtype=BF):
    return pltpu.VMEM(shape, dtype)


SCRATCH = dict(
    x=vm(ROWS, D),
    w=vm(SECTIONS, D, 4 * D),
    ys=vm(SECTIONS, ROWS, D),
    igs=vm(SECTIONS, ROWS, D),
    norms=vm(SECTIONS, ROWS, D),
    qkvs=vm(2, ROWS, 3 * D),
    atts=vm(2, ROWS, D),
    ffs=vm(2, ROWS, 2 * FF),
    probs=vm(HEADS, ROWS, CTX),
    stat=vm(ROWS, 128, dtype=F32),
    flip=vm(D, ROWS),
    gb=vm(ROWS, D),
    gkv=vm(2 * HEADS, HEAD, CTX, dtype=F32),
    gres=vm(ROWS, D, dtype=F32),
    dw=vm(2, D, 4 * D),
    small=vm(SECTIONS, 8, D, dtype=F32),
    load_sem=pltpu.SemaphoreType.DMA((16,)),
    dw_sem=pltpu.SemaphoreType.DMA((SECTIONS,)),
    act_send=pltpu.SemaphoreType.DMA((SECTIONS,)),
    act_recv=pltpu.SemaphoreType.DMA((SECTIONS,)),
    ig_send=pltpu.SemaphoreType.DMA((SECTIONS,)),
    ig_recv=pltpu.SemaphoreType.DMA((SECTIONS,)),
)


class Names:
    def __init__(self, names, refs):
        self.__dict__.update(zip(names, refs, strict=True))


INPUTS = ("inputs", "cot", "counts", "weight", "par")
OUTPUTS = ("acts", "grads", "dweight", "dsmall", "kept")


def kernel(*refs):
    o = Names(INPUTS + OUTPUTS + tuple(SCRATCH), refs)
    me = lax.axis_index("section")
    dp = lax.axis_index("dp")

    barrier = pltpu.get_barrier_semaphore()
    for r in range(1, SECTIONS):
        pl.semaphore_signal(barrier, inc=1, device_id=(me ^ r, dp), device_id_type=MESH)
    pl.semaphore_wait(barrier, SECTIONS - 1)

    count = o.counts[me]
    loads = [pltpu.make_async_copy(o.inputs.at[me], o.x, o.load_sem.at[0])]
    for j in range(SECTIONS):
        loads.append(pltpu.make_async_copy(o.weight.at[j], o.w.at[j], o.load_sem.at[1 + j]))
    loads.append(pltpu.make_async_copy(o.cot.at[me], o.igs.at[0], o.load_sem.at[5]))
    for load in loads:
        load.start()

    def deliver(block, out, j, send, recv):
        @pl.when(me == j)
        def _():
            pltpu.make_async_copy(block, out.at[j], recv.at[j]).start()

        @pl.when(me != j)
        def _():
            pltpu.make_async_remote_copy(
                src_ref=block,
                dst_ref=out.at[me],
                send_sem=send.at[j],
                recv_sem=recv.at[me],
                device_id=(j, dp),
                device_id_type=MESH,
            ).start()

    def sent(block, out, j, send, recv):
        @pl.when(me != j)
        def _():
            pltpu.make_async_remote_copy(
                src_ref=block,
                dst_ref=out.at[me],
                send_sem=send.at[j],
                recv_sem=recv.at[me],
                device_id=(j, dp),
                device_id_type=MESH,
            ).wait_send()

    def arrived(block, out, n, recv):
        pltpu.make_async_copy(block, out.at[n], recv.at[n]).wait()

    keep = pltpu.make_async_copy(o.probs, o.kept, o.load_sem.at[6])
    bring = pltpu.make_async_copy(o.kept, o.probs, o.load_sem.at[7])

    loads[0].wait()
    for j in range(SECTIONS):
        loads[1 + j].wait()
        layer = j // 2
        h = o.x if j == 0 else o.ys.at[j - 1]
        w, par, y, normed = o.w.at[j], o.par.at[j], o.ys.at[j], o.norms.at[j]
        if j % 2 == 0:
            if j == 2:
                keep.wait()
            attend_forward(j, h, w, par, count, o.qkvs.at[layer], o.probs, o.atts.at[layer], o.stat, normed, y)
            if j == 0:
                keep.start()
        else:
            f = o.ffs.at[layer]
            feed_forward(j, h, w, par, count, f.at[:, :FF], f.at[:, FF:], o.stat, normed, y)
        deliver(y, o.acts, j, o.act_send, o.act_recv)

    loads[5].wait()
    dw_copies = []
    for j in reversed(range(SECTIONS)):
        layer = j // 2
        h = o.x if j == 0 else o.ys.at[j - 1]
        w, par, normed = o.w.at[j], o.par.at[j], o.norms.at[j]
        ig, small, dw = o.igs.at[j], o.small.at[j], o.dw.at[j % 2]
        if j == 3:

            def gy_of(r):
                return o.igs[0, pl.ds(r, TILE), :].astype(F32) * live_rows(count, r, TILE)
        else:

            def gy_of(r, j=j):
                return o.igs[j + 1, pl.ds(r, TILE), :].astype(F32)

        f = o.ffs.at[layer]
        if j % 2 == 0:
            if j == 0:
                bring.wait()
            pool = o.ffs.at[1]
            gqkv, gatt = pool.at[:, : 3 * D], pool.at[:, 3 * D :]
            attend_backward(
                j, gy_of, w, par, o.qkvs.at[layer], o.probs, o.atts.at[layer], o.stat, normed, o.gb, gatt, gqkv,
                o.gkv, o.gres, ig, small,
            )
            if j == 2:
                bring.start()
        else:
            feed_backward(j, gy_of, w, par, f.at[:, :FF], f.at[:, FF:], o.stat, normed, o.gb, ig, small)
        deliver(ig, o.grads, j, o.ig_send, o.ig_recv)
        if len(dw_copies) >= 2:
            dw_copies[-2].wait()
        if j % 2 == 0:
            attend_weights(h, o.atts.at[layer], gqkv, o.gb, o.flip, dw)
        else:
            feed_weights(h, f.at[:, :FF], f.at[:, FF:], o.gb, o.flip, dw)
        copy = pltpu.make_async_copy(dw, o.dweight.at[j], o.dw_sem.at[j])
        copy.start()
        dw_copies.append(copy)

    o.dsmall[...] = o.small[...]
    for copy in dw_copies[-2:]:
        copy.wait()
    for j in range(SECTIONS):
        sent(o.ys.at[j], o.acts, j, o.act_send, o.act_recv)
        sent(o.igs.at[j], o.grads, j, o.ig_send, o.ig_recv)
    for n in range(SECTIONS):
        arrived(o.ys.at[0], o.acts, n, o.act_recv)
        arrived(o.igs.at[0], o.grads, n, o.ig_recv)


def shards(inputs, cotangent, query_counts, section_weight, section_bias, section_norm):
    dp = lax.axis_index("dp")
    me = lax.axis_index("section")
    size = lax.axis_size("dp")

    def gathered(v, axis):
        v = lax.all_gather(v, "dp", axis=axis, tiled=True)
        return lax.all_gather(v, "section", axis=0, tiled=True)

    weight = gathered(section_weight, 1)
    bias = gathered(section_bias, 1)
    norm = gathered(section_norm, 2)
    par = jnp.concatenate([bias.reshape(SECTIONS, 3, D), norm, jnp.zeros((SECTIONS, 3, D), BF)], axis=1).astype(F32)
    anywhere = pl.BlockSpec(memory_space=pl.ANY)
    whole = pl.BlockSpec(memory_space=pltpu.VMEM)
    acts, grads, dweight, dsmall, _ = pl.pallas_call(
        kernel,
        out_shape=(
            jax.ShapeDtypeStruct((SECTIONS, ROWS, D), BF),
            jax.ShapeDtypeStruct((SECTIONS, ROWS, D), BF),
            jax.ShapeDtypeStruct((SECTIONS, D, 4 * D), BF),
            jax.ShapeDtypeStruct((SECTIONS, 8, D), F32),
            jax.ShapeDtypeStruct((HEADS, ROWS, CTX), BF),
        ),
        in_specs=[anywhere, anywhere, pl.BlockSpec(memory_space=pltpu.SMEM), anywhere, whole],
        out_specs=(anywhere, anywhere, anywhere, whole, anywhere),
        scratch_shapes=list(SCRATCH.values()),
        compiler_params=pltpu.CompilerParams(
            collective_id=0, has_side_effects=True, vmem_limit_bytes=63 * MIB
        ),
    )(inputs, cotangent, query_counts, weight, par)

    def scattered(v, axis):
        v = lax.psum_scatter(v, "dp", scatter_dimension=axis, tiled=True)
        return lax.psum_scatter(v, "section", scatter_dimension=0, tiled=True)

    dw = scattered(dweight, 1).astype(F32)
    db = scattered(dsmall[:, :3].reshape(SECTIONS, 3 * D), 1)
    dn = scattered(dsmall[:, 3:5], 2)
    return acts[None], grads[None], dw, db, dn


def solution(mesh):
    return jax.shard_map(
        shards,
        mesh=mesh,
        in_specs=(
            P("dp", None, None),
            P("dp", None, None),
            P("dp"),
            P("section", "dp", None),
            P("section", "dp"),
            P("section", None, "dp"),
        ),
        out_specs=(
            P("section", "dp", None, None),
            P("section", "dp", None, None),
            P("section", "dp", None),
            P("section", "dp"),
            P("section", None, "dp"),
        ),
        check_vma=False,
    )
```

```python
import functools
import math

import jax
import jax.numpy as jnp
from jax import lax
from jax.experimental import pallas as pl
from jax.experimental.pallas import tpu as pltpu
from jax.sharding import PartitionSpec as P

D = 512
HEADS = 4
HEAD = 128
FF = 1024
CTX = 896
ROWS = 1024
SECTIONS = 4
TILE = 256
F32 = jnp.float32
BF = jnp.bfloat16
LOG2E = math.log2(math.e)
MESH = pl.DeviceIdType.MESH
MIB = 1 << 20


def dot(a, b):
    return lax.dot_general(a, b, (((1,), (0,)), ((), ())), preferred_element_type=F32)


def dot_t(a, b):
    return lax.dot_general(a, b, (((1,), (1,)), ((), ())), preferred_element_type=F32)


def t_dot(a, b):
    return lax.dot_general(a, b, (((0,), (0,)), ((), ())), preferred_element_type=F32)


def colsum(x):
    return jnp.sum(x, axis=0, keepdims=True)


def rows_loop(total, step, body):
    def one(i, carry):
        body(pl.multiple_of(i * step, step))
        return carry

    lax.fori_loop(0, total // step, one, 0)


LANE_RSTD = 0
LANE_NORMAL = 8
LANE_INNER = 16


def norm_forward(res, par):
    mean = jnp.mean(res, axis=-1, keepdims=True)
    center = res - mean
    inverse = lax.rsqrt(jnp.mean(center * center, axis=-1, keepdims=True) + 1e-5)
    normed = center * inverse
    return normed * par[3:4, :] + par[4:5, :], normed, inverse


def norm_backward(gy, normed, inverse, par):
    u = gy * par[3:4, :]
    m1 = jnp.mean(u, axis=-1, keepdims=True)
    m2 = jnp.mean(u * normed, axis=-1, keepdims=True)
    return inverse * (u - m1 - normed * m2)


def live_rows(count, begin, n):
    ids = lax.broadcasted_iota(jnp.int32, (n, 1), 0) + begin
    return jnp.where(ids < CTX + count, 1.0, 0.0).astype(F32)


def gelu_parts(z):
    t = 1.0 / (1.0 + (0.3275911 / math.sqrt(2.0)) * jnp.abs(z))
    e = jnp.exp2(z * z * (-0.5 * LOG2E))
    a = [0.254829592, -0.284496736, 1.421413741, -1.453152027, 1.061405429]
    a = [0.5 * v for v in a]
    tail = t * (a[0] + t * (a[1] + t * (a[2] + t * (a[3] + t * a[4])))) * e
    phi = jnp.where(z >= 0, 1.0 - tail, tail)
    return z * phi, phi + z * e * (1.0 / math.sqrt(2 * math.pi))


def finish_forward(j, res, par, count, begin, normed, stat, y):
    rows = pl.ds(begin, TILE)
    out, unit, inverse = norm_forward(res, par)
    y[rows, :] = (out * live_rows(count, begin, TILE)).astype(BF)
    normed[rows, :] = unit.astype(BF)
    stat[rows, LANE_RSTD + j : LANE_RSTD + j + 1] = inverse


def attend_forward(j, h, w, par, count, qkv, probs, att, stat, normed, y, between):
    factor = LOG2E / math.sqrt(HEAD)
    lane = LANE_NORMAL + 2 * j

    def project(r):
        rows = pl.ds(r, 512)
        x = h[rows, :]
        qkv[rows, 0:D] = ((dot(x, w[:, 0:D]) + par[0:1, :]) * factor).astype(BF)
        qkv[rows, D : 2 * D] = dot(x, w[:, D : 2 * D]).astype(BF)
        qkv[rows, 2 * D : 3 * D] = (dot(x, w[:, 2 * D : 3 * D]) + par[1:2, :]).astype(BF)

    rows_loop(ROWS, 512, project)
    between(0)

    def heads(r):
        rows = pl.ds(r, TILE)
        for hd in range(HEADS):
            c = hd * HEAD
            s = dot_t(qkv[rows, c : c + HEAD], qkv[0:CTX, D + c : D + c + HEAD])
            e = jnp.exp2(s - jnp.max(s, axis=-1, keepdims=True))
            normal = 1.0 / jnp.sum(e, axis=-1, keepdims=True)
            low = e.astype(BF)
            probs[hd, rows, :] = low
            stat[rows, lane + hd : lane + hd + 1] = normal
            o = dot(low, qkv[0:CTX, 2 * D + c : 2 * D + c + HEAD])
            att[rows, c : c + HEAD] = (o * normal).astype(BF)

    rows_loop(ROWS, TILE, heads)
    between(1)

    def project_out(r):
        rows = pl.ds(r, TILE)
        res = dot(att[rows, :], w[:, 3 * D : 4 * D]) + par[2:3, :] + h[rows, :].astype(F32)
        finish_forward(j, res, par, count, r, normed, stat, y)

    rows_loop(ROWS, TILE, project_out)


def feed_forward(j, h, w, par, count, act, slope, stat, normed, y):
    def body(r):
        rows = pl.ds(r, TILE)
        x = h[rows, :]
        for k in range(2):
            c = k * 512
            g, dg = gelu_parts(dot(x, w[:, c : c + 512]) + par[k : k + 1, :])
            act[rows, c : c + 512] = g.astype(BF)
            slope[rows, c : c + 512] = dg.astype(BF)
        res = dot_t(act[rows, :], w[:, FF:]) + par[2:3, :] + x.astype(F32)
        finish_forward(j, res, par, count, r, normed, stat, y)

    rows_loop(ROWS, TILE, body)


def start_backward(j, r, gy, par, normed, stat, gb, small):
    rows = pl.ds(r, TILE)
    unit = normed[rows, :].astype(F32)
    gres = norm_backward(gy, unit, stat[rows, LANE_RSTD + j : LANE_RSTD + j + 1], par)
    small[3:4, :] += colsum(gy * unit)
    small[4:5, :] += colsum(gy)
    low = gres.astype(BF)
    gb[rows, :] = low
    small[2:3, :] += colsum(low.astype(F32))
    return gres, low


def feed_backward(j, gy_of, w, par, act, slope, stat, normed, gb, ig, small):
    small[...] = jnp.zeros(small.shape, F32)

    def body(r):
        rows = pl.ds(r, TILE)
        gres, low = start_backward(j, r, gy_of(r), par, normed, stat, gb, small)
        for k in range(2):
            c = k * 512
            ga = dot(low, w[:, FF + c : FF + c + 512])
            gp = (ga * slope[rows, c : c + 512].astype(F32)).astype(BF)
            slope[rows, c : c + 512] = gp
            small[k : k + 1, :] += colsum(gp.astype(F32))
        ig[rows, :] = (gres + dot_t(slope[rows, :], w[:, 0:FF])).astype(BF)

    rows_loop(ROWS, TILE, body)


def feed_weights(h, act, gpre, gb, flip, dw):
    flip[...] = h[...].T
    for c in range(0, FF, 512):
        dw[:, c : c + 512] = dot(flip[...], gpre[:, c : c + 512]).astype(BF)
    flip[...] = gb[...].T
    for c in range(0, FF, 512):
        dw[:, FF + c : FF + c + 512] = dot(flip[...], act[:, c : c + 512]).astype(BF)


def attend_backward(j, gy_of, w, par, qkv, probs, att, stat, normed, gb, gatt, gqkv, gkv, gres_ref, ig, small,
                    between):
    lane = LANE_NORMAL + 2 * j
    small[...] = jnp.zeros(small.shape, F32)

    def body(r):
        rows = pl.ds(r, TILE)
        gres, low = start_backward(j, r, gy_of(r), par, normed, stat, gb, small)
        gres_ref[rows, :] = gres
        ga = dot_t(low, w[:, 3 * D : 4 * D])
        a = att[rows, :].astype(F32)
        for hd in range(HEADS):
            c = hd * HEAD
            g = ga[:, c : c + HEAD] * stat[rows, lane + hd : lane + hd + 1]
            gatt[rows, c : c + HEAD] = g.astype(BF)
            stat[rows, LANE_INNER + hd : LANE_INNER + hd + 1] = jnp.sum(
                g * a[:, c : c + HEAD], axis=-1, keepdims=True
            )

    rows_loop(ROWS, TILE, body)
    between(0)
    gkv[...] = jnp.zeros(gkv.shape, F32)

    def heads(r):
        rows = pl.ds(r, TILE)
        for hd in range(HEADS):
            c = hd * HEAD
            ga = gatt[rows, c : c + HEAD]
            gp = dot_t(ga, qkv[0:CTX, 2 * D + c : 2 * D + c + HEAD])
            low = probs[hd, rows, :]
            inner = stat[rows, LANE_INNER + hd : LANE_INNER + hd + 1]
            gs = (low.astype(F32) * (gp - inner)).astype(BF)
            gkv[HEADS + hd, :, :] += t_dot(ga, low)
            gkv[hd, :, :] += t_dot(qkv[rows, c : c + HEAD], gs)
            gq = dot(gs, qkv[0:CTX, D + c : D + c + HEAD])
            gqkv[rows, c : c + HEAD] = (gq * (1.0 / math.sqrt(HEAD))).astype(BF)

    rows_loop(ROWS, TILE, heads)
    between(1)
    for hd in range(HEADS):
        c = hd * HEAD
        gqkv[0:CTX, D + c : D + c + HEAD] = (gkv[hd, :, :] * (1.0 / LOG2E)).T.astype(BF)
        gqkv[0:CTX, 2 * D + c : 2 * D + c + HEAD] = gkv[HEADS + hd, :, :].T.astype(BF)
    gqkv[CTX:ROWS, D : 3 * D] = jnp.zeros((ROWS - CTX, 2 * D), BF)

    def project(r):
        rows = pl.ds(r, TILE)
        ig[rows, :] = (gres_ref[rows, :] + dot_t(gqkv[rows, :], w[:, 0 : 3 * D])).astype(BF)
        small[0:1, :] += colsum(gqkv[rows, 0:D].astype(F32))
        small[1:2, :] += colsum(gqkv[rows, 2 * D : 3 * D].astype(F32))

    rows_loop(ROWS, TILE, project)


def attend_weights(h, att, gqkv, gb, flip, dw):
    flip[...] = h[...].T
    for c in range(0, 3 * D, 512):
        dw[:, c : c + 512] = dot(flip[...], gqkv[:, c : c + 512]).astype(BF)
    flip[...] = att[...].T
    dw[:, 3 * D :] = dot(flip[...], gb[...]).astype(BF)


def vm(*shape, dtype=BF):
    return pltpu.VMEM(shape, dtype)


SCRATCH = dict(
    x=vm(ROWS, D),
    w=vm(SECTIONS, D, 4 * D),
    ys=vm(SECTIONS, ROWS, D),
    igs=vm(SECTIONS, ROWS, D),
    norms=vm(SECTIONS, ROWS, D),
    qkvs=vm(2, ROWS, 3 * D),
    atts=vm(2, ROWS, D),
    ffs=vm(2, ROWS, 2 * FF),
    probs=vm(HEADS, ROWS, CTX),
    stat=vm(ROWS, 128, dtype=F32),
    flip=vm(D, ROWS),
    gb=vm(ROWS, D),
    gkv=vm(2 * HEADS, HEAD, CTX, dtype=F32),
    gres=vm(ROWS, D, dtype=F32),
    dw=vm(2, D, 4 * D),
    small=vm(SECTIONS, 8, D, dtype=F32),
    load_sem=pltpu.SemaphoreType.DMA((8,)),
    act_send=pltpu.SemaphoreType.DMA((SECTIONS,)),
    act_recv=pltpu.SemaphoreType.DMA((SECTIONS,)),
    ig_send=pltpu.SemaphoreType.DMA((SECTIONS,)),
    ig_recv=pltpu.SemaphoreType.DMA((SECTIONS,)),
)


def spread_scratch(size):
    half = size // 2
    sem = pltpu.SemaphoreType.DMA
    return dict(
        parts=vm(size, 8, D, dtype=F32),
        par=vm(SECTIONS, 8, D, dtype=F32),
        sum_plane=vm(SECTIONS, 8, D, dtype=F32),
        sum_dp=vm(size, 8, D, dtype=F32),
        stage=vm(half, D // size, 4 * D),
        last=vm(D // size, 4 * D, dtype=F32),
        w_recv=sem((SECTIONS + 1, size)),
        w_send=sem((64,)),
        parts_recv=sem((size,)),
        par_recv=sem((SECTIONS,)),
        a_recv=sem((SECTIONS, half)),
        b_recv=sem((SECTIONS, half // 2)),
        c_recv=sem((SECTIONS,)),
        d_recv=sem((SECTIONS,)),
        sp_recv=sem((SECTIONS,)),
        sd_recv=sem((size,)),
        dw_send=sem((128,)),
        stage_sem=sem((1,)),
    )


class Names:
    def __init__(self, names, refs):
        self.__dict__.update(zip(names, refs, strict=True))


INPUTS = ("inputs", "cot", "counts", "weight", "par_in")
OUTPUTS = ("acts", "grads", "dweight", "dsmall", "kept")
LANDING = ("land_a", "land_b", "land_c", "land_d")


class Sends:
    def __init__(self, sems):
        self.sems, self.used, self.started = sems, 0, {}

    def push(self, group, src, dst, recv_sem, target, when=None):
        k = self.used
        self.used += 1

        def copy():
            return pltpu.make_async_remote_copy(
                src_ref=src,
                dst_ref=dst,
                send_sem=self.sems.at[k],
                recv_sem=recv_sem,
                device_id=target,
                device_id_type=MESH,
            )

        self.started.setdefault(group, []).append((when, copy))
        guarded(when, lambda: copy().start())

    def drain(self, group):
        for when, copy in self.started.pop(group, ()):
            guarded(when, lambda copy=copy: copy().wait_send())


def guarded(when, action):
    if when is None:
        action()
    else:
        pl.when(when)(action)


def landed(dst, sem):
    pltpu.make_async_copy(dst, dst, sem).wait()


class Spread:
    def __init__(self, o, me, dp, size):
        self.o, self.me, self.dp, self.size = o, me, dp, size
        self.block = D // size
        self.sends = Sends(o.w_send)
        self.outs = Sends(o.dw_send)
        self.own = (dp, dp ^ 2, dp ^ 4, dp ^ 6)


    def shard(self, part, d):
        rows = pl.ds(pl.multiple_of(d * self.block, self.block), self.block)
        if isinstance(part, int) and part == SECTIONS:
            return self.o.w.at[0, rows, pl.ds(3 * D, D)]
        if isinstance(part, int) and part == 0:
            return self.o.w.at[0, rows, pl.ds(0, 3 * D)]
        return self.o.w.at[part, rows, :]

    def send_shard(self, part, d, section, dp, when=None):
        ref = self.shard(part, d)
        self.sends.push("w", ref, ref, self.o.w_recv.at[part, d], (section, dp), when)

    def wait_shard(self, part, d):
        landed(self.shard(part, d), self.o.w_recv.at[part, d])

    def begin(self):
        o, me, dp = self.o, self.me, self.dp
        load = pltpu.make_async_copy(o.weight.at[0], o.w.at[me, pl.ds(pl.multiple_of(dp * self.block, self.block), self.block), :], o.load_sem.at[1])
        load.start()
        o.parts[dp, :, :] = o.par_in[...]
        load.wait()

    def first(self):
        o, me, dp = self.o, self.me, self.dp
        parts = (0, SECTIONS)
        for part in parts:
            for r in range(1, SECTIONS):
                self.send_shard(part, dp, r, dp, me == 0)
        for k in range(1, self.size):
            self.sends.push("w", o.parts.at[dp], o.parts.at[dp], o.parts_recv.at[dp], (me, dp ^ k))
        for part in parts:
            pl.when(me != 0)(lambda part=part: self.wait_shard(part, dp))
            for other in (dp ^ 4, dp ^ 2, dp ^ 1):
                self.send_shard(part, dp, me, other)
        self.own_begin()
        for part in parts:
            self.wait_shard(part, dp ^ 4)
            self.send_shard(part, dp ^ 4, me, dp ^ 2)
            self.send_shard(part, dp ^ 4, me, dp ^ 1)
        for k in range(1, self.size):
            landed(o.parts.at[dp ^ k], o.parts_recv.at[dp ^ k])
        o.par[me, :, :] = jnp.sum(o.parts[...], axis=0)
        for r in range(1, SECTIONS):
            self.sends.push("w", o.par.at[me], o.par.at[me], o.par_recv.at[me], (me ^ r, dp))
        for part in parts:
            for d in self.own[1::2]:
                self.wait_shard(part, d)
                self.send_shard(part, d, me, dp ^ 1)
        for r in range(1, SECTIONS):
            landed(o.par.at[me ^ r], o.par_recv.at[me ^ r])
        for d in self.own:
            self.wait_shard(0, d ^ 1)

    def first_rest(self):
        for d in self.own:
            self.wait_shard(SECTIONS, d ^ 1)

    def fan_out(self, d):
        me, dp = self.me, self.dp
        later = me != 0
        for r in (1, 2, 3):
            self.send_shard(me, d, me ^ r, dp, later)
        self.send_shard(me, d, me, dp ^ 1, later)

    def own_begin(self):
        me, dp = self.me, self.dp
        for other in (dp ^ 4, dp ^ 2):
            self.send_shard(me, dp, me, other, me != 0)
        self.fan_out(dp)

    def own_step(self, step):
        me, dp = self.me, self.dp
        if step == 0:
            pl.when(me != 0)(lambda: self.wait_shard(me, dp ^ 4))
            self.send_shard(me, dp ^ 4, me, dp ^ 2, me != 0)
            self.fan_out(dp ^ 4)
        else:
            for d in (dp ^ 2, dp ^ 6):
                pl.when(me != 0)(lambda d=d: self.wait_shard(me, d))
                self.fan_out(d)

    def settle(self, j):
        me, dp = self.me, self.dp
        for d in self.own:
            pl.when(me != j)(lambda d=d: self.wait_shard(j, d))
            self.send_shard(j, d, me, dp ^ 1, me != j)
        for d in self.own:
            self.wait_shard(j, d ^ 1)


    def dw_block(self, j, k, core):
        begin = pl.multiple_of((2 * k + core) * self.block, self.block)
        return self.o.dw.at[j % 2, pl.ds(begin, self.block), :]

    def sum_start(self, j):
        o, me, dp = self.o, self.me, self.dp
        core = dp & 1
        for k in range(self.size // 2):
            self.outs.push(j, self.dw_block(j, k, 1 - core), o.land_a.at[j, k], o.a_recv.at[j, k], (me, dp ^ 1))
        o_small = o.small.at[j]
        self.outs.push(j, o_small, o.sum_plane.at[me], o.sp_recv.at[me], (j, dp), me != j)

    def add(self, pairs):
        o = self.o
        for t, (land, sem, _) in enumerate(pairs):
            landed(land, sem)
            pltpu.make_async_copy(land, o.stage.at[t], o.stage_sem.at[0]).start()
            pltpu.make_async_copy(land, o.stage.at[t], o.stage_sem.at[0]).wait()
        for t, (_, _, ref) in enumerate(pairs):
            ref[...] = (ref[...].astype(F32) + o.stage[t].astype(F32)).astype(BF)

    def sum_step(self, j, step):
        o, me, dp = self.o, self.me, self.dp
        core, z = dp & 1, dp >> 1
        half = self.size // 2
        if step == 0:
            self.add([(o.land_a.at[j, k], o.a_recv.at[j, k], self.dw_block(j, k, core)) for k in range(half)])
            for t in range(half // 2):
                k = 2 * t + 1 - (z & 1)
                self.outs.push(j, self.dw_block(j, k, core), o.land_b.at[j, t], o.b_recv.at[j, t], (me, dp ^ 2))
        elif step == 1:
            self.add([(o.land_b.at[j, t], o.b_recv.at[j, t], self.dw_block(j, 2 * t + (z & 1), core)) for t in range(half // 2)])
            self.outs.push(j, self.dw_block(j, z ^ 2, core), o.land_c.at[j], o.c_recv.at[j], (me, dp ^ 4))
        else:
            block = self.dw_block(j, z, core)
            self.add([(o.land_c.at[j], o.c_recv.at[j], block)])
            self.outs.push(j, block, o.land_d.at[me], o.d_recv.at[me], (j, dp), me != j)

            @pl.when(me == j)
            def _():
                o.last[...] = block[...].astype(F32)
                o.sum_plane[me, :, :] = o.small[j, :, :]

    def finish(self):
        o, me, dp = self.o, self.me, self.dp
        for r in range(1, SECTIONS):
            landed(o.sum_plane.at[me ^ r], o.sp_recv.at[me ^ r])
        o.sum_dp[dp, :, :] = jnp.sum(o.sum_plane[...], axis=0)
        for k in range(1, self.size):
            self.outs.push("s", o.sum_dp.at[dp], o.sum_dp.at[dp], o.sd_recv.at[dp], (me, dp ^ k))
        for r in range(1, SECTIONS):
            landed(o.land_d.at[me ^ r], o.d_recv.at[me ^ r])
            copy = pltpu.make_async_copy(o.land_d.at[me ^ r], o.stage.at[0], o.stage_sem.at[0])
            copy.start()
            copy.wait()
            o.last[...] += o.stage[0].astype(F32)
        out = pltpu.make_async_copy(o.last, o.dweight.at[0], o.stage_sem.at[0])
        out.start()
        for k in range(1, self.size):
            landed(o.sum_dp.at[dp ^ k], o.sd_recv.at[dp ^ k])
        o.dsmall[...] = jnp.sum(o.sum_dp[...], axis=0)
        out.wait()
        self.sends.drain("w")
        for group in list(self.outs.started):
            self.outs.drain(group)


class Local:
    def __init__(self, o):
        self.o = o
        self.loads = [pltpu.make_async_copy(o.weight.at[j], o.w.at[j], o.load_sem.at[1 + j]) for j in range(SECTIONS)]
        self.stores = {}

    def begin(self):
        for load in self.loads:
            load.start()

    def first(self):
        self.loads[0].wait()

    def first_rest(self):
        pass

    def own_step(self, step):
        pass

    def settle(self, j):
        self.loads[j].wait()

    def sum_start(self, j):
        copy = pltpu.make_async_copy(self.o.dw.at[j % 2], self.o.dweight.at[j], self.o.load_sem.at[1 + j])
        copy.start()
        self.stores[j] = copy

    def sum_step(self, j, step):
        if step == 2:
            self.stores[j].wait()

    def finish(self):
        self.o.dsmall[...] = self.o.small[...]


def kernel(size, spread, *refs):
    names = INPUTS + OUTPUTS + (LANDING if spread else ()) + tuple(SCRATCH)
    if spread:
        names += tuple(spread_scratch(size))
    o = Names(names, refs)
    me = lax.axis_index("section")
    dp = lax.axis_index("dp")

    barrier = pltpu.get_barrier_semaphore()
    peers = [(me ^ r, dp) for r in range(1, SECTIONS)]
    if spread:
        peers += [(me, dp ^ k) for k in range(1, size)]
    else:
        o.par = o.par_in
    for peer in peers:
        pl.semaphore_signal(barrier, inc=1, device_id=peer, device_id_type=MESH)

    net = Spread(o, me, dp, size) if spread else Local(o)
    count = o.counts[me]
    load_x = pltpu.make_async_copy(o.inputs.at[me], o.x, o.load_sem.at[0])
    load_cot = pltpu.make_async_copy(o.cot.at[me], o.igs.at[0], o.load_sem.at[5])
    load_x.start()
    load_cot.start()
    net.begin()
    pl.semaphore_wait(barrier, len(peers))

    def deliver(block, out, j, send, recv, action):
        @pl.when(me == j)
        def _():
            if action == "start":
                pltpu.make_async_copy(block, out.at[j], recv.at[j]).start()

        @pl.when(me != j)
        def _():
            copy = pltpu.make_async_remote_copy(
                src_ref=block,
                dst_ref=out.at[me],
                send_sem=send.at[j],
                recv_sem=recv.at[me],
                device_id=(j, dp),
                device_id_type=MESH,
            )
            copy.start() if action == "start" else copy.wait_send()

    keep = pltpu.make_async_copy(o.probs, o.kept, o.load_sem.at[6])
    bring = pltpu.make_async_copy(o.kept, o.probs, o.load_sem.at[7])

    load_x.wait()
    net.first()
    for j in range(SECTIONS):
        layer = j // 2
        h = o.x if j == 0 else o.ys.at[j - 1]
        w, par, y, normed = o.w.at[j], o.par.at[j], o.ys.at[j], o.norms.at[j]
        if j > 0:
            net.settle(j)
        if j % 2 == 0:
            if j == 2:
                keep.wait()

            def between(step, j=j):
                if j == 0:
                    if step == 0:
                        net.own_step(0)
                    else:
                        net.own_step(1)
                        net.first_rest()

            attend_forward(
                j, h, w, par, count, o.qkvs.at[layer], o.probs, o.atts.at[layer], o.stat, normed, y, between
            )
            if j == 0:
                keep.start()
        else:
            f = o.ffs.at[layer]
            feed_forward(j, h, w, par, count, f.at[:, :FF], f.at[:, FF:], o.stat, normed, y)
        deliver(y, o.acts, j, o.act_send, o.act_recv, "start")

    load_cot.wait()
    for j in reversed(range(SECTIONS)):
        layer = j // 2
        h = o.x if j == 0 else o.ys.at[j - 1]
        w, par, normed = o.w.at[j], o.par.at[j], o.norms.at[j]
        ig, small, dw = o.igs.at[j], o.small.at[j], o.dw.at[j % 2]

        def gy_of(r, j=j):
            rows = pl.ds(r, TILE)
            if j == SECTIONS - 1:
                return o.igs[0, rows, :].astype(F32) * live_rows(count, r, TILE)
            return o.igs[j + 1, rows, :].astype(F32)

        f = o.ffs.at[layer]
        if j % 2 == 0:
            if j == 0:
                bring.wait()
            pool = o.ffs.at[1]
            gqkv, gatt = pool.at[:, : 3 * D], pool.at[:, 3 * D :]

            def between(step, j=j):
                if j == 0:
                    net.sum_step(2, step + 1)
                net.sum_step(j + 1, step)

            attend_backward(
                j, gy_of, w, par, o.qkvs.at[layer], o.probs, o.atts.at[layer], o.stat, normed, o.gb, gatt, gqkv,
                o.gkv, o.gres, ig, small, between,
            )
            if j == 2:
                bring.start()
        else:
            feed_backward(j, gy_of, w, par, f.at[:, :FF], f.at[:, FF:], o.stat, normed, o.gb, ig, small)
        deliver(ig, o.grads, j, o.ig_send, o.ig_recv, "start")
        if j == 2:
            net.sum_step(3, 2)
        if j == 1:
            net.sum_step(2, 0)
        if spread and j < 2:
            net.outs.drain(j + 2)
        if j % 2 == 0:
            attend_weights(h, o.atts.at[layer], gqkv, o.gb, o.flip, dw)
        else:
            feed_weights(h, f.at[:, :FF], f.at[:, FF:], o.gb, o.flip, dw)
        net.sum_start(j)

    net.sum_step(1, 2)
    for step in range(3):
        net.sum_step(0, step)
    net.finish()
    for j in range(SECTIONS):
        deliver(o.ys.at[j], o.acts, j, o.act_send, o.act_recv, "sent")
        deliver(o.igs.at[j], o.grads, j, o.ig_send, o.ig_recv, "sent")
    for n in range(SECTIONS):
        landed(o.acts.at[n], o.act_recv.at[n])
        landed(o.grads.at[n], o.ig_recv.at[n])


def shards(inputs, cotangent, query_counts, section_weight, section_bias, section_norm):
    dp = lax.axis_index("dp")
    size = lax.axis_size("dp")
    block = section_weight.shape[1]
    spread = size == 8

    if spread:
        bias = lax.dynamic_update_slice(jnp.zeros((3 * D,), F32), section_bias[0].astype(F32), (dp * section_bias.shape[1],))
        norm = lax.dynamic_update_slice(jnp.zeros((2, D), F32), section_norm[0].astype(F32), (0, dp * section_norm.shape[2]))
        weight = section_weight
        par = jnp.concatenate([bias.reshape(3, D), norm, jnp.zeros((3, D), F32)], axis=0)
    else:

        def gathered(v, axis):
            v = lax.all_gather(v, "dp", axis=axis, tiled=True)
            return lax.all_gather(v, "section", axis=0, tiled=True)

        weight = gathered(section_weight, 1)
        bias = gathered(section_bias, 1)
        norm = gathered(section_norm, 2)
        par = jnp.concatenate([bias.reshape(SECTIONS, 3, D), norm, jnp.zeros((SECTIONS, 3, D), BF)], axis=1).astype(F32)

    anywhere = pl.BlockSpec(memory_space=pl.ANY)
    whole = pl.BlockSpec(memory_space=pltpu.VMEM)
    half = size // 2
    if spread:
        grad_shapes = [((1, block, 4 * D), F32), ((8, D), F32)]
        landing = [
            ((SECTIONS, half, block, 4 * D), BF),
            ((SECTIONS, half // 2, block, 4 * D), BF),
            ((SECTIONS, block, 4 * D), BF),
            ((SECTIONS, block, 4 * D), BF),
        ]
    else:
        grad_shapes = [((SECTIONS, D, 4 * D), BF), ((SECTIONS, 8, D), F32)]
        landing = []
    out_shapes = [((SECTIONS, ROWS, D), BF)] * 2 + grad_shapes + [((HEADS, ROWS, CTX), BF)] + landing
    scratch = list(SCRATCH.values())
    if spread:
        scratch += list(spread_scratch(size).values())
    results = pl.pallas_call(
        functools.partial(kernel, size, spread),
        out_shape=[jax.ShapeDtypeStruct(*s) for s in out_shapes],
        in_specs=[anywhere, anywhere, pl.BlockSpec(memory_space=pltpu.SMEM), anywhere, whole],
        out_specs=[anywhere, anywhere, anywhere, whole] + [anywhere] * (1 + len(landing)),
        scratch_shapes=scratch,
        compiler_params=pltpu.CompilerParams(
            collective_id=0, has_side_effects=True, vmem_limit_bytes=63 * MIB
        ),
    )(inputs, cotangent, query_counts, weight, par)
    acts, grads, dweight, dsmall = results[:4]

    if spread:
        db = lax.dynamic_slice(dsmall[:3].reshape(3 * D), (dp * section_bias.shape[1],), section_bias.shape[1:])[None]
        dn = lax.dynamic_slice(dsmall[3:5], (0, dp * section_norm.shape[2]), section_norm.shape[1:])[None]
        return acts[None], grads[None], dweight, db, dn

    def scattered(v, axis):
        v = lax.psum_scatter(v, "dp", scatter_dimension=axis, tiled=True)
        return lax.psum_scatter(v, "section", scatter_dimension=0, tiled=True)

    dw = scattered(dweight, 1).astype(F32)
    db = scattered(dsmall[:, :3].reshape(SECTIONS, 3 * D), 1)
    dn = scattered(dsmall[:, 3:5], 2)
    return acts[None], grads[None], dw, db, dn


def solution(mesh):
    return jax.shard_map(
        shards,
        mesh=mesh,
        in_specs=(
            P("dp", None, None),
            P("dp", None, None),
            P("dp"),
            P("section", "dp", None),
            P("section", "dp"),
            P("section", None, "dp"),
        ),
        out_specs=(
            P("section", "dp", None, None),
            P("section", "dp", None, None),
            P("section", "dp", None),
            P("section", "dp"),
            P("section", None, "dp"),
        ),
        check_vma=False,
    )
```

```python
import functools
import math

import jax
import jax.numpy as jnp
from jax import lax
from jax.experimental import pallas as pl
from jax.experimental.pallas import tpu as pltpu
from jax.sharding import PartitionSpec as P

D = 512
HEADS = 4
HEAD = 128
FF = 1024
CTX = 896
ROWS = 1024
SECTIONS = 4
TILE = 256
F32 = jnp.float32
BF = jnp.bfloat16
LOG2E = math.log2(math.e)
MESH = pl.DeviceIdType.MESH
MIB = 1 << 20


def dot(a, b):
    return lax.dot_general(a, b, (((1,), (0,)), ((), ())), preferred_element_type=F32)


def dot_t(a, b):
    return lax.dot_general(a, b, (((1,), (1,)), ((), ())), preferred_element_type=F32)


def t_dot(a, b):
    return lax.dot_general(a, b, (((0,), (0,)), ((), ())), preferred_element_type=F32)


def colsum(x):
    return jnp.sum(x, axis=0, keepdims=True)


def rows_loop(total, step, body):
    def one(i, carry):
        body(pl.multiple_of(i * step, step))
        return carry

    lax.fori_loop(0, total // step, one, 0)


LANE_RSTD = 0
LANE_NORMAL = 8
LANE_INNER = 16


def norm_forward(res, par):
    mean = jnp.mean(res, axis=-1, keepdims=True)
    center = res - mean
    inverse = lax.rsqrt(jnp.mean(center * center, axis=-1, keepdims=True) + 1e-5)
    normed = center * inverse
    return normed * par[3:4, :] + par[4:5, :], normed, inverse


def norm_backward(gy, normed, inverse, par):
    u = gy * par[3:4, :]
    m1 = jnp.mean(u, axis=-1, keepdims=True)
    m2 = jnp.mean(u * normed, axis=-1, keepdims=True)
    return inverse * (u - m1 - normed * m2)


def live_rows(count, begin, n):
    ids = lax.broadcasted_iota(jnp.int32, (n, 1), 0) + begin
    return jnp.where(ids < CTX + count, 1.0, 0.0).astype(F32)


def gelu_parts(z):
    t = 1.0 / (1.0 + (0.3275911 / math.sqrt(2.0)) * jnp.abs(z))
    e = jnp.exp2(z * z * (-0.5 * LOG2E))
    a = [0.254829592, -0.284496736, 1.421413741, -1.453152027, 1.061405429]
    a = [0.5 * v for v in a]
    tail = t * (a[0] + t * (a[1] + t * (a[2] + t * (a[3] + t * a[4])))) * e
    phi = jnp.where(z >= 0, 1.0 - tail, tail)
    return z * phi, phi + z * e * (1.0 / math.sqrt(2 * math.pi))


def ahead(items, first, second):
    ready = first(items[0])
    for i, item in enumerate(items):
        now = ready
        if i + 1 < len(items):
            ready = first(items[i + 1])
        second(item, now)


def finish_forward(j, res, par, count, begin, normed, stat, y):
    rows = pl.ds(begin, res.shape[0])
    out, unit, inverse = norm_forward(res, par)
    out = out * live_rows(count, begin, res.shape[0])
    y[rows, :] = out.astype(BF)
    normed[rows, :] = unit.astype(BF)
    stat[rows, LANE_RSTD + j : LANE_RSTD + j + 1] = inverse


def attend_forward(j, h, w, par, count, qkv, probs, att, stat, normed, y, between):
    factor = LOG2E / math.sqrt(HEAD)
    lane = LANE_NORMAL + 2 * j
    x = h[...]
    for c in range(0, 3 * D, 256):
        z = dot(x, w[:, c : c + 256])
        if c < D:
            z = (z + par[0:1, c : c + 256]) * factor
        elif c >= 2 * D:
            z = z + par[1:2, c - 2 * D : c - 2 * D + 256]
        qkv[:, c : c + 256] = z.astype(BF)
    between(0)
    step = 512

    def score(item):
        r, hd = item
        c = hd * HEAD
        return dot_t(qkv[pl.ds(r, step), c : c + HEAD], qkv[0:CTX, D + c : D + c + HEAD])

    def attend(item, s):
        r, hd = item
        c = hd * HEAD
        rows = pl.ds(r, step)
        e = jnp.exp2(s - jnp.max(s, axis=-1, keepdims=True))
        normal = 1.0 / jnp.sum(e, axis=-1, keepdims=True)
        low = e.astype(BF)
        probs[hd, rows, :] = low
        stat[rows, lane + hd : lane + hd + 1] = normal
        o = dot(low, qkv[0:CTX, 2 * D + c : 2 * D + c + HEAD])
        att[rows, c : c + HEAD] = (o * normal).astype(BF)
        if hd == HEADS - 1:
            for t in range(0, step, TILE):
                q = r + t
                out = pl.ds(q, TILE)
                res = dot(att[out, :], w[:, 3 * D : 4 * D]) + par[2:3, :] + h[out, :].astype(F32)
                finish_forward(j, res, par, count, q, normed, stat, y)

    ahead([(r, hd) for r in range(0, ROWS, step) for hd in range(HEADS)], score, attend)
    between(1)


def feed_forward(j, h, w, par, count, act, slope, stat, normed, y):
    width = 512

    def first(item):
        r, k = item
        return dot(h[r : r + TILE, :], w[:, k * width : (k + 1) * width])

    def second(item, z):
        r, k = item
        rows = pl.ds(r, TILE)
        c = k * width
        g, dg = gelu_parts(z + par[k : k + 1, :])
        act[rows, c : c + width] = g.astype(BF)
        slope[rows, c : c + width] = dg.astype(BF)
        if k == 1:
            res = dot_t(act[rows, :], w[:, FF:]) + par[2:3, :] + h[rows, :].astype(F32)
            finish_forward(j, res, par, count, r, normed, stat, y)

    ahead([(r, k) for r in range(0, ROWS, TILE) for k in range(2)], first, second)


def start_backward(j, r, gy, par, normed, stat, gb, small):
    rows = pl.ds(r, TILE)
    unit = normed[rows, :].astype(F32)
    gres = norm_backward(gy, unit, stat[rows, LANE_RSTD + j : LANE_RSTD + j + 1], par)
    small[3:4, :] += colsum(gy * unit)
    small[4:5, :] += colsum(gy)
    low = gres.astype(BF)
    gb[rows, :] = low
    small[2:3, :] += colsum(low.astype(F32))
    return low


def feed_backward(j, gy_of, w, par, act, slope, stat, normed, gb, ig, small):
    small[...] = jnp.zeros(small.shape, F32)

    def first(r):
        low = start_backward(j, r, gy_of(r), par, normed, stat, gb, small)
        return [dot(low, w[:, FF + c : FF + c + 512]) for c in (0, 512)]

    def second(r, gas):
        rows = pl.ds(r, TILE)
        for k, ga in enumerate(gas):
            c = k * 512
            gp = (ga * slope[rows, c : c + 512].astype(F32)).astype(BF)
            slope[rows, c : c + 512] = gp
            small[k : k + 1, :] += colsum(gp.astype(F32))
        ig[rows, :] = (gb[rows, :].astype(F32) + dot_t(slope[rows, :], w[:, 0:FF])).astype(BF)

    ahead(list(range(0, ROWS, TILE)), first, second)


def flipped(flip, v):
    for r in (0, 512):
        flip[r : r + 512, :] = v[r : r + 512, :].T


def put_weights(dw, chunk, flip, v, c=0):
    z = dot(flip[0:512, :], v[0:512, c : c + 512]) + dot(flip[512:1024, :], v[512:1024, c : c + 512])
    z = z.astype(BF)
    c = chunk * 512
    for d in range(8):
        high = (d >> 2) * 64
        dw[d & 1, (d >> 1) & 1, high : high + 64, c : c + 512] = z[d * 64 : d * 64 + 64]


def feed_weights(h, act, gpre, gb, flip, dw, clear, done):
    flipped(flip, h)
    for k in range(2):
        clear(k)
        put_weights(dw, k, flip, gpre, k * 512)
        done(k)
    flipped(flip, gb)
    for k in range(2):
        clear(2 + k)
        put_weights(dw, 2 + k, flip, act, k * 512)
        done(2 + k)


def attend_backward(j, h, gy_of, w, par, qkv, probs, att, stat, normed, gb, gatt, gqkv, ig, small, dw, clear,
                    done, tick):
    lane = LANE_NORMAL + 2 * j
    small[...] = jnp.zeros(small.shape, F32)

    def first(r):
        low = start_backward(j, r, gy_of(r), par, normed, stat, gb, small)
        return dot_t(low, w[:, 3 * D : 4 * D])

    def second(r, ga):
        rows = pl.ds(r, TILE)
        a = att[rows, :].astype(F32)
        for hd in range(HEADS):
            c = hd * HEAD
            g = ga[:, c : c + HEAD] * stat[rows, lane + hd : lane + hd + 1]
            gatt[rows, c : c + HEAD] = g.astype(BF)
            stat[rows, LANE_INNER + hd : LANE_INNER + hd + 1] = jnp.sum(
                g * a[:, c : c + HEAD], axis=-1, keepdims=True
            )

    ahead(list(range(0, ROWS, TILE)), first, second)
    tick(3.0)
    flipped(normed, att)
    clear(3)
    put_weights(dw, 3, normed, gb)
    done(3)
    flipped(normed, h)
    gqkv[CTX:ROWS, D : 3 * D] = jnp.zeros((ROWS - CTX, 2 * D), BF)

    def values(hd, carry):
        lanes = pl.ds(pl.multiple_of(hd * HEAD, HEAD), HEAD)
        gv = t_dot(gatt[:, lanes], probs[hd])
        gqkv[0:CTX, pl.ds(pl.multiple_of(2 * D + hd * HEAD, HEAD), HEAD)] = gv.T.astype(BF)
        return carry

    lax.fori_loop(0, HEADS, values, 0)
    tick(1.0)
    clear(2)
    put_weights(dw, 2, normed, gqkv, 2 * D)
    done(2)
    step = 512

    def first(item):
        hd, r = item
        c = hd * HEAD
        return dot_t(gatt[r : r + step, c : c + HEAD], qkv[0:CTX, 2 * D + c : 2 * D + c + HEAD])

    def second(item, gp):
        hd, r = item
        c = hd * HEAD
        rows = pl.ds(r, step)
        inner = stat[rows, LANE_INNER + hd : LANE_INNER + hd + 1]
        gs = (probs[hd, rows, :].astype(F32) * (gp - inner)).astype(BF)
        probs[hd, rows, :] = gs
        gq = dot(gs, qkv[0:CTX, D + c : D + c + HEAD])
        gqkv[rows, c : c + HEAD] = (gq * (1.0 / math.sqrt(HEAD))).astype(BF)

    for pair in (0, 2):
        ahead([(hd, r) for hd in (pair, pair + 1) for r in range(0, ROWS, step)], first, second)
        tick(2.3)

    def keys(hd, carry):
        lanes = pl.ds(pl.multiple_of(hd * HEAD, HEAD), HEAD)
        gk = t_dot(qkv[:, lanes], probs[hd])
        gqkv[0:CTX, pl.ds(pl.multiple_of(D + hd * HEAD, HEAD), HEAD)] = (gk * (1.0 / LOG2E)).T.astype(BF)
        return carry

    lax.fori_loop(0, HEADS, keys, 0)
    tick(1.8)
    for r in range(0, ROWS, TILE):
        rows = pl.ds(r, TILE)
        ig[rows, :] = (gb[rows, :].astype(F32) + dot_t(gqkv[rows, :], w[:, 0 : 3 * D])).astype(BF)
        small[0:1, :] += colsum(gqkv[rows, 0:D].astype(F32))
        small[1:2, :] += colsum(gqkv[rows, 2 * D : 3 * D].astype(F32))


def attend_weights(gqkv, flip, dw, clear, done):
    for k in (1, 0):
        clear(k)
        put_weights(dw, k, flip, gqkv, k * D)
        done(k)


def vm(*shape, dtype=BF):
    return pltpu.VMEM(shape, dtype)


SCRATCH = dict(
    x=vm(ROWS, D),
    w=vm(SECTIONS, D, 4 * D),
    ys=vm(SECTIONS - 1, ROWS, D),
    igs=vm(SECTIONS, ROWS, D),
    norms=vm(SECTIONS, ROWS, D),
    qkvs=vm(2, ROWS, 3 * D),
    atts=vm(2, ROWS, D),
    ffs=vm(2, ROWS, 2 * FF),
    probs=vm(HEADS, ROWS, CTX),
    stat=vm(ROWS, 128, dtype=F32),
    gb=vm(ROWS, D),
    dw=vm(2, 2, 128, 4 * D),
    small=vm(SECTIONS, 8, D, dtype=F32),
    load_sem=pltpu.SemaphoreType.DMA((8,)),
    act_send=pltpu.SemaphoreType.DMA((SECTIONS,)),
    act_recv=pltpu.SemaphoreType.DMA((SECTIONS,)),
    ig_send=pltpu.SemaphoreType.DMA((SECTIONS,)),
    ig_recv=pltpu.SemaphoreType.DMA((SECTIONS,)),
)


def spread_scratch(size):
    sem = pltpu.SemaphoreType.DMA
    return dict(
        parts=vm(size, 8, D, dtype=F32),
        par=vm(SECTIONS, 8, D, dtype=F32),
        sum_plane=vm(SECTIONS, 8, D, dtype=F32),
        sum_dp=vm(size, 8, D, dtype=F32),
        land_a=vm(SECTIONS, 4, 2, 2 * (D // size), 512),
        land_b=vm(2, 4, 2 * (D // size), 512),
        land_c=vm(2, 4, D // size, 512),
        land_d=vm(SECTIONS, 4, D // size, 512),
        last=vm(D // size, 4 * D, dtype=F32),
        w_recv=sem((SECTIONS, size)),
        w_send=sem((96,)),
        parts_recv=sem((size,)),
        par_recv=sem((SECTIONS,)),
        a_recv=sem((SECTIONS, 4)),
        b_recv=sem((SECTIONS, 4)),
        c_recv=sem((SECTIONS, 4)),
        d_recv=sem((SECTIONS, 4)),
        sp_recv=sem((SECTIONS,)),
        sd_recv=sem((size,)),
        dw_send=sem((128,)),
    )


class Names:
    def __init__(self, names, refs):
        self.__dict__.update(zip(names, refs, strict=True))


INPUTS = ("inputs", "cot", "counts", "weight", "par_in")
OUTPUTS = ("acts", "grads", "dweight", "dsmall", "kept")


class Sends:
    def __init__(self, sems):
        self.sems, self.used, self.started = sems, 0, {}

    def push(self, group, src, dst, recv_sem, target, when=None):
        k = self.used
        self.used += 1
        assert k < self.sems.shape[0]

        def copy():
            return pltpu.make_async_remote_copy(
                src_ref=src,
                dst_ref=dst,
                send_sem=self.sems.at[k],
                recv_sem=recv_sem,
                device_id=target,
                device_id_type=MESH,
            )

        self.started.setdefault(group, []).append((when, copy))
        guarded(when, lambda: copy().start())

    def drain(self, group):
        for when, copy in self.started.pop(group, ()):
            guarded(when, lambda copy=copy: copy().wait_send())


def guarded(when, action):
    if when is None:
        action()
    else:
        pl.when(when)(action)


def landed(dst, sem):
    pltpu.make_async_copy(dst, dst, sem).wait()


class Spread:
    def __init__(self, o, me, dp, size):
        self.o, self.me, self.dp, self.size = o, me, dp, size
        self.block = D // size
        self.sends = Sends(o.w_send)
        self.outs = Sends(o.dw_send)
        self.own = (dp, dp ^ 2, dp ^ 4, dp ^ 6)
        self.now, self.free, self.state = 0.0, {}, {}


    def shard(self, j, d):
        rows = pl.ds(pl.multiple_of(d * self.block, self.block), self.block)
        return self.o.w.at[j, rows, :]

    def send_shard(self, j, d, section, dp, when=None):
        ref = self.shard(j, d)
        self.sends.push("w", ref, ref, self.o.w_recv.at[j, d], (section, dp), when)

    def wait_shard(self, j, d):
        landed(self.shard(j, d), self.o.w_recv.at[j, d])

    def begin(self):
        o, me, dp = self.o, self.me, self.dp
        load = pltpu.make_async_copy(o.weight.at[0], self.shard(me, dp), o.load_sem.at[1])
        load.start()
        o.parts[dp, :, :] = o.par_in[...]
        load.wait()

    def spread_own(self, d, r, when=None):
        self.send_shard(self.me, d, self.me ^ r, self.dp, when)

    def to_core(self, d):
        self.send_shard(self.me, d, self.me, self.dp ^ 1)

    def pass_on(self, r, d, when):
        me, dp = self.me, self.dp
        pl.when(when)(lambda: self.wait_shard(me ^ r, d))
        self.send_shard(me ^ r, d, me ^ (3 - r), dp, when)
        self.send_shard(me ^ r, d, me, dp ^ 1, when)

    def first(self):
        o, me, dp = self.o, self.me, self.dp
        d0, d1, d2, d3 = self.own
        self.send_shard(me, d0, me, d2)
        self.send_shard(me, d0, me, d1)
        self.spread_own(d0, 1)
        self.spread_own(d0, 2)
        self.to_core(d0)
        for k in range(1, self.size):
            self.sends.push("w", o.parts.at[dp], o.parts.at[dp], o.parts_recv.at[dp], (me, dp ^ k))
        self.wait_shard(me, d1)
        self.spread_own(d1, 1, me != 2)
        self.spread_own(d1, 2, me != 1)
        self.to_core(d1)
        self.pass_on(1, d0, me & 1 == 1)
        self.wait_shard(me, d2)
        self.send_shard(me, d2, me, d1)
        self.spread_own(d2, 1, me != 2)
        self.spread_own(d2, 2, me != 1)
        self.to_core(d2)
        self.pass_on(2, d1, me >= 2)
        for k in range(1, self.size):
            landed(o.parts.at[dp ^ k], o.parts_recv.at[dp ^ k])
        o.par[me, :, :] = jnp.sum(o.parts[...], axis=0)
        for r in range(1, SECTIONS):
            self.sends.push("w", o.par.at[me], o.par.at[me], o.par_recv.at[me], (me ^ r, dp))
        self.wait_shard(me, d3)
        self.spread_own(d3, 1, me != 2)
        self.spread_own(d3, 2, me != 1)
        self.to_core(d3)
        self.pass_on(1, d2, me & 1 == 1)
        self.pass_on(2, d3, me >= 2)
        for d in (d1, d2, d3):
            self.spread_own(d, 1, me == 2)
            self.spread_own(d, 2, me == 1)
        self.pass_on(1, d0, me & 1 == 0)
        self.pass_on(2, d1, me < 2)
        self.todo = {
            1: [d1, d3],
            2: [d0, d2],
            3: [d0, d1, d2, d3],
        }
        for r in range(1, SECTIONS):
            landed(o.par.at[me ^ r], o.par_recv.at[me ^ r])
        self.settle(0)

    def rest(self):
        _, _, d2, d3 = self.own
        self.pass_on(1, d2, self.me & 1 == 0)
        self.pass_on(2, d3, self.me < 2)

    def settle(self, j):
        me, dp = self.me, self.dp
        for r, shards_left in self.todo.items():

            @pl.when(me ^ r == j)
            def _(r=r, shards_left=shards_left):
                for d in shards_left:
                    self.wait_shard(j, d)

            for d in shards_left:
                self.send_shard(j, d, me, dp ^ 1, me ^ r == j)
        for d in self.own:
            self.wait_shard(j, d ^ 1)


    def expected(self, link, cost):
        self.free[link] = max(self.free.get(link, 0.0), self.now) + cost
        return self.free[link] + 2.0

    def done(self, j, q):
        o, me, dp = self.o, self.me, self.dp
        self.passed(0.65)
        part = o.dw.at[1 - (dp & 1), :, :, pl.ds(q * 512, 512)]
        self.outs.push((j, q), part, o.land_a.at[j, q], o.a_recv.at[j, q], (me, dp ^ 1))
        self.state[j, q] = ("b", self.expected("core", 0.6))

    def passed(self, us):
        self.now += us
        for unit in sorted(self.state, key=lambda u: (-u[0], u)):
            while self.state[unit][0] != "end" and self.state[unit][1] <= self.now and self.allowed(unit):
                self.step(unit)

    def allowed(self, unit):
        stage = self.state[unit][0]
        if unit[0] >= 2 or stage == "d":
            return True
        return self.state[2, 3][0] > ("c" if stage == "b" else "d")

    def landing(self, unit):
        o = self.o
        j, q = unit
        if j >= 2:
            return o.land_b.at[j - 2, q], o.land_c.at[j - 2, q]
        columns = pl.ds(q * 512, 512)
        return o.w.at[3, pl.ds(128 * j, 128), columns], o.w.at[3, pl.ds(256 + 64 * j, 64), columns]

    def step(self, unit):
        o, me, dp = self.o, self.me, self.dp
        j, q = unit
        core, zlow, zhigh = dp & 1, (dp >> 1) & 1, dp >> 2
        stage = self.state[unit][0]
        half, (land_b, land_c) = o.land_a.at[j, q], self.landing(unit)
        if stage == "b":
            landed(half, o.a_recv.at[j, q])
            mine = o.dw[core, :, :, q * 512 : q * 512 + 512]
            half[...] = (half[...].astype(F32) + mine.astype(F32)).astype(BF)
            self.outs.drain(unit)
            self.outs.push("z", half.at[1 - zlow], land_b, o.b_recv.at[j, q], (me, dp ^ 2))
            self.state[unit] = ("c", self.expected("near", 2.9))
        elif stage == "c":
            landed(land_b, o.b_recv.at[j, q])
            mine = half.at[zlow]
            mine[...] = (mine[...].astype(F32) + land_b[...].astype(F32)).astype(BF)
            there = pl.ds(pl.multiple_of((1 - zhigh) * 64, 64), 64)
            self.outs.push("z", mine.at[there], land_c, o.c_recv.at[j, q], (me, dp ^ 4))
            self.state[unit] = ("d", self.expected("far", 2.9))
        else:
            landed(land_c, o.c_recv.at[j, q])
            here = pl.ds(pl.multiple_of(zhigh * 64, 64), 64)
            total = half[zlow, here, :].astype(F32) + land_c[...].astype(F32)
            mine = o.norms.at[SECTIONS - 1, pl.ds((4 * j + q) * self.block, self.block)]
            mine[...] = total.astype(BF)
            self.outs.push("d", mine, o.land_d.at[me, q], o.d_recv.at[me, q], (j, dp), me != j)

            @pl.when(me == j)
            def _():
                o.last[:, q * 512 : q * 512 + 512] = total

            self.state[unit] = ("end", 0)

    def smalls(self, j):
        o, me, dp = self.o, self.me, self.dp
        self.outs.push("s", o.small.at[j], o.sum_plane.at[me], o.sp_recv.at[me], (j, dp), me != j)

        @pl.when(me == j)
        def _():
            o.sum_plane[me, :, :] = o.small[j, :, :]

    def reuse(self, j, q):
        if self.state[j, q][0] == "b":
            if not self.allowed((j, q)):
                self.force((2, 3), "c")
            self.step((j, q))

    def force(self, unit, stage):
        while self.state[unit][0] <= stage:
            self.step(unit)

    def release(self):
        self.sends.drain("w")

    def finish(self):
        o, me, dp = self.o, self.me, self.dp
        while any(stage != "end" for stage, _ in self.state.values()):
            self.passed(0.5)
        for r in range(1, SECTIONS):
            landed(o.sum_plane.at[me ^ r], o.sp_recv.at[me ^ r])
        o.sum_dp[dp, :, :] = jnp.sum(o.sum_plane[...], axis=0)
        for k in range(1, self.size):
            self.outs.push("s", o.sum_dp.at[dp], o.sum_dp.at[dp], o.sd_recv.at[dp], (me, dp ^ k))
        for r in range(1, SECTIONS):
            for q in range(4):
                landed(o.land_d.at[me ^ r, q], o.d_recv.at[me ^ r, q])
                o.last[:, q * 512 : q * 512 + 512] += o.land_d[me ^ r, q].astype(F32)
        out = pltpu.make_async_copy(o.last, o.dweight.at[0], o.load_sem.at[2])
        out.start()
        for k in range(1, self.size):
            landed(o.sum_dp.at[dp ^ k], o.sd_recv.at[dp ^ k])
        o.dsmall[...] = jnp.sum(o.sum_dp[...], axis=0)
        out.wait()
        for group in list(self.outs.started):
            self.outs.drain(group)


class Local:
    def __init__(self, o):
        self.o = o
        self.loads = [pltpu.make_async_copy(o.weight.at[j], o.w.at[j], o.load_sem.at[1 + j]) for j in range(SECTIONS)]
        self.stores, self.counted = {}, {}

    def begin(self):
        for load in self.loads:
            load.start()

    def first(self):
        self.loads[0].wait()

    def rest(self):
        pass

    def settle(self, j):
        self.loads[j].wait()

    def done(self, j, q):
        if j not in self.counted:
            self.counted[j] = 0
        self.counted[j] += 1
        if self.counted[j] == 4:
            copy = pltpu.make_async_copy(self.o.dw, self.o.dweight.at[j], self.o.load_sem.at[1 + j])
            copy.start()
            self.stores[j] = copy

    def passed(self, us):
        pass

    def smalls(self, j):
        pass

    def release(self):
        pass

    def reuse(self, j, q):
        if j in self.stores:
            self.stores.pop(j).wait()

    def finish(self):
        for copy in self.stores.values():
            copy.wait()
        self.o.dsmall[...] = self.o.small[...]


def kernel(size, spread, *refs):
    names = INPUTS + OUTPUTS + tuple(SCRATCH)
    if spread:
        names += tuple(spread_scratch(size))
    o = Names(names, refs)
    me = lax.axis_index("section")
    dp = lax.axis_index("dp")

    barrier = pltpu.get_barrier_semaphore()
    peers = [(me ^ r, dp) for r in range(1, SECTIONS)]
    if spread:
        peers += [(me, dp ^ k) for k in range(1, size)]
    else:
        o.par = o.par_in
    for peer in peers:
        pl.semaphore_signal(barrier, inc=1, device_id=peer, device_id_type=MESH)

    net = Spread(o, me, dp, size) if spread else Local(o)
    count = o.counts[me]
    load_x = pltpu.make_async_copy(o.inputs.at[me], o.x, o.load_sem.at[0])
    load_cot = pltpu.make_async_copy(o.cot.at[me], o.igs.at[1], o.load_sem.at[5])
    ys = [o.ys.at[0], o.ys.at[1], o.ys.at[2], o.igs.at[0]]
    igs = [o.norms.at[1], o.igs.at[1], o.igs.at[2], o.igs.at[3]]
    dw = o.dw
    load_x.start()
    load_cot.start()
    net.begin()
    pl.semaphore_wait(barrier, len(peers))

    def deliver(block, out, j, send, recv, action):
        @pl.when(me == j)
        def _():
            if action == "start":
                pltpu.make_async_copy(block, out.at[j], recv.at[j]).start()

        @pl.when(me != j)
        def _():
            copy = pltpu.make_async_remote_copy(
                src_ref=block,
                dst_ref=out.at[me],
                send_sem=send.at[j],
                recv_sem=recv.at[me],
                device_id=(j, dp),
                device_id_type=MESH,
            )
            copy.start() if action == "start" else copy.wait_send()

    keep = pltpu.make_async_copy(o.probs, o.kept, o.load_sem.at[6])
    bring = pltpu.make_async_copy(o.kept, o.probs, o.load_sem.at[7])

    load_x.wait()
    net.first()
    for j in range(SECTIONS):
        layer = j // 2
        h = o.x if j == 0 else ys[j - 1]
        w, par, y, normed = o.w.at[j], o.par.at[j], ys[j], o.norms.at[j]
        if j > 0:
            net.settle(j)
        if j % 2 == 0:
            if j == 2:
                keep.wait()

            def between(step):
                pass

            attend_forward(
                j, h, w, par, count, o.qkvs.at[layer], o.probs, o.atts.at[layer], o.stat, normed, y, between
            )
            if j == 0:
                keep.start()
                net.rest()
        else:
            f = o.ffs.at[layer]
            feed_forward(j, h, w, par, count, f.at[:, :FF], f.at[:, FF:], o.stat, normed, y)
        deliver(y, o.acts, j, o.act_send, o.act_recv, "start")

    load_cot.wait()
    for j in reversed(range(SECTIONS)):
        layer = j // 2
        h = o.x if j == 0 else ys[j - 1]
        w, par, normed = o.w.at[j], o.par.at[j], o.norms.at[j]
        ig, small = igs[j], o.small.at[j]

        def gy_of(r, j=j):
            rows = pl.ds(r, TILE)
            if j == SECTIONS - 1:
                return o.igs[1, rows, :].astype(F32) * live_rows(count, r, TILE)
            return o.igs[j + 1, rows, :].astype(F32)

        f = o.ffs.at[layer]

        def done(q, j=j):
            net.done(j, q)

        def clear(q, j=j):
            if j + 1 < SECTIONS:
                net.reuse(j + 1, q)

        if j == 2:
            net.release()
        if j % 2 == 0:
            if j == 0:
                bring.wait()
            pool = o.ffs.at[1]
            gqkv, gatt = pool.at[:, : 3 * D], pool.at[:, 3 * D :]
            attend_backward(
                j, h, gy_of, w, par, o.qkvs.at[layer], o.probs, o.atts.at[layer], o.stat, normed, o.gb, gatt, gqkv,
                ig, small, dw, clear, done, net.passed,
            )
            if j == 2:
                bring.start()
        else:
            feed_backward(j, gy_of, w, par, f.at[:, :FF], f.at[:, FF:], o.stat, normed, o.gb, ig, small)
        deliver(ig, o.grads, j, o.ig_send, o.ig_recv, "start")
        net.smalls(j)
        net.passed(2.0 if j % 2 == 0 else 3.8)
        if j % 2 == 0:
            attend_weights(gqkv, normed, dw, clear, done)
        else:
            feed_weights(h, f.at[:, :FF], f.at[:, FF:], o.gb, normed, dw, clear, done)

    net.finish()
    for j in range(SECTIONS):
        deliver(ys[j], o.acts, j, o.act_send, o.act_recv, "sent")
        deliver(igs[j], o.grads, j, o.ig_send, o.ig_recv, "sent")
    for n in range(SECTIONS):
        landed(o.acts.at[n], o.act_recv.at[n])
        landed(o.grads.at[n], o.ig_recv.at[n])


def shards(inputs, cotangent, query_counts, section_weight, section_bias, section_norm):
    dp = lax.axis_index("dp")
    size = lax.axis_size("dp")
    block = section_weight.shape[1]
    spread = size == 8

    if spread:
        bias = lax.dynamic_update_slice(jnp.zeros((3 * D,), F32), section_bias[0].astype(F32), (dp * section_bias.shape[1],))
        norm = lax.dynamic_update_slice(jnp.zeros((2, D), F32), section_norm[0].astype(F32), (0, dp * section_norm.shape[2]))
        weight = section_weight
        par = jnp.concatenate([bias.reshape(3, D), norm, jnp.zeros((3, D), F32)], axis=0)
    else:

        def gathered(v, axis):
            v = lax.all_gather(v, "dp", axis=axis, tiled=True)
            return lax.all_gather(v, "section", axis=0, tiled=True)

        weight = gathered(section_weight, 1)
        bias = gathered(section_bias, 1)
        norm = gathered(section_norm, 2)
        par = jnp.concatenate([bias.reshape(SECTIONS, 3, D), norm, jnp.zeros((SECTIONS, 3, D), BF)], axis=1).astype(F32)

    anywhere = pl.BlockSpec(memory_space=pl.ANY)
    whole = pl.BlockSpec(memory_space=pltpu.VMEM)
    if spread:
        grad_shapes = [((1, block, 4 * D), F32), ((8, D), F32)]
    else:
        grad_shapes = [((SECTIONS, 2, 2, 128, 4 * D), BF), ((SECTIONS, 8, D), F32)]
    out_shapes = [((SECTIONS, ROWS, D), BF)] * 2 + grad_shapes + [((HEADS, ROWS, CTX), BF)]
    scratch = list(SCRATCH.values())
    if spread:
        scratch += list(spread_scratch(size).values())
    results = pl.pallas_call(
        functools.partial(kernel, size, spread),
        out_shape=[jax.ShapeDtypeStruct(*s) for s in out_shapes],
        in_specs=[anywhere, anywhere, pl.BlockSpec(memory_space=pltpu.SMEM), anywhere, whole],
        out_specs=[anywhere, anywhere, anywhere, whole] + [anywhere],
        scratch_shapes=scratch,
        compiler_params=pltpu.CompilerParams(
            collective_id=0, has_side_effects=True, vmem_limit_bytes=63 * MIB
        ),
    )(inputs, cotangent, query_counts, weight, par)
    acts, grads, dweight, dsmall = results[:4]

    if spread:
        db = lax.dynamic_slice(dsmall[:3].reshape(3 * D), (dp * section_bias.shape[1],), section_bias.shape[1:])[None]
        dn = lax.dynamic_slice(dsmall[3:5], (0, dp * section_norm.shape[2]), section_norm.shape[1:])[None]
        return acts[None], grads[None], dweight, db, dn

    def scattered(v, axis):
        v = lax.psum_scatter(v, "dp", scatter_dimension=axis, tiled=True)
        return lax.psum_scatter(v, "section", scatter_dimension=0, tiled=True)

    dweight = dweight.reshape(SECTIONS, 2, 2, 2, 64, 4 * D).transpose(0, 3, 2, 1, 4, 5)
    dw = scattered(dweight.reshape(SECTIONS, D, 4 * D), 1).astype(F32)
    db = scattered(dsmall[:, :3].reshape(SECTIONS, 3 * D), 1)
    dn = scattered(dsmall[:, 3:5], 2)
    return acts[None], grads[None], dw, db, dn


def solution(mesh):
    return jax.shard_map(
        shards,
        mesh=mesh,
        in_specs=(
            P("dp", None, None),
            P("dp", None, None),
            P("dp"),
            P("section", "dp", None),
            P("section", "dp"),
            P("section", None, "dp"),
        ),
        out_specs=(
            P("section", "dp", None, None),
            P("section", "dp", None, None),
            P("section", "dp", None),
            P("section", "dp"),
            P("section", None, "dp"),
        ),
        check_vma=False,
    )
```

```python
import functools
import math

import jax
import jax.numpy as jnp
from jax import lax
from jax.experimental import pallas as pl
from jax.experimental.pallas import tpu as pltpu
from jax.sharding import PartitionSpec as P

D = 512
HEADS = 4
HEAD = 128
FF = 1024
CTX = 896
ROWS = 1024
SECTIONS = 4
TILE = 256
F32 = jnp.float32
BF = jnp.bfloat16
LOG2E = math.log2(math.e)
MESH = pl.DeviceIdType.MESH
MIB = 1 << 20


def dot(a, b):
    return lax.dot_general(a, b, (((1,), (0,)), ((), ())), preferred_element_type=F32)


def dot_t(a, b):
    return lax.dot_general(a, b, (((1,), (1,)), ((), ())), preferred_element_type=F32)


def t_dot(a, b):
    return lax.dot_general(a, b, (((0,), (0,)), ((), ())), preferred_element_type=F32)


def colsum(x):
    return jnp.sum(x, axis=0, keepdims=True)


def rows_loop(total, step, body):
    def one(i, carry):
        body(pl.multiple_of(i * step, step))
        return carry

    lax.fori_loop(0, total // step, one, 0)


LANE_RSTD = 0
LANE_NORMAL = 8
LANE_INNER = 16


def norm_forward(res, par):
    mean = jnp.mean(res, axis=-1, keepdims=True)
    center = res - mean
    inverse = lax.rsqrt(jnp.mean(center * center, axis=-1, keepdims=True) + 1e-5)
    normed = center * inverse
    return normed * par[3:4, :] + par[4:5, :], normed, inverse


def norm_backward(gy, normed, inverse, par):
    u = gy * par[3:4, :]
    m1 = jnp.mean(u, axis=-1, keepdims=True)
    m2 = jnp.mean(u * normed, axis=-1, keepdims=True)
    return inverse * (u - m1 - normed * m2)


def live_rows(count, begin, n):
    ids = lax.broadcasted_iota(jnp.int32, (n, 1), 0) + begin
    return jnp.where(ids < CTX + count, 1.0, 0.0).astype(F32)


def gelu_parts(z):
    t = 1.0 / (1.0 + (0.3275911 / math.sqrt(2.0)) * jnp.abs(z))
    e = jnp.exp2(z * z * (-0.5 * LOG2E))
    a = [0.254829592, -0.284496736, 1.421413741, -1.453152027, 1.061405429]
    a = [0.5 * v for v in a]
    tail = t * (a[0] + t * (a[1] + t * (a[2] + t * (a[3] + t * a[4])))) * e
    phi = jnp.where(z >= 0, 1.0 - tail, tail)
    return z * phi, phi + z * e * (1.0 / math.sqrt(2 * math.pi))


def ahead(items, first, second):
    ready = first(items[0])
    for i, item in enumerate(items):
        now = ready
        if i + 1 < len(items):
            ready = first(items[i + 1])
        second(item, now)


def finish_forward(j, res, par, count, begin, normed, stat, y):
    rows = pl.ds(begin, res.shape[0])
    out, unit, inverse = norm_forward(res, par)
    out = out * live_rows(count, begin, res.shape[0])
    y[rows, :] = out.astype(BF)
    normed[rows, :] = unit.astype(BF)
    stat[rows, LANE_RSTD + j : LANE_RSTD + j + 1] = inverse


def attend_forward(j, h, w, par, count, qkv, probs, att, stat, normed, y, between):
    factor = LOG2E / math.sqrt(HEAD)
    lane = LANE_NORMAL + 2 * j
    x = h[...]
    for c in range(0, 3 * D, 256):
        z = dot(x, w[:, c : c + 256])
        if c < D:
            z = (z + par[0:1, c : c + 256]) * factor
        elif c >= 2 * D:
            z = z + par[1:2, c - 2 * D : c - 2 * D + 256]
        qkv[:, c : c + 256] = z.astype(BF)
    between(0)
    step = 512

    def score(item):
        r, hd = item
        c = hd * HEAD
        return dot_t(qkv[pl.ds(r, step), c : c + HEAD], qkv[0:CTX, D + c : D + c + HEAD])

    def attend(item, s):
        r, hd = item
        c = hd * HEAD
        rows = pl.ds(r, step)
        e = jnp.exp2(s - jnp.max(s, axis=-1, keepdims=True))
        normal = 1.0 / jnp.sum(e, axis=-1, keepdims=True)
        low = e.astype(BF)
        probs[hd, rows, :] = low
        stat[rows, lane + hd : lane + hd + 1] = normal
        o = dot(low, qkv[0:CTX, 2 * D + c : 2 * D + c + HEAD])
        att[rows, c : c + HEAD] = (o * normal).astype(BF)
        if hd == HEADS - 1:
            for t in range(0, step, TILE):
                q = r + t
                out = pl.ds(q, TILE)
                res = dot(att[out, :], w[:, 3 * D : 4 * D]) + par[2:3, :] + h[out, :].astype(F32)
                finish_forward(j, res, par, count, q, normed, stat, y)

    ahead([(r, hd) for r in range(0, ROWS, step) for hd in range(HEADS)], score, attend)
    between(1)


def feed_forward(j, h, w, par, count, act, slope, stat, normed, y):
    width = 512

    def first(item):
        r, k = item
        return dot(h[r : r + TILE, :], w[:, k * width : (k + 1) * width])

    def second(item, z):
        r, k = item
        rows = pl.ds(r, TILE)
        c = k * width
        g, dg = gelu_parts(z + par[k : k + 1, :])
        act[rows, c : c + width] = g.astype(BF)
        slope[rows, c : c + width] = dg.astype(BF)
        if k == 1:
            res = dot_t(act[rows, :], w[:, FF:]) + par[2:3, :] + h[rows, :].astype(F32)
            finish_forward(j, res, par, count, r, normed, stat, y)

    ahead([(r, k) for r in range(0, ROWS, TILE) for k in range(2)], first, second)


def start_backward(j, r, gy, par, normed, stat, gb, small):
    rows = pl.ds(r, TILE)
    unit = normed[rows, :].astype(F32)
    gres = norm_backward(gy, unit, stat[rows, LANE_RSTD + j : LANE_RSTD + j + 1], par)
    small[3:4, :] += colsum(gy * unit)
    small[4:5, :] += colsum(gy)
    low = gres.astype(BF)
    gb[rows, :] = low
    small[2:3, :] += colsum(low.astype(F32))
    return low


def feed_backward(j, gy_of, w, par, act, slope, stat, normed, gb, ig, small):
    small[...] = jnp.zeros(small.shape, F32)

    def first(r):
        low = start_backward(j, r, gy_of(r), par, normed, stat, gb, small)
        return [dot(low, w[:, FF + c : FF + c + 512]) for c in (0, 512)]

    def second(r, gas):
        rows = pl.ds(r, TILE)
        for k, ga in enumerate(gas):
            c = k * 512
            gp = (ga * slope[rows, c : c + 512].astype(F32)).astype(BF)
            slope[rows, c : c + 512] = gp
            small[k : k + 1, :] += colsum(gp.astype(F32))
        ig[rows, :] = (gb[rows, :].astype(F32) + dot_t(slope[rows, :], w[:, 0:FF])).astype(BF)

    ahead(list(range(0, ROWS, TILE)), first, second)


def flipped(flip, v):
    for r in (0, 512):
        flip[r : r + 512, :] = v[r : r + 512, :].T


def put_weights(dw, chunk, flip, v, c=0):
    z = dot(flip[0:512, :], v[0:512, c : c + 512]) + dot(flip[512:1024, :], v[512:1024, c : c + 512])
    z = z.astype(BF)
    c = chunk * 512
    for d in range(8):
        high = (d >> 2) * 64
        dw[d & 1, (d >> 1) & 1, high : high + 64, c : c + 512] = z[d * 64 : d * 64 + 64]


def feed_weights(h, act, gpre, gb, flip, dw, clear, done):
    flipped(flip, h)
    for k in range(2):
        clear(k)
        put_weights(dw, k, flip, gpre, k * 512)
        done(k)
    flipped(flip, gb)
    for k in range(2):
        clear(2 + k)
        put_weights(dw, 2 + k, flip, act, k * 512)
        done(2 + k)


def attend_backward(j, h, gy_of, w, par, qkv, probs, att, stat, normed, gb, gatt, gqkv, ig, small, dw, clear,
                    done, tick):
    lane = LANE_NORMAL + 2 * j
    small[...] = jnp.zeros(small.shape, F32)

    def first(r):
        low = start_backward(j, r, gy_of(r), par, normed, stat, gb, small)
        return dot_t(low, w[:, 3 * D : 4 * D])

    def second(r, ga):
        rows = pl.ds(r, TILE)
        a = att[rows, :].astype(F32)
        for hd in range(HEADS):
            c = hd * HEAD
            g = ga[:, c : c + HEAD] * stat[rows, lane + hd : lane + hd + 1]
            gatt[rows, c : c + HEAD] = g.astype(BF)
            stat[rows, LANE_INNER + hd : LANE_INNER + hd + 1] = jnp.sum(
                g * a[:, c : c + HEAD], axis=-1, keepdims=True
            )

    ahead(list(range(0, ROWS, TILE)), first, second)
    tick(3.0)
    flipped(normed, att)
    clear(3)
    put_weights(dw, 3, normed, gb)
    done(3)
    flipped(normed, h)
    gqkv[CTX:ROWS, D : 3 * D] = jnp.zeros((ROWS - CTX, 2 * D), BF)

    def values(hd, carry):
        lanes = pl.ds(pl.multiple_of(hd * HEAD, HEAD), HEAD)
        gv = t_dot(gatt[:, lanes], probs[hd])
        gqkv[0:CTX, pl.ds(pl.multiple_of(2 * D + hd * HEAD, HEAD), HEAD)] = gv.T.astype(BF)
        return carry

    lax.fori_loop(0, HEADS, values, 0)
    tick(1.0)
    clear(2)
    put_weights(dw, 2, normed, gqkv, 2 * D)
    done(2)
    step = 512

    def first(item):
        hd, r = item
        c = hd * HEAD
        return dot_t(gatt[r : r + step, c : c + HEAD], qkv[0:CTX, 2 * D + c : 2 * D + c + HEAD])

    def second(item, gp):
        hd, r = item
        c = hd * HEAD
        rows = pl.ds(r, step)
        inner = stat[rows, LANE_INNER + hd : LANE_INNER + hd + 1]
        gs = (probs[hd, rows, :].astype(F32) * (gp - inner)).astype(BF)
        probs[hd, rows, :] = gs
        gq = dot(gs, qkv[0:CTX, D + c : D + c + HEAD])
        gqkv[rows, c : c + HEAD] = (gq * (1.0 / math.sqrt(HEAD))).astype(BF)

    for pair in (0, 2):
        ahead([(hd, r) for hd in (pair, pair + 1) for r in range(0, ROWS, step)], first, second)
        tick(2.3)

    def keys(hd, carry):
        lanes = pl.ds(pl.multiple_of(hd * HEAD, HEAD), HEAD)
        gk = t_dot(qkv[:, lanes], probs[hd])
        gqkv[0:CTX, pl.ds(pl.multiple_of(D + hd * HEAD, HEAD), HEAD)] = (gk * (1.0 / LOG2E)).T.astype(BF)
        return carry

    lax.fori_loop(0, HEADS, keys, 0)
    tick(1.8)
    for r in range(0, ROWS, TILE):
        rows = pl.ds(r, TILE)
        ig[rows, :] = (gb[rows, :].astype(F32) + dot_t(gqkv[rows, :], w[:, 0 : 3 * D])).astype(BF)
        small[0:1, :] += colsum(gqkv[rows, 0:D].astype(F32))
        small[1:2, :] += colsum(gqkv[rows, 2 * D : 3 * D].astype(F32))


def attend_weights(gqkv, flip, dw, clear, done):
    for k in (1, 0):
        clear(k)
        put_weights(dw, k, flip, gqkv, k * D)
        done(k)


def vm(*shape, dtype=BF):
    return pltpu.VMEM(shape, dtype)


SCRATCH = dict(
    x=vm(ROWS, D),
    w=vm(SECTIONS, D, 4 * D),
    ys=vm(SECTIONS - 1, ROWS, D),
    igs=vm(SECTIONS, ROWS, D),
    norms=vm(SECTIONS, ROWS, D),
    qkvs=vm(2, ROWS, 3 * D),
    atts=vm(2, ROWS, D),
    ffs=vm(2, ROWS, 2 * FF),
    probs=vm(HEADS, ROWS, CTX),
    stat=vm(ROWS, 128, dtype=F32),
    gb=vm(ROWS, D),
    dw=vm(2, 2, 128, 4 * D),
    small=vm(SECTIONS, 8, D, dtype=F32),
    load_sem=pltpu.SemaphoreType.DMA((8,)),
    act_send=pltpu.SemaphoreType.DMA((SECTIONS,)),
    act_recv=pltpu.SemaphoreType.DMA((SECTIONS,)),
    ig_send=pltpu.SemaphoreType.DMA((SECTIONS,)),
    ig_recv=pltpu.SemaphoreType.DMA((SECTIONS,)),
)


def spread_scratch(size):
    sem = pltpu.SemaphoreType.DMA
    return dict(
        parts=vm(size, 8, D, dtype=F32),
        par=vm(SECTIONS, 8, D, dtype=F32),
        sum_plane=vm(SECTIONS, 8, D, dtype=F32),
        sum_dp=vm(size, 8, D, dtype=F32),
        land_a=vm(SECTIONS, 4, 2, 2 * (D // size), 512),
        land_b=vm(2, 4, 2 * (D // size), 512),
        land_c=vm(2, 4, D // size, 512),
        land_d=vm(SECTIONS, 4, D // size, 512),
        last=vm(D // size, 4 * D, dtype=F32),
        w_recv=sem((SECTIONS, 2, size)),
        w_send=sem((160,)),
        parts_recv=sem((size,)),
        par_recv=sem((SECTIONS,)),
        a_recv=sem((SECTIONS, 4)),
        b_recv=sem((SECTIONS, 4)),
        c_recv=sem((SECTIONS, 4)),
        d_recv=sem((SECTIONS, 4)),
        sp_recv=sem((SECTIONS,)),
        sd_recv=sem((size,)),
        dw_send=sem((128,)),
    )


class Names:
    def __init__(self, names, refs):
        self.__dict__.update(zip(names, refs, strict=True))


INPUTS = ("inputs", "cot", "counts", "weight")
OUTPUTS = ("acts", "grads", "dweight", "dsmall", "kept")


class Sends:
    def __init__(self, sems):
        self.sems, self.used, self.started = sems, 0, {}

    def push(self, group, src, dst, recv_sem, target, when=None):
        k = self.used
        self.used += 1
        assert k < self.sems.shape[0]

        def copy():
            return pltpu.make_async_remote_copy(
                src_ref=src,
                dst_ref=dst,
                send_sem=self.sems.at[k],
                recv_sem=recv_sem,
                device_id=target,
                device_id_type=MESH,
            )

        self.started.setdefault(group, []).append((when, copy))
        guarded(when, lambda: copy().start())

    def drain(self, group):
        for when, copy in self.started.pop(group, ()):
            guarded(when, lambda copy=copy: copy().wait_send())


def guarded(when, action):
    if when is None:
        action()
    else:
        pl.when(when)(action)


def landed(dst, sem):
    pltpu.make_async_copy(dst, dst, sem).wait()


class Spread:
    def __init__(self, o, me, dp, size):
        self.o, self.me, self.dp, self.size = o, me, dp, size
        self.block = D // size
        self.sends = Sends(o.w_send)
        self.outs = Sends(o.dw_send)
        self.own = (dp, dp ^ 2, dp ^ 4, dp ^ 6)
        self.now, self.free, self.state = 0.0, {}, {}


    def shard(self, j, d, part):
        rows = pl.ds(pl.multiple_of(d * self.block, self.block), self.block)
        return self.o.w.at[j, rows, pl.ds(part * 2 * D, 2 * D)]

    def send_shard(self, j, d, part, section, dp, when=None):
        ref = self.shard(j, d, part)
        self.sends.push("w", ref, ref, self.o.w_recv.at[j, part, d], (section, dp), when)

    def wait_shard(self, j, d, part):
        landed(self.shard(j, d, part), self.o.w_recv.at[j, part, d])

    def begin(self):
        o, me, dp = self.o, self.me, self.dp
        rows = pl.ds(pl.multiple_of(dp * self.block, self.block), self.block)
        load = pltpu.make_async_copy(o.weight.at[0], o.w.at[me, rows, :], o.load_sem.at[1])
        load.start()
        width = o.bias_in.shape[1]
        bias = jnp.concatenate([o.bias_in[...].astype(F32), jnp.zeros((1, 3 * D - width), F32)], axis=1)
        bias = pltpu.roll(jnp.broadcast_to(bias, (8, 3 * D)), dp * width, 1)
        width = o.norm_in.shape[2]
        norm = jnp.concatenate([o.norm_in[0].astype(F32), jnp.zeros((2, D - width), F32)], axis=1)
        norm = pltpu.roll(jnp.concatenate([norm, jnp.zeros((6, D), F32)], axis=0), dp * width, 1)
        for k in range(3):
            o.parts[dp, k : k + 1, :] = bias[0:1, k * D : k * D + D]
        o.parts[dp, 3:5, :] = norm[0:2]
        o.parts[dp, 5:8, :] = jnp.zeros((3, D), F32)
        load.wait()

    def spread_own(self, d, part):
        me, dp = self.me, self.dp
        self.send_shard(me, d, part, me ^ 1, dp)
        self.send_shard(me, d, part, me ^ 2, dp)
        self.send_shard(me, d, part, me, dp ^ 1)

    def pass_on(self, r, d):
        me, dp = self.me, self.dp
        for part in range(2):
            self.wait_shard(me ^ r, d, part)
            self.send_shard(me ^ r, d, part, me ^ (3 - r), dp)
            self.send_shard(me ^ r, d, part, me, dp ^ 1)

    def first(self):
        o, me, dp = self.o, self.me, self.dp
        d0, d1, d2, d3 = self.own
        for part in range(2):
            self.send_shard(me, d0, part, me, d2)
            self.send_shard(me, d0, part, me, d1)
            self.spread_own(d0, part)
        for k in range(1, self.size):
            self.sends.push("w", o.parts.at[dp], o.parts.at[dp], o.parts_recv.at[dp], (me, dp ^ k))
        for part in range(2):
            self.wait_shard(me, d1, part)
            self.spread_own(d1, part)
        for part in range(2):
            self.wait_shard(me, d2, part)
            self.send_shard(me, d2, part, me, d1)
            self.spread_own(d2, part)
        self.pass_on(1, d0)
        for k in range(1, self.size):
            landed(o.parts.at[dp ^ k], o.parts_recv.at[dp ^ k])
        o.par[me, :, :] = jnp.sum(o.parts[...], axis=0)
        for r in range(1, SECTIONS):
            self.sends.push("w", o.par.at[me], o.par.at[me], o.par_recv.at[me], (me ^ r, dp))
        self.pass_on(2, d1)
        for part in range(2):
            self.wait_shard(me, d3, part)
            self.spread_own(d3, part)
        self.pass_on(1, d2)
        self.pass_on(2, d3)
        self.todo = {1: [d1, d3], 2: [d0, d2], 3: [d0, d1, d2, d3]}
        for r in range(1, SECTIONS):
            landed(o.par.at[me ^ r], o.par_recv.at[me ^ r])
        self.settle(0)

    def settle(self, j):
        me, dp = self.me, self.dp
        pieces = [(d, part) for d in self.own for part in range(2)]
        for r, shards_left in self.todo.items():
            left = [(d, part) for d, part in pieces if any(d is e for e in shards_left)]

            @pl.when(me ^ r == j)
            def _(left=left):
                for d, part in left:
                    self.wait_shard(j, d, part)

            for d, part in left:
                self.send_shard(j, d, part, me, dp ^ 1, me ^ r == j)
        for d, part in pieces:
            self.wait_shard(j, d ^ 1, part)


    def expected(self, link, cost):
        self.free[link] = max(self.free.get(link, 0.0), self.now) + cost
        return self.free[link] + 2.0

    def done(self, j, q):
        o, me, dp = self.o, self.me, self.dp
        self.passed(0.65)
        part = o.dw.at[1 - (dp & 1), :, :, pl.ds(q * 512, 512)]
        self.outs.push((j, q), part, o.land_a.at[j, q], o.a_recv.at[j, q], (me, dp ^ 1))
        self.state[j, q] = ("b", self.expected("core", 0.6))

    def passed(self, us):
        self.now += us
        for unit in sorted(self.state, key=lambda u: (-u[0], u)):
            while self.state[unit][0] != "end" and self.state[unit][1] <= self.now and self.allowed(unit):
                self.step(unit)

    def allowed(self, unit):
        stage = self.state[unit][0]
        if unit[0] >= 2 or stage == "d":
            return True
        return self.state[2, 3][0] > ("c" if stage == "b" else "d")

    def landing(self, unit):
        o = self.o
        j, q = unit
        if j >= 2:
            return o.land_b.at[j - 2, q], o.land_c.at[j - 2, q]
        columns = pl.ds(q * 512, 512)
        return o.w.at[3, pl.ds(128 * j, 128), columns], o.w.at[3, pl.ds(256 + 64 * j, 64), columns]

    def step(self, unit):
        o, me, dp = self.o, self.me, self.dp
        j, q = unit
        core, zlow, zhigh = dp & 1, (dp >> 1) & 1, dp >> 2
        stage = self.state[unit][0]
        half, (land_b, land_c) = o.land_a.at[j, q], self.landing(unit)
        if stage == "b":
            landed(half, o.a_recv.at[j, q])
            mine = o.dw[core, :, :, q * 512 : q * 512 + 512]
            half[...] = (half[...].astype(F32) + mine.astype(F32)).astype(BF)
            self.outs.drain(unit)
            self.outs.push("z", half.at[1 - zlow], land_b, o.b_recv.at[j, q], (me, dp ^ 2))
            self.state[unit] = ("c", self.expected("near", 2.9))
        elif stage == "c":
            landed(land_b, o.b_recv.at[j, q])
            mine = half.at[zlow]
            mine[...] = (mine[...].astype(F32) + land_b[...].astype(F32)).astype(BF)
            there = pl.ds(pl.multiple_of((1 - zhigh) * 64, 64), 64)
            self.outs.push("z", mine.at[there], land_c, o.c_recv.at[j, q], (me, dp ^ 4))
            self.state[unit] = ("d", self.expected("far", 2.9))
        else:
            landed(land_c, o.c_recv.at[j, q])
            here = pl.ds(pl.multiple_of(zhigh * 64, 64), 64)
            total = half[zlow, here, :].astype(F32) + land_c[...].astype(F32)
            mine = o.norms.at[SECTIONS - 1, pl.ds((4 * j + q) * self.block, self.block)]
            mine[...] = total.astype(BF)
            self.outs.push("d", mine, o.land_d.at[me, q], o.d_recv.at[me, q], (j, dp), me != j)

            @pl.when(me == j)
            def _():
                o.last[:, q * 512 : q * 512 + 512] = total

            self.state[unit] = ("end", 0)

    def smalls(self, j):
        o, me, dp = self.o, self.me, self.dp
        self.outs.push("s", o.small.at[j], o.sum_plane.at[me], o.sp_recv.at[me], (j, dp), me != j)

        @pl.when(me == j)
        def _():
            o.sum_plane[me, :, :] = o.small[j, :, :]

    def reuse(self, j, q):
        if self.state[j, q][0] == "b":
            if not self.allowed((j, q)):
                self.force((2, 3), "c")
            self.step((j, q))

    def force(self, unit, stage):
        while self.state[unit][0] <= stage:
            self.step(unit)

    def release(self):
        self.sends.drain("w")

    def finish(self):
        o, me, dp = self.o, self.me, self.dp
        while any(stage != "end" for stage, _ in self.state.values()):
            self.passed(0.5)
        for r in range(1, SECTIONS):
            landed(o.sum_plane.at[me ^ r], o.sp_recv.at[me ^ r])
        o.sum_dp[dp, :, :] = jnp.sum(o.sum_plane[...], axis=0)
        for k in range(1, self.size):
            self.outs.push("s", o.sum_dp.at[dp], o.sum_dp.at[dp], o.sd_recv.at[dp], (me, dp ^ k))
        for r in range(1, SECTIONS):
            for q in range(4):
                landed(o.land_d.at[me ^ r, q], o.d_recv.at[me ^ r, q])
                o.last[:, q * 512 : q * 512 + 512] += o.land_d[me ^ r, q].astype(F32)
        out = pltpu.make_async_copy(o.last, o.dweight.at[0], o.load_sem.at[2])
        out.start()
        for k in range(1, self.size):
            landed(o.sum_dp.at[dp ^ k], o.sd_recv.at[dp ^ k])
        o.dsmall[...] = jnp.sum(o.sum_dp[...], axis=0)
        out.wait()
        for group in list(self.outs.started):
            self.outs.drain(group)


class Local:
    def __init__(self, o):
        self.o = o
        self.loads = [pltpu.make_async_copy(o.weight.at[j], o.w.at[j], o.load_sem.at[1 + j]) for j in range(SECTIONS)]
        self.stores, self.counted = {}, {}

    def begin(self):
        for load in self.loads:
            load.start()

    def first(self):
        self.loads[0].wait()

    def settle(self, j):
        self.loads[j].wait()

    def done(self, j, q):
        if j not in self.counted:
            self.counted[j] = 0
        self.counted[j] += 1
        if self.counted[j] == 4:
            copy = pltpu.make_async_copy(self.o.dw, self.o.dweight.at[j], self.o.load_sem.at[1 + j])
            copy.start()
            self.stores[j] = copy

    def passed(self, us):
        pass

    def smalls(self, j):
        pass

    def release(self):
        pass

    def reuse(self, j, q):
        if j in self.stores:
            self.stores.pop(j).wait()

    def finish(self):
        for copy in self.stores.values():
            copy.wait()
        self.o.dsmall[...] = self.o.small[...]


def kernel(size, spread, *refs):
    names = INPUTS + (("bias_in", "norm_in") if spread else ("par",)) + OUTPUTS + tuple(SCRATCH)
    if spread:
        names += tuple(spread_scratch(size))
    o = Names(names, refs)
    me = lax.axis_index("section")
    dp = lax.axis_index("dp")

    barrier = pltpu.get_barrier_semaphore()
    peers = [(me ^ r, dp) for r in range(1, SECTIONS)]
    if spread:
        peers += [(me, dp ^ k) for k in range(1, size)]
    for peer in peers:
        pl.semaphore_signal(barrier, inc=1, device_id=peer, device_id_type=MESH)

    net = Spread(o, me, dp, size) if spread else Local(o)
    count = o.counts[me]
    load_x = pltpu.make_async_copy(o.inputs.at[me], o.x, o.load_sem.at[0])
    load_cot = pltpu.make_async_copy(o.cot.at[me], o.igs.at[1], o.load_sem.at[5])
    ys = [o.ys.at[0], o.ys.at[1], o.ys.at[2], o.igs.at[0]]
    igs = [o.norms.at[1], o.igs.at[1], o.igs.at[2], o.igs.at[3]]
    dw = o.dw
    load_x.start()
    load_cot.start()
    net.begin()
    pl.semaphore_wait(barrier, len(peers))

    def deliver(block, out, j, send, recv, action):
        @pl.when(me == j)
        def _():
            if action == "start":
                pltpu.make_async_copy(block, out.at[j], recv.at[j]).start()

        @pl.when(me != j)
        def _():
            copy = pltpu.make_async_remote_copy(
                src_ref=block,
                dst_ref=out.at[me],
                send_sem=send.at[j],
                recv_sem=recv.at[me],
                device_id=(j, dp),
                device_id_type=MESH,
            )
            copy.start() if action == "start" else copy.wait_send()

    keep = pltpu.make_async_copy(o.probs, o.kept, o.load_sem.at[6])
    bring = pltpu.make_async_copy(o.kept, o.probs, o.load_sem.at[7])

    load_x.wait()
    net.first()
    for j in range(SECTIONS):
        layer = j // 2
        h = o.x if j == 0 else ys[j - 1]
        w, par, y, normed = o.w.at[j], o.par.at[j], ys[j], o.norms.at[j]
        if j > 0:
            net.settle(j)
        if j % 2 == 0:
            if j == 2:
                keep.wait()

            def between(step):
                pass

            attend_forward(
                j, h, w, par, count, o.qkvs.at[layer], o.probs, o.atts.at[layer], o.stat, normed, y, between
            )
            if j == 0:
                keep.start()
        else:
            f = o.ffs.at[layer]
            feed_forward(j, h, w, par, count, f.at[:, :FF], f.at[:, FF:], o.stat, normed, y)
        deliver(y, o.acts, j, o.act_send, o.act_recv, "start")

    load_cot.wait()
    for j in reversed(range(SECTIONS)):
        layer = j // 2
        h = o.x if j == 0 else ys[j - 1]
        w, par, normed = o.w.at[j], o.par.at[j], o.norms.at[j]
        ig, small = igs[j], o.small.at[j]

        def gy_of(r, j=j):
            rows = pl.ds(r, TILE)
            if j == SECTIONS - 1:
                return o.igs[1, rows, :].astype(F32) * live_rows(count, r, TILE)
            return o.igs[j + 1, rows, :].astype(F32)

        f = o.ffs.at[layer]

        def done(q, j=j):
            net.done(j, q)

        def clear(q, j=j):
            if j + 1 < SECTIONS:
                net.reuse(j + 1, q)

        if j == 2:
            net.release()
        if j % 2 == 0:
            if j == 0:
                bring.wait()
            pool = o.ffs.at[1]
            gqkv, gatt = pool.at[:, : 3 * D], pool.at[:, 3 * D :]
            attend_backward(
                j, h, gy_of, w, par, o.qkvs.at[layer], o.probs, o.atts.at[layer], o.stat, normed, o.gb, gatt, gqkv,
                ig, small, dw, clear, done, net.passed,
            )
            if j == 2:
                bring.start()
        else:
            feed_backward(j, gy_of, w, par, f.at[:, :FF], f.at[:, FF:], o.stat, normed, o.gb, ig, small)
        deliver(ig, o.grads, j, o.ig_send, o.ig_recv, "start")
        net.smalls(j)
        net.passed(2.0 if j % 2 == 0 else 3.8)
        if j % 2 == 0:
            attend_weights(gqkv, normed, dw, clear, done)
        else:
            feed_weights(h, f.at[:, :FF], f.at[:, FF:], o.gb, normed, dw, clear, done)

    net.finish()
    for j in range(SECTIONS):
        deliver(ys[j], o.acts, j, o.act_send, o.act_recv, "sent")
        deliver(igs[j], o.grads, j, o.ig_send, o.ig_recv, "sent")
    for n in range(SECTIONS):
        landed(o.acts.at[n], o.act_recv.at[n])
        landed(o.grads.at[n], o.ig_recv.at[n])


def finish_kernel(acts, grads, dweight, dsmall, acts_out, grads_out, dweight_out, db, dn, rows, last, sems):
    moves = []
    for n in range(SECTIONS):
        moves.append((acts.at[n], rows.at[2 * n], acts_out.at[0, n]))
        moves.append((grads.at[n], rows.at[2 * n + 1], grads_out.at[0, n]))
    moves.append((dweight, last, dweight_out))
    ins = [pltpu.make_async_copy(src, mid, sems.at[0, k]) for k, (src, mid, _) in enumerate(moves)]
    copies = [pltpu.make_async_copy(mid, dst, sems.at[1, k]) for k, (_, mid, dst) in enumerate(moves)]
    for copy in ins:
        copy.start()
    for k, copy in enumerate(ins):
        copy.wait()
        copies[k].start()
    dp = lax.axis_index("dp")
    width = db.shape[1]
    bias = jnp.concatenate([dsmall[k : k + 1, :] for k in range(3)], axis=1)
    bias = pltpu.roll(jnp.broadcast_to(bias, (8, 3 * D)), 3 * D - dp * width, 1)
    db[...] = bias[0:1, 0:width]
    width = dn.shape[2]
    norm = pltpu.roll(dsmall[...], D - dp * width, 1)
    dn[0, :, :] = norm[3:5, 0:width]
    for copy in copies:
        copy.wait()


def shards(inputs, cotangent, query_counts, section_weight, section_bias, section_norm):
    size = lax.axis_size("dp")
    block = section_weight.shape[1]
    spread = size == 8
    anywhere = pl.BlockSpec(memory_space=pl.ANY)
    whole = pl.BlockSpec(memory_space=pltpu.VMEM)

    if spread:
        weight = section_weight
        small = [section_bias, section_norm]
        grad_shapes = [((1, block, 4 * D), F32), ((8, D), F32)]
    else:

        def gathered(v, axis):
            v = lax.all_gather(v, "dp", axis=axis, tiled=True)
            return lax.all_gather(v, "section", axis=0, tiled=True)

        weight = gathered(section_weight, 1)
        bias = gathered(section_bias, 1)
        norm = gathered(section_norm, 2)
        par = jnp.concatenate([bias.reshape(SECTIONS, 3, D), norm, jnp.zeros((SECTIONS, 3, D), BF)], axis=1).astype(F32)
        small = [par]
        grad_shapes = [((SECTIONS, 2, 2, 128, 4 * D), BF), ((SECTIONS, 8, D), F32)]

    out_shapes = [((SECTIONS, ROWS, D), BF)] * 2 + grad_shapes + [((HEADS, ROWS, CTX), BF)]
    scratch = list(SCRATCH.values())
    if spread:
        scratch += list(spread_scratch(size).values())
    results = pl.pallas_call(
        functools.partial(kernel, size, spread),
        out_shape=[jax.ShapeDtypeStruct(*s) for s in out_shapes],
        in_specs=[anywhere, anywhere, pl.BlockSpec(memory_space=pltpu.SMEM), anywhere] + [whole] * len(small),
        out_specs=[anywhere, anywhere, anywhere, whole, anywhere],
        scratch_shapes=scratch,
        compiler_params=pltpu.CompilerParams(
            collective_id=0, has_side_effects=True, vmem_limit_bytes=63 * MIB
        ),
    )(inputs, cotangent, query_counts, weight, *small)
    acts, grads, dweight, dsmall = results[:4]

    if spread:
        return pl.pallas_call(
            finish_kernel,
            out_shape=[
                jax.ShapeDtypeStruct((1,) + acts.shape, BF),
                jax.ShapeDtypeStruct((1,) + grads.shape, BF),
                jax.ShapeDtypeStruct(dweight.shape, F32),
                jax.ShapeDtypeStruct(section_bias.shape, F32),
                jax.ShapeDtypeStruct(section_norm.shape, F32),
            ],
            in_specs=[anywhere, anywhere, anywhere, whole],
            out_specs=[anywhere, anywhere, anywhere, whole, whole],
            scratch_shapes=[
                vm(2 * SECTIONS, ROWS, D),
                vm(*dweight.shape, dtype=F32),
                pltpu.SemaphoreType.DMA((2, 2 * SECTIONS + 1)),
            ],
            compiler_params=pltpu.CompilerParams(vmem_limit_bytes=62 * MIB),
        )(acts, grads, dweight, dsmall)

    def scattered(v, axis):
        v = lax.psum_scatter(v, "dp", scatter_dimension=axis, tiled=True)
        return lax.psum_scatter(v, "section", scatter_dimension=0, tiled=True)

    dweight = dweight.reshape(SECTIONS, 2, 2, 2, 64, 4 * D).transpose(0, 3, 2, 1, 4, 5)
    dw = scattered(dweight.reshape(SECTIONS, D, 4 * D), 1).astype(F32)
    db = scattered(dsmall[:, :3].reshape(SECTIONS, 3 * D), 1)
    dn = scattered(dsmall[:, 3:5], 2)
    return acts[None], grads[None], dw, db, dn


def solution(mesh):
    return jax.shard_map(
        shards,
        mesh=mesh,
        in_specs=(
            P("dp", None, None),
            P("dp", None, None),
            P("dp"),
            P("section", "dp", None),
            P("section", "dp"),
            P("section", None, "dp"),
        ),
        out_specs=(
            P("section", "dp", None, None),
            P("section", "dp", None, None),
            P("section", "dp", None),
            P("section", "dp"),
            P("section", None, "dp"),
        ),
        check_vma=False,
    )
```

```python
import functools
import math

import jax
import jax.numpy as jnp
from jax import lax
from jax.experimental import pallas as pl
from jax.experimental.pallas import tpu as pltpu
from jax.sharding import PartitionSpec as P

D = 512
HEADS = 4
HEAD = 128
FF = 1024
CTX = 896
ROWS = 1024
SECTIONS = 4
PIECE = 1024
TILE = 256
F32 = jnp.float32
BF = jnp.bfloat16
LOG2E = math.log2(math.e)
MESH = pl.DeviceIdType.MESH
MIB = 1 << 20


def dot(a, b):
    return lax.dot_general(a, b, (((1,), (0,)), ((), ())), preferred_element_type=F32)


def dot_t(a, b):
    return lax.dot_general(a, b, (((1,), (1,)), ((), ())), preferred_element_type=F32)


def t_dot(a, b):
    return lax.dot_general(a, b, (((0,), (0,)), ((), ())), preferred_element_type=F32)


def colsum(x):
    return jnp.sum(x, axis=0, keepdims=True)


def rows_loop(total, step, body):
    def one(i, carry):
        body(pl.multiple_of(i * step, step))
        return carry

    lax.fori_loop(0, total // step, one, 0)


LANE_RSTD = 0
LANE_NORMAL = 8
LANE_INNER = 16


def norm_forward(res, par):
    mean = jnp.mean(res, axis=-1, keepdims=True)
    center = res - mean
    inverse = lax.rsqrt(jnp.mean(center * center, axis=-1, keepdims=True) + 1e-5)
    normed = center * inverse
    return normed * par[3:4, :] + par[4:5, :], normed, inverse


def norm_backward(gy, normed, inverse, par):
    u = gy * par[3:4, :]
    m1 = jnp.mean(u, axis=-1, keepdims=True)
    m2 = jnp.mean(u * normed, axis=-1, keepdims=True)
    return inverse * (u - m1 - normed * m2)


def live_rows(count, begin, n):
    ids = lax.broadcasted_iota(jnp.int32, (n, 1), 0) + begin
    return jnp.where(ids < CTX + count, 1.0, 0.0).astype(F32)


def gelu_parts(z):
    t = 1.0 / (1.0 + (0.3275911 / math.sqrt(2.0)) * jnp.abs(z))
    e = jnp.exp2(z * z * (-0.5 * LOG2E))
    a = [0.254829592, -0.284496736, 1.421413741, -1.453152027, 1.061405429]
    a = [0.5 * v for v in a]
    tail = t * (a[0] + t * (a[1] + t * (a[2] + t * (a[3] + t * a[4])))) * e
    phi = jnp.where(z >= 0, 1.0 - tail, tail)
    return z * phi, phi + z * e * (1.0 / math.sqrt(2 * math.pi))


def ahead(items, first, second):
    ready = first(items[0])
    for i, item in enumerate(items):
        now = ready
        if i + 1 < len(items):
            ready = first(items[i + 1])
        second(item, now)


def finish_forward(j, res, par, count, begin, normed, stat, y):
    rows = pl.ds(begin, res.shape[0])
    out, unit, inverse = norm_forward(res, par)
    out = out * live_rows(count, begin, res.shape[0])
    y[rows, :] = out.astype(BF)
    normed[rows, :] = unit.astype(BF)
    stat[rows, LANE_RSTD + j : LANE_RSTD + j + 1] = inverse


def attend_forward(j, h, w, par, count, qkv, probs, att, stat, normed, y, between):
    factor = LOG2E / math.sqrt(HEAD)
    lane = LANE_NORMAL + 2 * j
    x = h[...]
    for c in range(0, 3 * D, 256):
        z = dot(x, w[:, c : c + 256])
        if c < D:
            z = (z + par[0:1, c : c + 256]) * factor
        elif c >= 2 * D:
            z = z + par[1:2, c - 2 * D : c - 2 * D + 256]
        qkv[:, c : c + 256] = z.astype(BF)
    between(0)
    step = 512

    def score(item):
        r, hd = item
        c = hd * HEAD
        return dot_t(qkv[pl.ds(r, step), c : c + HEAD], qkv[0:CTX, D + c : D + c + HEAD])

    def attend(item, s):
        r, hd = item
        c = hd * HEAD
        rows = pl.ds(r, step)
        e = jnp.exp2(s - jnp.max(s, axis=-1, keepdims=True))
        normal = 1.0 / jnp.sum(e, axis=-1, keepdims=True)
        low = e.astype(BF)
        probs[hd, rows, :] = low
        stat[rows, lane + hd : lane + hd + 1] = normal
        o = dot(low, qkv[0:CTX, 2 * D + c : 2 * D + c + HEAD])
        att[rows, c : c + HEAD] = (o * normal).astype(BF)
        if hd == HEADS - 1:
            for t in range(0, step, TILE):
                q = r + t
                out = pl.ds(q, TILE)
                res = dot(att[out, :], w[:, 3 * D : 4 * D]) + par[2:3, :] + h[out, :].astype(F32)
                finish_forward(j, res, par, count, q, normed, stat, y)

    ahead([(r, hd) for r in range(0, ROWS, step) for hd in range(HEADS)], score, attend)
    between(1)


def feed_forward(j, h, w, par, count, act, slope, stat, normed, y):
    width = 512

    def first(item):
        r, k = item
        return dot(h[r : r + TILE, :], w[:, k * width : (k + 1) * width])

    def second(item, z):
        r, k = item
        rows = pl.ds(r, TILE)
        c = k * width
        g, dg = gelu_parts(z + par[k : k + 1, :])
        act[rows, c : c + width] = g.astype(BF)
        slope[rows, c : c + width] = dg.astype(BF)
        if k == 1:
            res = dot_t(act[rows, :], w[:, FF:]) + par[2:3, :] + h[rows, :].astype(F32)
            finish_forward(j, res, par, count, r, normed, stat, y)

    ahead([(r, k) for r in range(0, ROWS, TILE) for k in range(2)], first, second)


def start_backward(j, r, gy, par, normed, stat, gb, small):
    rows = pl.ds(r, TILE)
    unit = normed[rows, :].astype(F32)
    gres = norm_backward(gy, unit, stat[rows, LANE_RSTD + j : LANE_RSTD + j + 1], par)
    small[3:4, :] += colsum(gy * unit)
    small[4:5, :] += colsum(gy)
    low = gres.astype(BF)
    gb[rows, :] = low
    small[2:3, :] += colsum(low.astype(F32))
    return low


def feed_backward(j, gy_of, w, par, act, slope, stat, normed, gb, ig, small):
    small[...] = jnp.zeros(small.shape, F32)

    def first(r):
        low = start_backward(j, r, gy_of(r), par, normed, stat, gb, small)
        return [dot(low, w[:, FF + c : FF + c + 512]) for c in (0, 512)]

    def second(r, gas):
        rows = pl.ds(r, TILE)
        for k, ga in enumerate(gas):
            c = k * 512
            gp = (ga * slope[rows, c : c + 512].astype(F32)).astype(BF)
            slope[rows, c : c + 512] = gp
            small[k : k + 1, :] += colsum(gp.astype(F32))
        ig[rows, :] = (gb[rows, :].astype(F32) + dot_t(slope[rows, :], w[:, 0:FF])).astype(BF)

    ahead(list(range(0, ROWS, TILE)), first, second)


def flipped(flip, v):
    for r in (0, 512):
        flip[r : r + 512, :] = v[r : r + 512, :].T


def put_weights(dw, chunk, flip, v, c=0):
    z = dot(flip[0:512, :], v[0:512, c : c + 512]) + dot(flip[512:1024, :], v[512:1024, c : c + 512])
    z = z.astype(BF)
    c = chunk * 512
    for d in range(8):
        high = (d >> 2) * 64
        dw[d & 1, (d >> 1) & 1, high : high + 64, c : c + 512] = z[d * 64 : d * 64 + 64]


def feed_weights(h, act, gpre, gb, flip, dw, clear, done):
    flipped(flip, h)
    for k in range(2):
        clear(k)
        put_weights(dw, k, flip, gpre, k * 512)
        done(k)
    flipped(flip, gb)
    for k in range(2):
        clear(2 + k)
        put_weights(dw, 2 + k, flip, act, k * 512)
        done(2 + k)


def attend_backward(j, h, gy_of, w, par, qkv, probs, att, stat, normed, gb, gatt, gqkv, ig, small, dw, clear,
                    done, tick):
    lane = LANE_NORMAL + 2 * j
    small[...] = jnp.zeros(small.shape, F32)

    def first(r):
        low = start_backward(j, r, gy_of(r), par, normed, stat, gb, small)
        return dot_t(low, w[:, 3 * D : 4 * D])

    def second(r, ga):
        rows = pl.ds(r, TILE)
        a = att[rows, :].astype(F32)
        for hd in range(HEADS):
            c = hd * HEAD
            g = ga[:, c : c + HEAD] * stat[rows, lane + hd : lane + hd + 1]
            gatt[rows, c : c + HEAD] = g.astype(BF)
            stat[rows, LANE_INNER + hd : LANE_INNER + hd + 1] = jnp.sum(
                g * a[:, c : c + HEAD], axis=-1, keepdims=True
            )

    ahead(list(range(0, ROWS, TILE)), first, second)
    tick(3.0)
    flipped(normed, att)
    clear(3)
    put_weights(dw, 3, normed, gb)
    done(3)
    flipped(normed, h)
    gqkv[CTX:ROWS, D : 3 * D] = jnp.zeros((ROWS - CTX, 2 * D), BF)

    def values(hd, carry):
        lanes = pl.ds(pl.multiple_of(hd * HEAD, HEAD), HEAD)
        gv = t_dot(gatt[:, lanes], probs[hd])
        gqkv[0:CTX, pl.ds(pl.multiple_of(2 * D + hd * HEAD, HEAD), HEAD)] = gv.T.astype(BF)
        return carry

    lax.fori_loop(0, HEADS, values, 0)
    tick(1.0)
    clear(2)
    put_weights(dw, 2, normed, gqkv, 2 * D)
    done(2)
    step = 512

    def first(item):
        hd, r = item
        c = hd * HEAD
        return dot_t(gatt[r : r + step, c : c + HEAD], qkv[0:CTX, 2 * D + c : 2 * D + c + HEAD])

    def second(item, gp):
        hd, r = item
        c = hd * HEAD
        rows = pl.ds(r, step)
        inner = stat[rows, LANE_INNER + hd : LANE_INNER + hd + 1]
        gs = (probs[hd, rows, :].astype(F32) * (gp - inner)).astype(BF)
        probs[hd, rows, :] = gs
        gq = dot(gs, qkv[0:CTX, D + c : D + c + HEAD])
        gqkv[rows, c : c + HEAD] = (gq * (1.0 / math.sqrt(HEAD))).astype(BF)

    for pair in (0, 2):
        ahead([(hd, r) for hd in (pair, pair + 1) for r in range(0, ROWS, step)], first, second)
        tick(2.3)

    def keys(hd, carry):
        lanes = pl.ds(pl.multiple_of(hd * HEAD, HEAD), HEAD)
        gk = t_dot(qkv[:, lanes], probs[hd])
        gqkv[0:CTX, pl.ds(pl.multiple_of(D + hd * HEAD, HEAD), HEAD)] = (gk * (1.0 / LOG2E)).T.astype(BF)
        return carry

    lax.fori_loop(0, HEADS, keys, 0)
    tick(1.8)
    for r in range(0, ROWS, TILE):
        rows = pl.ds(r, TILE)
        ig[rows, :] = (gb[rows, :].astype(F32) + dot_t(gqkv[rows, :], w[:, 0 : 3 * D])).astype(BF)
        small[0:1, :] += colsum(gqkv[rows, 0:D].astype(F32))
        small[1:2, :] += colsum(gqkv[rows, 2 * D : 3 * D].astype(F32))


def attend_weights(gqkv, flip, dw, clear, done):
    for k in (1, 0):
        clear(k)
        put_weights(dw, k, flip, gqkv, k * D)
        done(k)


def vm(*shape, dtype=BF):
    return pltpu.VMEM(shape, dtype)


SCRATCH = dict(
    x=vm(ROWS, D),
    w=vm(SECTIONS, D, 4 * D),
    ys=vm(SECTIONS - 1, ROWS, D),
    igs=vm(SECTIONS, ROWS, D),
    norms=vm(SECTIONS, ROWS, D),
    qkvs=vm(2, ROWS, 3 * D),
    atts=vm(2, ROWS, D),
    ffs=vm(2, ROWS, 2 * FF),
    probs=vm(HEADS, ROWS, CTX),
    stat=vm(ROWS, 128, dtype=F32),
    gb=vm(ROWS, D),
    dw=vm(2, 2, 128, 4 * D),
    small=vm(SECTIONS, 8, D, dtype=F32),
    load_sem=pltpu.SemaphoreType.DMA((8,)),
    act_send=pltpu.SemaphoreType.DMA((SECTIONS,)),
    act_recv=pltpu.SemaphoreType.DMA((SECTIONS,)),
    ig_send=pltpu.SemaphoreType.DMA((SECTIONS,)),
    ig_recv=pltpu.SemaphoreType.DMA((SECTIONS,)),
)


def spread_scratch(size):
    sem = pltpu.SemaphoreType.DMA
    return dict(
        parts=vm(size, 8, D, dtype=F32),
        par=vm(SECTIONS, 8, D, dtype=F32),
        sum_plane=vm(SECTIONS, 8, D, dtype=F32),
        sum_dp=vm(size, 8, D, dtype=F32),
        land_a=vm(SECTIONS, 4, 2, 2 * (D // size), 512),
        land_b=vm(2, 4, 2 * (D // size), 512),
        land_c=vm(2, 4, D // size, 512),
        land_d=vm(SECTIONS, 4, D // size, 512),
        last=vm(D // size, 4 * D, dtype=F32),
        w_recv=sem((SECTIONS, 2, size)),
        w_send=sem((160,)),
        parts_recv=sem((size,)),
        par_recv=sem((SECTIONS,)),
        a_recv=sem((SECTIONS, 4)),
        b_recv=sem((SECTIONS, 4)),
        c_recv=sem((SECTIONS, 4)),
        d_recv=sem((SECTIONS, 4)),
        sp_recv=sem((SECTIONS,)),
        sd_recv=sem((size,)),
        dw_send=sem((128,)),
    )


class Names:
    def __init__(self, names, refs):
        self.__dict__.update(zip(names, refs, strict=True))


INPUTS = ("inputs", "cot", "counts", "weight")
OUTPUTS = ("acts", "grads", "dweight", "dsmall", "kept")


class Sends:
    def __init__(self, sems):
        self.sems, self.used, self.started = sems, 0, {}

    def push(self, group, src, dst, recv_sem, target, when=None):
        k = self.used
        self.used += 1
        assert k < self.sems.shape[0]

        def copy():
            return pltpu.make_async_remote_copy(
                src_ref=src,
                dst_ref=dst,
                send_sem=self.sems.at[k],
                recv_sem=recv_sem,
                device_id=target,
                device_id_type=MESH,
            )

        self.started.setdefault(group, []).append((when, copy))
        guarded(when, lambda: copy().start())

    def drain(self, group):
        for when, copy in self.started.pop(group, ()):
            guarded(when, lambda copy=copy: copy().wait_send())


def guarded(when, action):
    if when is None:
        action()
    else:
        pl.when(when)(action)


def landed(dst, sem):
    pltpu.make_async_copy(dst, dst, sem).wait()


class Spread:
    def __init__(self, o, me, dp, size):
        self.o, self.me, self.dp, self.size = o, me, dp, size
        self.block = D // size
        self.sends = Sends(o.w_send)
        self.outs = Sends(o.dw_send)
        self.own = (dp, dp ^ 2, dp ^ 4, dp ^ 6)
        self.now, self.free, self.state = 0.0, {}, {}


    def shard(self, j, d, part):
        rows = pl.ds(pl.multiple_of(d * self.block, self.block), self.block)
        return self.o.w.at[j, rows, pl.ds(part * 2 * D, 2 * D)]

    def send_shard(self, j, d, part, section, dp, when=None):
        ref = self.shard(j, d, part)
        self.sends.push("w", ref, ref, self.o.w_recv.at[j, part, d], (section, dp), when)

    def wait_shard(self, j, d, part):
        landed(self.shard(j, d, part), self.o.w_recv.at[j, part, d])

    def begin(self):
        o, me, dp = self.o, self.me, self.dp
        rows = pl.ds(pl.multiple_of(dp * self.block, self.block), self.block)
        load = pltpu.make_async_copy(o.weight.at[0], o.w.at[me, rows, :], o.load_sem.at[1])
        load.start()
        width = o.bias_in.shape[1]
        bias = jnp.concatenate([o.bias_in[...].astype(F32), jnp.zeros((1, 3 * D - width), F32)], axis=1)
        bias = pltpu.roll(jnp.broadcast_to(bias, (8, 3 * D)), dp * width, 1)
        width = o.norm_in.shape[2]
        norm = jnp.concatenate([o.norm_in[0].astype(F32), jnp.zeros((2, D - width), F32)], axis=1)
        norm = pltpu.roll(jnp.concatenate([norm, jnp.zeros((6, D), F32)], axis=0), dp * width, 1)
        for k in range(3):
            o.parts[dp, k : k + 1, :] = bias[0:1, k * D : k * D + D]
        o.parts[dp, 3:5, :] = norm[0:2]
        o.parts[dp, 5:8, :] = jnp.zeros((3, D), F32)
        load.wait()

    def spread_own(self, d, part):
        me, dp = self.me, self.dp
        self.send_shard(me, d, part, me ^ 1, dp)
        self.send_shard(me, d, part, me ^ 2, dp)
        self.send_shard(me, d, part, me, dp ^ 1)

    def pass_on(self, r, d):
        me, dp = self.me, self.dp
        for part in range(2):
            self.wait_shard(me ^ r, d, part)
            self.send_shard(me ^ r, d, part, me ^ (3 - r), dp)
            self.send_shard(me ^ r, d, part, me, dp ^ 1)

    def first(self):
        o, me, dp = self.o, self.me, self.dp
        d0, d1, d2, d3 = self.own
        for part in range(2):
            self.send_shard(me, d0, part, me, d2)
            self.send_shard(me, d0, part, me, d1)
            self.spread_own(d0, part)
        for k in range(1, self.size):
            self.sends.push("w", o.parts.at[dp], o.parts.at[dp], o.parts_recv.at[dp], (me, dp ^ k))
        for part in range(2):
            self.wait_shard(me, d1, part)
            self.spread_own(d1, part)
        for part in range(2):
            self.wait_shard(me, d2, part)
            self.send_shard(me, d2, part, me, d1)
            self.spread_own(d2, part)
        self.pass_on(1, d0)
        for k in range(1, self.size):
            landed(o.parts.at[dp ^ k], o.parts_recv.at[dp ^ k])
        o.par[me, :, :] = jnp.sum(o.parts[...], axis=0)
        for r in range(1, SECTIONS):
            self.sends.push("w", o.par.at[me], o.par.at[me], o.par_recv.at[me], (me ^ r, dp))
        self.pass_on(2, d1)
        for part in range(2):
            self.wait_shard(me, d3, part)
            self.spread_own(d3, part)
        self.pass_on(1, d2)
        self.pass_on(2, d3)
        self.todo = {1: [d1, d3], 2: [d0, d2], 3: [d0, d1, d2, d3]}
        for r in range(1, SECTIONS):
            landed(o.par.at[me ^ r], o.par_recv.at[me ^ r])
        self.settle(0)

    def settle(self, j):
        me, dp = self.me, self.dp
        pieces = [(d, part) for d in self.own for part in range(2)]
        for r, shards_left in self.todo.items():
            left = [(d, part) for d, part in pieces if any(d is e for e in shards_left)]

            @pl.when(me ^ r == j)
            def _(left=left):
                for d, part in left:
                    self.wait_shard(j, d, part)

            for d, part in left:
                self.send_shard(j, d, part, me, dp ^ 1, me ^ r == j)
        for d, part in pieces:
            self.wait_shard(j, d ^ 1, part)


    def expected(self, link, cost):
        self.free[link] = max(self.free.get(link, 0.0), self.now) + cost
        return self.free[link] + 2.5

    def done(self, j, q):
        o, me, dp = self.o, self.me, self.dp
        self.passed(0.65)
        part = o.dw.at[1 - (dp & 1), :, :, pl.ds(q * 512, 512)]
        self.outs.push((j, q), part, o.land_a.at[j, q], o.a_recv.at[j, q], (me, dp ^ 1))
        self.state[j, q] = ("b", self.expected("core", 0.6))

    def passed(self, us):
        self.now += us
        for unit in sorted(self.state, key=lambda u: (-u[0], u)):
            while self.state[unit][0] != "end" and self.state[unit][1] <= self.now and self.allowed(unit):
                self.step(unit)

    def allowed(self, unit):
        stage = self.state[unit][0]
        if unit[0] >= 2 or stage == "d":
            return True
        return self.state[2, 3][0] > ("c" if stage == "b" else "d")

    def landing(self, unit):
        o = self.o
        j, q = unit
        if j >= 2:
            return o.land_b.at[j - 2, q], o.land_c.at[j - 2, q]
        columns = pl.ds(q * 512, 512)
        return o.w.at[3, pl.ds(128 * j, 128), columns], o.w.at[3, pl.ds(256 + 64 * j, 64), columns]

    def step(self, unit):
        o, me, dp = self.o, self.me, self.dp
        j, q = unit
        core, zlow, zhigh = dp & 1, (dp >> 1) & 1, dp >> 2
        stage = self.state[unit][0]
        half, (land_b, land_c) = o.land_a.at[j, q], self.landing(unit)
        if stage == "b":
            landed(half, o.a_recv.at[j, q])
            mine = o.dw[core, :, :, q * 512 : q * 512 + 512]
            half[...] = (half[...].astype(F32) + mine.astype(F32)).astype(BF)
            self.outs.drain(unit)
            self.outs.push("z", half.at[1 - zlow], land_b, o.b_recv.at[j, q], (me, dp ^ 2))
            self.state[unit] = ("c", self.expected("near", 5.0))
        elif stage == "c":
            landed(land_b, o.b_recv.at[j, q])
            mine = half.at[zlow]
            mine[...] = (mine[...].astype(F32) + land_b[...].astype(F32)).astype(BF)
            there = pl.ds(pl.multiple_of((1 - zhigh) * 64, 64), 64)
            self.outs.push("z", mine.at[there], land_c, o.c_recv.at[j, q], (me, dp ^ 4))
            self.state[unit] = ("d", self.expected("far", 4.0))
        else:
            landed(land_c, o.c_recv.at[j, q])
            here = pl.ds(pl.multiple_of(zhigh * 64, 64), 64)
            total = half[zlow, here, :].astype(F32) + land_c[...].astype(F32)
            mine = o.norms.at[SECTIONS - 1, pl.ds((4 * j + q) * self.block, self.block)]
            mine[...] = total.astype(BF)
            self.outs.push("d", mine, o.land_d.at[me, q], o.d_recv.at[me, q], (j, dp), me != j)

            @pl.when(me == j)
            def _():
                o.last[:, q * 512 : q * 512 + 512] = total

            self.state[unit] = ("end", 0)

    def smalls(self, j):
        o, me, dp = self.o, self.me, self.dp
        self.outs.push("s", o.small.at[j], o.sum_plane.at[me], o.sp_recv.at[me], (j, dp), me != j)

        @pl.when(me == j)
        def _():
            o.sum_plane[me, :, :] = o.small[j, :, :]

    def reuse(self, j, q):
        if self.state[j, q][0] == "b":
            if not self.allowed((j, q)):
                self.force((2, 3), "c")
            self.step((j, q))

    def force(self, unit, stage):
        while self.state[unit][0] <= stage:
            self.step(unit)

    def release(self):
        self.sends.drain("w")

    def finish(self):
        o, me, dp = self.o, self.me, self.dp
        while any(stage != "end" for stage, _ in self.state.values()):
            self.passed(0.5)
        for r in range(1, SECTIONS):
            landed(o.sum_plane.at[me ^ r], o.sp_recv.at[me ^ r])
        o.sum_dp[dp, :, :] = jnp.sum(o.sum_plane[...], axis=0)
        for k in range(1, self.size):
            self.outs.push("s", o.sum_dp.at[dp], o.sum_dp.at[dp], o.sd_recv.at[dp], (me, dp ^ k))
        for r in range(1, SECTIONS):
            for q in range(4):
                landed(o.land_d.at[me ^ r, q], o.d_recv.at[me ^ r, q])
                o.last[:, q * 512 : q * 512 + 512] += o.land_d[me ^ r, q].astype(F32)
        out = pltpu.make_async_copy(o.last, o.dweight.at[0], o.load_sem.at[2])
        out.start()
        for k in range(1, self.size):
            landed(o.sum_dp.at[dp ^ k], o.sd_recv.at[dp ^ k])
        o.dsmall[...] = jnp.sum(o.sum_dp[...], axis=0)
        out.wait()
        for group in list(self.outs.started):
            self.outs.drain(group)


class Local:
    def __init__(self, o):
        self.o = o
        self.loads = [pltpu.make_async_copy(o.weight.at[j], o.w.at[j], o.load_sem.at[1 + j]) for j in range(SECTIONS)]
        self.stores, self.counted = {}, {}

    def begin(self):
        for load in self.loads:
            load.start()

    def first(self):
        self.loads[0].wait()

    def settle(self, j):
        self.loads[j].wait()

    def done(self, j, q):
        if j not in self.counted:
            self.counted[j] = 0
        self.counted[j] += 1
        if self.counted[j] == 4:
            copy = pltpu.make_async_copy(self.o.dw, self.o.dweight.at[j], self.o.load_sem.at[1 + j])
            copy.start()
            self.stores[j] = copy

    def passed(self, us):
        pass

    def smalls(self, j):
        pass

    def release(self):
        pass

    def reuse(self, j, q):
        if j in self.stores:
            self.stores.pop(j).wait()

    def finish(self):
        for copy in self.stores.values():
            copy.wait()
        self.o.dsmall[...] = self.o.small[...]


def kernel(size, spread, *refs):
    names = INPUTS + (("bias_in", "norm_in") if spread else ("par",)) + OUTPUTS + tuple(SCRATCH)
    if spread:
        names += tuple(spread_scratch(size))
    o = Names(names, refs)
    me = lax.axis_index("section")
    dp = lax.axis_index("dp")

    barrier = pltpu.get_barrier_semaphore()
    peers = [(me ^ r, dp) for r in range(1, SECTIONS)]
    if spread:
        peers += [(me, dp ^ k) for k in range(1, size)]
    for peer in peers:
        pl.semaphore_signal(barrier, inc=1, device_id=peer, device_id_type=MESH)

    net = Spread(o, me, dp, size) if spread else Local(o)
    count = o.counts[me]
    load_x = pltpu.make_async_copy(o.inputs.at[me], o.x, o.load_sem.at[0])
    load_cot = pltpu.make_async_copy(o.cot.at[me], o.igs.at[1], o.load_sem.at[5])
    ys = [o.ys.at[0], o.ys.at[1], o.ys.at[2], o.igs.at[0]]
    igs = [o.norms.at[1], o.igs.at[1], o.igs.at[2], o.igs.at[3]]
    dw = o.dw
    load_x.start()
    load_cot.start()
    net.begin()
    pl.semaphore_wait(barrier, len(peers))

    def deliver(block, out, j, send, recv, action):
        @pl.when(me == j)
        def _():
            if action == "start":
                pltpu.make_async_copy(block, out.at[j], recv.at[j]).start()

        @pl.when(me != j)
        def _():
            copy = pltpu.make_async_remote_copy(
                src_ref=block,
                dst_ref=out.at[me],
                send_sem=send.at[j],
                recv_sem=recv.at[me],
                device_id=(j, dp),
                device_id_type=MESH,
            )
            copy.start() if action == "start" else copy.wait_send()

    keep = pltpu.make_async_copy(o.probs, o.kept, o.load_sem.at[6])
    bring = pltpu.make_async_copy(o.kept, o.probs, o.load_sem.at[7])

    load_x.wait()
    net.first()
    for j in range(SECTIONS):
        layer = j // 2
        h = o.x if j == 0 else ys[j - 1]
        w, par, y, normed = o.w.at[j], o.par.at[j], ys[j], o.norms.at[j]
        if j > 0:
            net.settle(j)
        if j % 2 == 0:
            if j == 2:
                keep.wait()

            def between(step):
                pass

            attend_forward(
                j, h, w, par, count, o.qkvs.at[layer], o.probs, o.atts.at[layer], o.stat, normed, y, between
            )
            if j == 0:
                keep.start()
        else:
            f = o.ffs.at[layer]
            feed_forward(j, h, w, par, count, f.at[:, :FF], f.at[:, FF:], o.stat, normed, y)
        deliver(y, o.acts, j, o.act_send, o.act_recv, "start")

    load_cot.wait()
    for j in reversed(range(SECTIONS)):
        layer = j // 2
        h = o.x if j == 0 else ys[j - 1]
        w, par, normed = o.w.at[j], o.par.at[j], o.norms.at[j]
        ig, small = igs[j], o.small.at[j]

        def gy_of(r, j=j):
            rows = pl.ds(r, TILE)
            if j == SECTIONS - 1:
                return o.igs[1, rows, :].astype(F32) * live_rows(count, r, TILE)
            return o.igs[j + 1, rows, :].astype(F32)

        f = o.ffs.at[layer]

        def done(q, j=j):
            net.done(j, q)

        def clear(q, j=j):
            if j + 1 < SECTIONS:
                net.reuse(j + 1, q)

        if j == 2:
            net.release()
        if j % 2 == 0:
            if j == 0:
                bring.wait()
            pool = o.ffs.at[1]
            gqkv, gatt = pool.at[:, : 3 * D], pool.at[:, 3 * D :]
            attend_backward(
                j, h, gy_of, w, par, o.qkvs.at[layer], o.probs, o.atts.at[layer], o.stat, normed, o.gb, gatt, gqkv,
                ig, small, dw, clear, done, net.passed,
            )
            if j == 2:
                bring.start()
        else:
            feed_backward(j, gy_of, w, par, f.at[:, :FF], f.at[:, FF:], o.stat, normed, o.gb, ig, small)
        deliver(ig, o.grads, j, o.ig_send, o.ig_recv, "start")
        net.smalls(j)
        net.passed(2.0 if j % 2 == 0 else 3.8)
        if j % 2 == 0:
            attend_weights(gqkv, normed, dw, clear, done)
        else:
            feed_weights(h, f.at[:, :FF], f.at[:, FF:], o.gb, normed, dw, clear, done)

    net.finish()
    for j in range(SECTIONS):
        deliver(ys[j], o.acts, j, o.act_send, o.act_recv, "sent")
        deliver(igs[j], o.grads, j, o.ig_send, o.ig_recv, "sent")
    for n in range(SECTIONS):
        landed(o.acts.at[n], o.act_recv.at[n])
        landed(o.grads.at[n], o.ig_recv.at[n])


def finish_kernel(acts, grads, dweight, dsmall, acts_out, grads_out, dweight_out, db, dn, rows, last, sems):
    moves = []
    for n in range(SECTIONS):
        for begin in range(0, ROWS, PIECE):
            part = pl.ds(begin, PIECE)
            moves.append((acts.at[n, part], rows.at[2 * n, part], acts_out.at[0, n, part]))
            moves.append((grads.at[n, part], rows.at[2 * n + 1, part], grads_out.at[0, n, part]))
    moves.append((dweight, last, dweight_out))
    ins = [pltpu.make_async_copy(src, mid, sems.at[0, k]) for k, (src, mid, _) in enumerate(moves)]
    copies = [pltpu.make_async_copy(mid, dst, sems.at[1, k]) for k, (_, mid, dst) in enumerate(moves)]
    for copy in ins:
        copy.start()
    for k, copy in enumerate(ins):
        copy.wait()
        copies[k].start()
    dp = lax.axis_index("dp")
    width = db.shape[1]
    bias = jnp.concatenate([dsmall[k : k + 1, :] for k in range(3)], axis=1)
    bias = pltpu.roll(jnp.broadcast_to(bias, (8, 3 * D)), 3 * D - dp * width, 1)
    db[...] = bias[0:1, 0:width]
    width = dn.shape[2]
    norm = pltpu.roll(dsmall[...], D - dp * width, 1)
    dn[0, :, :] = norm[3:5, 0:width]
    for copy in copies:
        copy.wait()


def shards(inputs, cotangent, query_counts, section_weight, section_bias, section_norm):
    size = lax.axis_size("dp")
    block = section_weight.shape[1]
    spread = size == 8
    anywhere = pl.BlockSpec(memory_space=pl.ANY)
    whole = pl.BlockSpec(memory_space=pltpu.VMEM)

    if spread:
        weight = section_weight
        small = [section_bias, section_norm]
        grad_shapes = [((1, block, 4 * D), F32), ((8, D), F32)]
    else:

        def gathered(v, axis):
            v = lax.all_gather(v, "dp", axis=axis, tiled=True)
            return lax.all_gather(v, "section", axis=0, tiled=True)

        weight = gathered(section_weight, 1)
        bias = gathered(section_bias, 1)
        norm = gathered(section_norm, 2)
        par = jnp.concatenate([bias.reshape(SECTIONS, 3, D), norm, jnp.zeros((SECTIONS, 3, D), BF)], axis=1).astype(F32)
        small = [par]
        grad_shapes = [((SECTIONS, 2, 2, 128, 4 * D), BF), ((SECTIONS, 8, D), F32)]

    out_shapes = [((SECTIONS, ROWS, D), BF)] * 2 + grad_shapes + [((HEADS, ROWS, CTX), BF)]
    scratch = list(SCRATCH.values())
    if spread:
        scratch += list(spread_scratch(size).values())
    results = pl.pallas_call(
        functools.partial(kernel, size, spread),
        out_shape=[jax.ShapeDtypeStruct(*s) for s in out_shapes],
        in_specs=[anywhere, anywhere, pl.BlockSpec(memory_space=pltpu.SMEM), anywhere] + [whole] * len(small),
        out_specs=[anywhere, anywhere, anywhere, whole, anywhere],
        scratch_shapes=scratch,
        compiler_params=pltpu.CompilerParams(
            collective_id=0, has_side_effects=True, vmem_limit_bytes=63 * MIB
        ),
    )(inputs, cotangent, query_counts, weight, *small)
    acts, grads, dweight, dsmall = results[:4]

    if spread:
        return pl.pallas_call(
            finish_kernel,
            out_shape=[
                jax.ShapeDtypeStruct((1,) + acts.shape, BF),
                jax.ShapeDtypeStruct((1,) + grads.shape, BF),
                jax.ShapeDtypeStruct(dweight.shape, F32),
                jax.ShapeDtypeStruct(section_bias.shape, F32),
                jax.ShapeDtypeStruct(section_norm.shape, F32),
            ],
            in_specs=[anywhere, anywhere, anywhere, whole],
            out_specs=[anywhere, anywhere, anywhere, whole, whole],
            scratch_shapes=[
                vm(2 * SECTIONS, ROWS, D),
                vm(*dweight.shape, dtype=F32),
                pltpu.SemaphoreType.DMA((2, 2 * SECTIONS * (ROWS // PIECE) + 1)),
            ],
            compiler_params=pltpu.CompilerParams(vmem_limit_bytes=62 * MIB),
        )(acts, grads, dweight, dsmall)

    def scattered(v, axis):
        v = lax.psum_scatter(v, "dp", scatter_dimension=axis, tiled=True)
        return lax.psum_scatter(v, "section", scatter_dimension=0, tiled=True)

    dweight = dweight.reshape(SECTIONS, 2, 2, 2, 64, 4 * D).transpose(0, 3, 2, 1, 4, 5)
    dw = scattered(dweight.reshape(SECTIONS, D, 4 * D), 1).astype(F32)
    db = scattered(dsmall[:, :3].reshape(SECTIONS, 3 * D), 1)
    dn = scattered(dsmall[:, 3:5], 2)
    return acts[None], grads[None], dw, db, dn


def solution(mesh):
    return jax.shard_map(
        shards,
        mesh=mesh,
        in_specs=(
            P("dp", None, None),
            P("dp", None, None),
            P("dp"),
            P("section", "dp", None),
            P("section", "dp"),
            P("section", None, "dp"),
        ),
        out_specs=(
            P("section", "dp", None, None),
            P("section", "dp", None, None),
            P("section", "dp", None),
            P("section", "dp"),
            P("section", None, "dp"),
        ),
        check_vma=False,
    )
```

```python
import functools
import math

import jax
import jax.numpy as jnp
from jax import lax
from jax.experimental import pallas as pl
from jax.experimental.pallas import tpu as pltpu
from jax.sharding import PartitionSpec as P

D = 512
HEADS = 4
HEAD = 128
FF = 1024
CTX = 896
ROWS = 1024
SECTIONS = 4
PIECE = 1024
TILE = 256
F32 = jnp.float32
BF = jnp.bfloat16
LOG2E = math.log2(math.e)
MESH = pl.DeviceIdType.MESH
MIB = 1 << 20


def dot(a, b):
    return lax.dot_general(a, b, (((1,), (0,)), ((), ())), preferred_element_type=F32)


def dot_t(a, b):
    return lax.dot_general(a, b, (((1,), (1,)), ((), ())), preferred_element_type=F32)


def t_dot(a, b):
    return lax.dot_general(a, b, (((0,), (0,)), ((), ())), preferred_element_type=F32)


def colsum(x):
    return jnp.sum(x, axis=0, keepdims=True)


def rows_loop(total, step, body):
    def one(i, carry):
        body(pl.multiple_of(i * step, step))
        return carry

    lax.fori_loop(0, total // step, one, 0)


LANE_RSTD = 0
LANE_NORMAL = 8
LANE_INNER = 16


def norm_forward(res, par):
    mean = jnp.mean(res, axis=-1, keepdims=True)
    center = res - mean
    inverse = lax.rsqrt(jnp.mean(center * center, axis=-1, keepdims=True) + 1e-5)
    normed = center * inverse
    return normed * par[3:4, :] + par[4:5, :], normed, inverse


def norm_backward(gy, normed, inverse, par):
    u = gy * par[3:4, :]
    m1 = jnp.mean(u, axis=-1, keepdims=True)
    m2 = jnp.mean(u * normed, axis=-1, keepdims=True)
    return inverse * (u - m1 - normed * m2)


def live_rows(count, begin, n):
    ids = lax.broadcasted_iota(jnp.int32, (n, 1), 0) + begin
    return jnp.where(ids < CTX + count, 1.0, 0.0).astype(F32)


def gelu_parts(z):
    d = 1.0 + (0.3275911 / math.sqrt(2.0)) * jnp.abs(z)
    t = pltpu.reciprocal(d, approx=True)
    t = t * (2.0 - d * t)
    e = jnp.exp2(z * z * (-0.5 * LOG2E))
    a = [0.254829592, -0.284496736, 1.421413741, -1.453152027, 1.061405429]
    a = [0.5 * v for v in a]
    tail = t * (a[0] + t * (a[1] + t * (a[2] + t * (a[3] + t * a[4])))) * e
    phi = jnp.where(z >= 0, 1.0 - tail, tail)
    return z * phi, phi + z * e * (1.0 / math.sqrt(2 * math.pi))


def ahead(items, first, second):
    ready = first(items[0])
    for i, item in enumerate(items):
        now = ready
        if i + 1 < len(items):
            ready = first(items[i + 1])
        second(item, now)


def finish_forward(j, res, par, count, begin, normed, stat, y):
    rows = pl.ds(begin, res.shape[0])
    out, unit, inverse = norm_forward(res, par)
    out = out * live_rows(count, begin, res.shape[0])
    y[rows, :] = out.astype(BF)
    normed[rows, :] = unit.astype(BF)
    stat[rows, LANE_RSTD + j : LANE_RSTD + j + 1] = inverse


def attend_forward(j, h, w, par, count, qkv, probs, att, stat, normed, y, between):
    factor = LOG2E / math.sqrt(HEAD)
    lane = LANE_NORMAL + 2 * j
    x = h[...]
    for c in range(0, 3 * D, 256):
        z = dot(x, w[:, c : c + 256])
        if c < D:
            z = (z + par[0:1, c : c + 256]) * factor
        elif c >= 2 * D:
            z = z + par[1:2, c - 2 * D : c - 2 * D + 256]
        qkv[:, c : c + 256] = z.astype(BF)
    between(0)
    step = 512

    def score(item):
        r, hd = item
        c = hd * HEAD
        return dot_t(qkv[pl.ds(r, step), c : c + HEAD], qkv[0:CTX, D + c : D + c + HEAD])

    def attend(item, s):
        r, hd = item
        c = hd * HEAD
        rows = pl.ds(r, step)
        e = jnp.exp2(s - jnp.max(s, axis=-1, keepdims=True))
        normal = 1.0 / jnp.sum(e, axis=-1, keepdims=True)
        low = e.astype(BF)
        probs[hd, rows, :] = low
        stat[rows, lane + hd : lane + hd + 1] = normal
        o = dot(low, qkv[0:CTX, 2 * D + c : 2 * D + c + HEAD])
        att[rows, c : c + HEAD] = (o * normal).astype(BF)
        if hd == HEADS - 1:
            for t in range(0, step, TILE):
                q = r + t
                out = pl.ds(q, TILE)
                res = dot(att[out, :], w[:, 3 * D : 4 * D]) + par[2:3, :] + h[out, :].astype(F32)
                finish_forward(j, res, par, count, q, normed, stat, y)

    ahead([(r, hd) for r in range(0, ROWS, step) for hd in range(HEADS)], score, attend)
    between(1)


def feed_forward(j, h, w, par, count, act, slope, stat, normed, y):
    width = 512

    def first(item):
        r, k = item
        return dot(h[r : r + TILE, :], w[:, k * width : (k + 1) * width])

    def second(item, z):
        r, k = item
        rows = pl.ds(r, TILE)
        c = k * width
        g, dg = gelu_parts(z + par[k : k + 1, :])
        act[rows, c : c + width] = g.astype(BF)
        slope[rows, c : c + width] = dg.astype(BF)
        if k == 1:
            res = dot_t(act[rows, :], w[:, FF:]) + par[2:3, :] + h[rows, :].astype(F32)
            finish_forward(j, res, par, count, r, normed, stat, y)

    ahead([(r, k) for r in range(0, ROWS, TILE) for k in range(2)], first, second)


def start_backward(j, r, gy, par, normed, stat, gb, small):
    rows = pl.ds(r, TILE)
    unit = normed[rows, :].astype(F32)
    gres = norm_backward(gy, unit, stat[rows, LANE_RSTD + j : LANE_RSTD + j + 1], par)
    small[3:4, :] += colsum(gy * unit)
    small[4:5, :] += colsum(gy)
    low = gres.astype(BF)
    gb[rows, :] = low
    small[2:3, :] += colsum(low.astype(F32))
    return low


def feed_backward(j, gy_of, w, par, act, slope, stat, normed, gb, ig, small):
    small[...] = jnp.zeros(small.shape, F32)

    def first(r):
        low = start_backward(j, r, gy_of(r), par, normed, stat, gb, small)
        return [dot(low, w[:, FF + c : FF + c + 512]) for c in (0, 512)]

    def second(r, gas):
        rows = pl.ds(r, TILE)
        for k, ga in enumerate(gas):
            c = k * 512
            gp = (ga * slope[rows, c : c + 512].astype(F32)).astype(BF)
            slope[rows, c : c + 512] = gp
            small[k : k + 1, :] += colsum(gp.astype(F32))
        ig[rows, :] = (gb[rows, :].astype(F32) + dot_t(slope[rows, :], w[:, 0:FF])).astype(BF)

    ahead(list(range(0, ROWS, TILE)), first, second)


def flipped(flip, v):
    for r in (0, 512):
        flip[r : r + 512, :] = v[r : r + 512, :].T


def put_weights(dw, chunk, flip, v, c=0):
    z = dot(flip[0:512, :], v[0:512, c : c + 512]) + dot(flip[512:1024, :], v[512:1024, c : c + 512])
    z = z.astype(BF)
    c = chunk * 512
    for d in range(8):
        high = (d >> 2) * 64
        dw[d & 1, (d >> 1) & 1, high : high + 64, c : c + 512] = z[d * 64 : d * 64 + 64]


def feed_weights(h, act, gpre, gb, flip, dw, clear, done):
    flipped(flip, h)
    for k in range(2):
        clear(k)
        put_weights(dw, k, flip, gpre, k * 512)
        done(k)
    flipped(flip, gb)
    for k in range(2):
        clear(2 + k)
        put_weights(dw, 2 + k, flip, act, k * 512)
        done(2 + k)


def attend_backward(j, h, gy_of, w, par, qkv, probs, att, stat, normed, gb, gatt, gqkv, ig, small, dw, clear,
                    done, tick):
    lane = LANE_NORMAL + 2 * j
    small[...] = jnp.zeros(small.shape, F32)

    def first(r):
        low = start_backward(j, r, gy_of(r), par, normed, stat, gb, small)
        return dot_t(low, w[:, 3 * D : 4 * D])

    def second(r, ga):
        rows = pl.ds(r, TILE)
        a = att[rows, :].astype(F32)
        for hd in range(HEADS):
            c = hd * HEAD
            g = ga[:, c : c + HEAD] * stat[rows, lane + hd : lane + hd + 1]
            gatt[rows, c : c + HEAD] = g.astype(BF)
            stat[rows, LANE_INNER + hd : LANE_INNER + hd + 1] = jnp.sum(
                g * a[:, c : c + HEAD], axis=-1, keepdims=True
            )

    ahead(list(range(0, ROWS, TILE)), first, second)
    tick(3.0)
    flipped(normed, att)
    clear(3)
    put_weights(dw, 3, normed, gb)
    done(3)
    flipped(normed, h)
    gqkv[CTX:ROWS, D : 3 * D] = jnp.zeros((ROWS - CTX, 2 * D), BF)

    def values(hd, carry):
        lanes = pl.ds(pl.multiple_of(hd * HEAD, HEAD), HEAD)
        gv = t_dot(gatt[:, lanes], probs[hd])
        gqkv[0:CTX, pl.ds(pl.multiple_of(2 * D + hd * HEAD, HEAD), HEAD)] = gv.T.astype(BF)
        return carry

    lax.fori_loop(0, HEADS, values, 0)
    tick(1.0)
    clear(2)
    put_weights(dw, 2, normed, gqkv, 2 * D)
    done(2)
    step = 512

    def first(item):
        hd, r = item
        c = hd * HEAD
        return dot_t(gatt[r : r + step, c : c + HEAD], qkv[0:CTX, 2 * D + c : 2 * D + c + HEAD])

    def second(item, gp):
        hd, r = item
        c = hd * HEAD
        rows = pl.ds(r, step)
        inner = stat[rows, LANE_INNER + hd : LANE_INNER + hd + 1]
        gs = (probs[hd, rows, :].astype(F32) * (gp - inner)).astype(BF)
        probs[hd, rows, :] = gs
        gq = dot(gs, qkv[0:CTX, D + c : D + c + HEAD])
        gqkv[rows, c : c + HEAD] = (gq * (1.0 / math.sqrt(HEAD))).astype(BF)

    for pair in (0, 2):
        ahead([(hd, r) for hd in (pair, pair + 1) for r in range(0, ROWS, step)], first, second)
        tick(2.3)

    def keys(hd, carry):
        lanes = pl.ds(pl.multiple_of(hd * HEAD, HEAD), HEAD)
        gk = t_dot(qkv[:, lanes], probs[hd])
        gqkv[0:CTX, pl.ds(pl.multiple_of(D + hd * HEAD, HEAD), HEAD)] = (gk * (1.0 / LOG2E)).T.astype(BF)
        return carry

    lax.fori_loop(0, HEADS, keys, 0)
    tick(1.8)
    for r in range(0, ROWS, TILE):
        rows = pl.ds(r, TILE)
        ig[rows, :] = (gb[rows, :].astype(F32) + dot_t(gqkv[rows, :], w[:, 0 : 3 * D])).astype(BF)
        small[0:1, :] += colsum(gqkv[rows, 0:D].astype(F32))
        small[1:2, :] += colsum(gqkv[rows, 2 * D : 3 * D].astype(F32))


def attend_weights(gqkv, flip, dw, clear, done):
    for k in (1, 0):
        clear(k)
        put_weights(dw, k, flip, gqkv, k * D)
        done(k)


def vm(*shape, dtype=BF):
    return pltpu.VMEM(shape, dtype)


SCRATCH = dict(
    x=vm(ROWS, D),
    w=vm(SECTIONS, D, 4 * D),
    ys=vm(SECTIONS - 1, ROWS, D),
    igs=vm(SECTIONS, ROWS, D),
    norms=vm(SECTIONS, ROWS, D),
    qkvs=vm(2, ROWS, 3 * D),
    atts=vm(2, ROWS, D),
    ffs=vm(2, ROWS, 2 * FF),
    probs=vm(HEADS, ROWS, CTX),
    stat=vm(ROWS, 128, dtype=F32),
    gb=vm(ROWS, D),
    dw=vm(2, 2, 128, 4 * D),
    small=vm(SECTIONS, 8, D, dtype=F32),
    load_sem=pltpu.SemaphoreType.DMA((8,)),
    act_send=pltpu.SemaphoreType.DMA((SECTIONS,)),
    act_recv=pltpu.SemaphoreType.DMA((SECTIONS,)),
    ig_send=pltpu.SemaphoreType.DMA((SECTIONS,)),
    ig_recv=pltpu.SemaphoreType.DMA((SECTIONS,)),
)


def spread_scratch(size):
    sem = pltpu.SemaphoreType.DMA
    return dict(
        parts=vm(size, 8, D, dtype=F32),
        par=vm(SECTIONS, 8, D, dtype=F32),
        sum_plane=vm(SECTIONS, 8, D, dtype=F32),
        sum_dp=vm(size, 8, D, dtype=F32),
        land_a=vm(SECTIONS, 4, 2, 2 * (D // size), 512),
        land_b=vm(2, 4, 2 * (D // size), 512),
        land_c=vm(2, 4, D // size, 512),
        land_d=vm(SECTIONS, 4, D // size, 512),
        last=vm(D // size, 4 * D, dtype=F32),
        w_recv=sem((SECTIONS, 2, size)),
        w_send=sem((160,)),
        parts_recv=sem((size,)),
        par_recv=sem((SECTIONS,)),
        a_recv=sem((SECTIONS, 4)),
        b_recv=sem((SECTIONS, 4)),
        c_recv=sem((SECTIONS, 4)),
        d_recv=sem((SECTIONS, 4)),
        sp_recv=sem((SECTIONS,)),
        sd_recv=sem((size,)),
        dw_send=sem((128,)),
    )


class Names:
    def __init__(self, names, refs):
        self.__dict__.update(zip(names, refs, strict=True))


INPUTS = ("inputs", "cot", "counts", "weight")
OUTPUTS = ("acts", "grads", "dweight", "dsmall", "kept")


class Sends:
    def __init__(self, sems):
        self.sems, self.used, self.started = sems, 0, {}

    def push(self, group, src, dst, recv_sem, target, when=None):
        k = self.used
        self.used += 1
        assert k < self.sems.shape[0]

        def copy():
            return pltpu.make_async_remote_copy(
                src_ref=src,
                dst_ref=dst,
                send_sem=self.sems.at[k],
                recv_sem=recv_sem,
                device_id=target,
                device_id_type=MESH,
            )

        self.started.setdefault(group, []).append((when, copy))
        guarded(when, lambda: copy().start())

    def drain(self, group):
        for when, copy in self.started.pop(group, ()):
            guarded(when, lambda copy=copy: copy().wait_send())


def guarded(when, action):
    if when is None:
        action()
    else:
        pl.when(when)(action)


def landed(dst, sem):
    pltpu.make_async_copy(dst, dst, sem).wait()


class Spread:
    def __init__(self, o, me, dp, size):
        self.o, self.me, self.dp, self.size = o, me, dp, size
        self.block = D // size
        self.sends = Sends(o.w_send)
        self.outs = Sends(o.dw_send)
        self.own = (dp, dp ^ 2, dp ^ 4, dp ^ 6)
        self.now, self.free, self.state = 0.0, {}, {}


    def shard(self, j, d, part):
        rows = pl.ds(pl.multiple_of(d * self.block, self.block), self.block)
        return self.o.w.at[j, rows, pl.ds(part * 2 * D, 2 * D)]

    def send_shard(self, j, d, part, section, dp, when=None):
        ref = self.shard(j, d, part)
        self.sends.push("w", ref, ref, self.o.w_recv.at[j, part, d], (section, dp), when)

    def wait_shard(self, j, d, part):
        landed(self.shard(j, d, part), self.o.w_recv.at[j, part, d])

    def begin(self):
        o, me, dp = self.o, self.me, self.dp
        rows = pl.ds(pl.multiple_of(dp * self.block, self.block), self.block)
        load = pltpu.make_async_copy(o.weight.at[0], o.w.at[me, rows, :], o.load_sem.at[1])
        load.start()
        width = o.bias_in.shape[1]
        bias = jnp.concatenate([o.bias_in[...].astype(F32), jnp.zeros((1, 3 * D - width), F32)], axis=1)
        bias = pltpu.roll(jnp.broadcast_to(bias, (8, 3 * D)), dp * width, 1)
        width = o.norm_in.shape[2]
        norm = jnp.concatenate([o.norm_in[0].astype(F32), jnp.zeros((2, D - width), F32)], axis=1)
        norm = pltpu.roll(jnp.concatenate([norm, jnp.zeros((6, D), F32)], axis=0), dp * width, 1)
        for k in range(3):
            o.parts[dp, k : k + 1, :] = bias[0:1, k * D : k * D + D]
        o.parts[dp, 3:5, :] = norm[0:2]
        o.parts[dp, 5:8, :] = jnp.zeros((3, D), F32)
        load.wait()

    def spread_own(self, d, part):
        me, dp = self.me, self.dp
        self.send_shard(me, d, part, me ^ 1, dp)
        self.send_shard(me, d, part, me ^ 2, dp)
        self.send_shard(me, d, part, me, dp ^ 1)

    def pass_on(self, r, d):
        me, dp = self.me, self.dp
        for part in range(2):
            self.wait_shard(me ^ r, d, part)
            self.send_shard(me ^ r, d, part, me ^ (3 - r), dp)
            self.send_shard(me ^ r, d, part, me, dp ^ 1)

    def first(self):
        o, me, dp = self.o, self.me, self.dp
        d0, d1, d2, d3 = self.own
        for part in range(2):
            self.send_shard(me, d0, part, me, d2)
            self.send_shard(me, d0, part, me, d1)
            self.spread_own(d0, part)
        for k in range(1, self.size):
            self.sends.push("w", o.parts.at[dp], o.parts.at[dp], o.parts_recv.at[dp], (me, dp ^ k))
        for part in range(2):
            self.wait_shard(me, d1, part)
            self.spread_own(d1, part)
        for part in range(2):
            self.wait_shard(me, d2, part)
            self.send_shard(me, d2, part, me, d1)
            self.spread_own(d2, part)
        self.pass_on(1, d0)
        for k in range(1, self.size):
            landed(o.parts.at[dp ^ k], o.parts_recv.at[dp ^ k])
        o.par[me, :, :] = jnp.sum(o.parts[...], axis=0)
        for r in range(1, SECTIONS):
            self.sends.push("w", o.par.at[me], o.par.at[me], o.par_recv.at[me], (me ^ r, dp))
        self.pass_on(2, d1)
        for part in range(2):
            self.wait_shard(me, d3, part)
            self.spread_own(d3, part)
        self.pass_on(1, d2)
        self.pass_on(2, d3)
        self.todo = {1: [d1, d3], 2: [d0, d2], 3: [d0, d1, d2, d3]}
        for r in range(1, SECTIONS):
            landed(o.par.at[me ^ r], o.par_recv.at[me ^ r])
        self.settle(0)

    def settle(self, j):
        me, dp = self.me, self.dp
        pieces = [(d, part) for d in self.own for part in range(2)]
        for r, shards_left in self.todo.items():
            left = [(d, part) for d, part in pieces if any(d is e for e in shards_left)]

            @pl.when(me ^ r == j)
            def _(left=left):
                for d, part in left:
                    self.wait_shard(j, d, part)

            for d, part in left:
                self.send_shard(j, d, part, me, dp ^ 1, me ^ r == j)
        for d, part in pieces:
            self.wait_shard(j, d ^ 1, part)


    def expected(self, link, cost):
        self.free[link] = max(self.free.get(link, 0.0), self.now) + cost
        return self.free[link] + 2.5

    def done(self, j, q):
        o, me, dp = self.o, self.me, self.dp
        self.passed(0.65)
        part = o.dw.at[1 - (dp & 1), :, :, pl.ds(q * 512, 512)]
        self.outs.push((j, q), part, o.land_a.at[j, q], o.a_recv.at[j, q], (me, dp ^ 1))
        self.state[j, q] = ("b", self.expected("core", 0.6))

    def passed(self, us):
        self.now += us
        for unit in sorted(self.state, key=lambda u: (-u[0], u)):
            while self.state[unit][0] != "end" and self.state[unit][1] <= self.now and self.allowed(unit):
                self.step(unit)

    def allowed(self, unit):
        stage = self.state[unit][0]
        if unit[0] >= 2 or stage == "d":
            return True
        return self.state[2, 3][0] > ("c" if stage == "b" else "d")

    def landing(self, unit):
        o = self.o
        j, q = unit
        if j >= 2:
            return o.land_b.at[j - 2, q], o.land_c.at[j - 2, q]
        columns = pl.ds(q * 512, 512)
        return o.w.at[3, pl.ds(128 * j, 128), columns], o.w.at[3, pl.ds(256 + 64 * j, 64), columns]

    def step(self, unit):
        o, me, dp = self.o, self.me, self.dp
        j, q = unit
        core, zlow, zhigh = dp & 1, (dp >> 1) & 1, dp >> 2
        stage = self.state[unit][0]
        half, (land_b, land_c) = o.land_a.at[j, q], self.landing(unit)
        if stage == "b":
            landed(half, o.a_recv.at[j, q])
            mine = o.dw[core, :, :, q * 512 : q * 512 + 512]
            half[...] = (half[...].astype(F32) + mine.astype(F32)).astype(BF)
            self.outs.drain(unit)
            self.outs.push("z", half.at[1 - zlow], land_b, o.b_recv.at[j, q], (me, dp ^ 2))
            self.state[unit] = ("c", self.expected("near", 5.0))
        elif stage == "c":
            landed(land_b, o.b_recv.at[j, q])
            mine = half.at[zlow]
            mine[...] = (mine[...].astype(F32) + land_b[...].astype(F32)).astype(BF)
            there = pl.ds(pl.multiple_of((1 - zhigh) * 64, 64), 64)
            self.outs.push("z", mine.at[there], land_c, o.c_recv.at[j, q], (me, dp ^ 4))
            self.state[unit] = ("d", self.expected("far", 4.0))
        else:
            landed(land_c, o.c_recv.at[j, q])
            here = pl.ds(pl.multiple_of(zhigh * 64, 64), 64)
            total = half[zlow, here, :].astype(F32) + land_c[...].astype(F32)
            mine = o.norms.at[SECTIONS - 1, pl.ds((4 * j + q) * self.block, self.block)]
            mine[...] = total.astype(BF)
            self.outs.push("d", mine, o.land_d.at[me, q], o.d_recv.at[me, q], (j, dp), me != j)

            @pl.when(me == j)
            def _():
                o.last[:, q * 512 : q * 512 + 512] = total

            self.state[unit] = ("end", 0)

    def smalls(self, j):
        o, me, dp = self.o, self.me, self.dp
        self.outs.push("s", o.small.at[j], o.sum_plane.at[me], o.sp_recv.at[me], (j, dp), me != j)

        @pl.when(me == j)
        def _():
            o.sum_plane[me, :, :] = o.small[j, :, :]

    def reuse(self, j, q):
        if self.state[j, q][0] == "b":
            if not self.allowed((j, q)):
                self.force((2, 3), "c")
            self.step((j, q))

    def force(self, unit, stage):
        while self.state[unit][0] <= stage:
            self.step(unit)

    def release(self):
        self.sends.drain("w")

    def finish(self):
        o, me, dp = self.o, self.me, self.dp
        while any(stage != "end" for stage, _ in self.state.values()):
            self.passed(0.5)
        for r in range(1, SECTIONS):
            landed(o.sum_plane.at[me ^ r], o.sp_recv.at[me ^ r])
        o.sum_dp[dp, :, :] = jnp.sum(o.sum_plane[...], axis=0)
        for k in range(1, self.size):
            self.outs.push("s", o.sum_dp.at[dp], o.sum_dp.at[dp], o.sd_recv.at[dp], (me, dp ^ k))
        for r in range(1, SECTIONS):
            for q in range(4):
                landed(o.land_d.at[me ^ r, q], o.d_recv.at[me ^ r, q])
                o.last[:, q * 512 : q * 512 + 512] += o.land_d[me ^ r, q].astype(F32)
        out = pltpu.make_async_copy(o.last, o.dweight.at[0], o.load_sem.at[2])
        out.start()
        for k in range(1, self.size):
            landed(o.sum_dp.at[dp ^ k], o.sd_recv.at[dp ^ k])
        o.dsmall[...] = jnp.sum(o.sum_dp[...], axis=0)
        out.wait()
        for group in list(self.outs.started):
            self.outs.drain(group)


class Local:
    def __init__(self, o):
        self.o = o
        self.loads = [pltpu.make_async_copy(o.weight.at[j], o.w.at[j], o.load_sem.at[1 + j]) for j in range(SECTIONS)]
        self.stores, self.counted = {}, {}

    def begin(self):
        for load in self.loads:
            load.start()

    def first(self):
        self.loads[0].wait()

    def settle(self, j):
        self.loads[j].wait()

    def done(self, j, q):
        if j not in self.counted:
            self.counted[j] = 0
        self.counted[j] += 1
        if self.counted[j] == 4:
            copy = pltpu.make_async_copy(self.o.dw, self.o.dweight.at[j], self.o.load_sem.at[1 + j])
            copy.start()
            self.stores[j] = copy

    def passed(self, us):
        pass

    def smalls(self, j):
        pass

    def release(self):
        pass

    def reuse(self, j, q):
        if j in self.stores:
            self.stores.pop(j).wait()

    def finish(self):
        for copy in self.stores.values():
            copy.wait()
        self.o.dsmall[...] = self.o.small[...]


def kernel(size, spread, *refs):
    names = INPUTS + (("bias_in", "norm_in") if spread else ("par",)) + OUTPUTS + tuple(SCRATCH)
    if spread:
        names += tuple(spread_scratch(size))
    o = Names(names, refs)
    me = lax.axis_index("section")
    dp = lax.axis_index("dp")

    barrier = pltpu.get_barrier_semaphore()
    peers = [(me ^ r, dp) for r in range(1, SECTIONS)]
    if spread:
        peers += [(me, dp ^ k) for k in range(1, size)]
    for peer in peers:
        pl.semaphore_signal(barrier, inc=1, device_id=peer, device_id_type=MESH)

    net = Spread(o, me, dp, size) if spread else Local(o)
    count = o.counts[me]
    load_x = pltpu.make_async_copy(o.inputs.at[me], o.x, o.load_sem.at[0])
    load_cot = pltpu.make_async_copy(o.cot.at[me], o.igs.at[1], o.load_sem.at[5])
    ys = [o.ys.at[0], o.ys.at[1], o.ys.at[2], o.igs.at[0]]
    igs = [o.norms.at[1], o.igs.at[1], o.igs.at[2], o.igs.at[3]]
    dw = o.dw
    load_x.start()
    load_cot.start()
    net.begin()
    pl.semaphore_wait(barrier, len(peers))

    def deliver(block, out, j, send, recv, action):
        @pl.when(me == j)
        def _():
            if action == "start":
                pltpu.make_async_copy(block, out.at[j], recv.at[j]).start()

        @pl.when(me != j)
        def _():
            copy = pltpu.make_async_remote_copy(
                src_ref=block,
                dst_ref=out.at[me],
                send_sem=send.at[j],
                recv_sem=recv.at[me],
                device_id=(j, dp),
                device_id_type=MESH,
            )
            copy.start() if action == "start" else copy.wait_send()

    keep = pltpu.make_async_copy(o.probs, o.kept, o.load_sem.at[6])
    bring = pltpu.make_async_copy(o.kept, o.probs, o.load_sem.at[7])

    load_x.wait()
    net.first()
    for j in range(SECTIONS):
        layer = j // 2
        h = o.x if j == 0 else ys[j - 1]
        w, par, y, normed = o.w.at[j], o.par.at[j], ys[j], o.norms.at[j]
        if j > 0:
            net.settle(j)
        if j % 2 == 0:
            if j == 2:
                keep.wait()

            def between(step):
                pass

            attend_forward(
                j, h, w, par, count, o.qkvs.at[layer], o.probs, o.atts.at[layer], o.stat, normed, y, between
            )
            if j == 0:
                keep.start()
        else:
            f = o.ffs.at[layer]
            feed_forward(j, h, w, par, count, f.at[:, :FF], f.at[:, FF:], o.stat, normed, y)
        deliver(y, o.acts, j, o.act_send, o.act_recv, "start")

    load_cot.wait()
    for j in reversed(range(SECTIONS)):
        layer = j // 2
        h = o.x if j == 0 else ys[j - 1]
        w, par, normed = o.w.at[j], o.par.at[j], o.norms.at[j]
        ig, small = igs[j], o.small.at[j]

        def gy_of(r, j=j):
            rows = pl.ds(r, TILE)
            if j == SECTIONS - 1:
                return o.igs[1, rows, :].astype(F32) * live_rows(count, r, TILE)
            return o.igs[j + 1, rows, :].astype(F32)

        f = o.ffs.at[layer]

        def done(q, j=j):
            net.done(j, q)

        def clear(q, j=j):
            if j + 1 < SECTIONS:
                net.reuse(j + 1, q)

        if j == 2:
            net.release()
        if j % 2 == 0:
            if j == 0:
                bring.wait()
            pool = o.ffs.at[1]
            gqkv, gatt = pool.at[:, : 3 * D], pool.at[:, 3 * D :]
            attend_backward(
                j, h, gy_of, w, par, o.qkvs.at[layer], o.probs, o.atts.at[layer], o.stat, normed, o.gb, gatt, gqkv,
                ig, small, dw, clear, done, net.passed,
            )
            if j == 2:
                bring.start()
        else:
            feed_backward(j, gy_of, w, par, f.at[:, :FF], f.at[:, FF:], o.stat, normed, o.gb, ig, small)
        deliver(ig, o.grads, j, o.ig_send, o.ig_recv, "start")
        net.smalls(j)
        net.passed(2.0 if j % 2 == 0 else 3.8)
        if j % 2 == 0:
            attend_weights(gqkv, normed, dw, clear, done)
        else:
            feed_weights(h, f.at[:, :FF], f.at[:, FF:], o.gb, normed, dw, clear, done)

    net.finish()
    for j in range(SECTIONS):
        deliver(ys[j], o.acts, j, o.act_send, o.act_recv, "sent")
        deliver(igs[j], o.grads, j, o.ig_send, o.ig_recv, "sent")
    for n in range(SECTIONS):
        landed(o.acts.at[n], o.act_recv.at[n])
        landed(o.grads.at[n], o.ig_recv.at[n])


def finish_kernel(acts, grads, dweight, dsmall, acts_out, grads_out, dweight_out, db, dn, rows, last, sems):
    moves = []
    for n in range(SECTIONS):
        for begin in range(0, ROWS, PIECE):
            part = pl.ds(begin, PIECE)
            moves.append((acts.at[n, part], rows.at[2 * n, part], acts_out.at[0, n, part]))
            moves.append((grads.at[n, part], rows.at[2 * n + 1, part], grads_out.at[0, n, part]))
    moves.append((dweight, last, dweight_out))
    ins = [pltpu.make_async_copy(src, mid, sems.at[0, k]) for k, (src, mid, _) in enumerate(moves)]
    copies = [pltpu.make_async_copy(mid, dst, sems.at[1, k]) for k, (_, mid, dst) in enumerate(moves)]
    for copy in ins:
        copy.start()
    for k, copy in enumerate(ins):
        copy.wait()
        copies[k].start()
    dp = lax.axis_index("dp")
    width = db.shape[1]
    bias = jnp.concatenate([dsmall[k : k + 1, :] for k in range(3)], axis=1)
    bias = pltpu.roll(jnp.broadcast_to(bias, (8, 3 * D)), 3 * D - dp * width, 1)
    db[...] = bias[0:1, 0:width]
    width = dn.shape[2]
    norm = pltpu.roll(dsmall[...], D - dp * width, 1)
    dn[0, :, :] = norm[3:5, 0:width]
    for copy in copies:
        copy.wait()


def shards(inputs, cotangent, query_counts, section_weight, section_bias, section_norm):
    size = lax.axis_size("dp")
    block = section_weight.shape[1]
    spread = size == 8
    anywhere = pl.BlockSpec(memory_space=pl.ANY)
    whole = pl.BlockSpec(memory_space=pltpu.VMEM)

    if spread:
        weight = section_weight
        small = [section_bias, section_norm]
        grad_shapes = [((1, block, 4 * D), F32), ((8, D), F32)]
    else:

        def gathered(v, axis):
            v = lax.all_gather(v, "dp", axis=axis, tiled=True)
            return lax.all_gather(v, "section", axis=0, tiled=True)

        weight = gathered(section_weight, 1)
        bias = gathered(section_bias, 1)
        norm = gathered(section_norm, 2)
        par = jnp.concatenate([bias.reshape(SECTIONS, 3, D), norm, jnp.zeros((SECTIONS, 3, D), BF)], axis=1).astype(F32)
        small = [par]
        grad_shapes = [((SECTIONS, 2, 2, 128, 4 * D), BF), ((SECTIONS, 8, D), F32)]

    out_shapes = [((SECTIONS, ROWS, D), BF)] * 2 + grad_shapes + [((HEADS, ROWS, CTX), BF)]
    scratch = list(SCRATCH.values())
    if spread:
        scratch += list(spread_scratch(size).values())
    results = pl.pallas_call(
        functools.partial(kernel, size, spread),
        out_shape=[jax.ShapeDtypeStruct(*s) for s in out_shapes],
        in_specs=[anywhere, anywhere, pl.BlockSpec(memory_space=pltpu.SMEM), anywhere] + [whole] * len(small),
        out_specs=[anywhere, anywhere, anywhere, whole, anywhere],
        scratch_shapes=scratch,
        compiler_params=pltpu.CompilerParams(
            collective_id=0, has_side_effects=True, vmem_limit_bytes=63 * MIB
        ),
    )(inputs, cotangent, query_counts, weight, *small)
    acts, grads, dweight, dsmall = results[:4]

    if spread:
        return pl.pallas_call(
            finish_kernel,
            out_shape=[
                jax.ShapeDtypeStruct((1,) + acts.shape, BF),
                jax.ShapeDtypeStruct((1,) + grads.shape, BF),
                jax.ShapeDtypeStruct(dweight.shape, F32),
                jax.ShapeDtypeStruct(section_bias.shape, F32),
                jax.ShapeDtypeStruct(section_norm.shape, F32),
            ],
            in_specs=[anywhere, anywhere, anywhere, whole],
            out_specs=[anywhere, anywhere, anywhere, whole, whole],
            scratch_shapes=[
                vm(2 * SECTIONS, ROWS, D),
                vm(*dweight.shape, dtype=F32),
                pltpu.SemaphoreType.DMA((2, 2 * SECTIONS * (ROWS // PIECE) + 1)),
            ],
            compiler_params=pltpu.CompilerParams(vmem_limit_bytes=62 * MIB),
        )(acts, grads, dweight, dsmall)

    def scattered(v, axis):
        v = lax.psum_scatter(v, "dp", scatter_dimension=axis, tiled=True)
        return lax.psum_scatter(v, "section", scatter_dimension=0, tiled=True)

    dweight = dweight.reshape(SECTIONS, 2, 2, 2, 64, 4 * D).transpose(0, 3, 2, 1, 4, 5)
    dw = scattered(dweight.reshape(SECTIONS, D, 4 * D), 1).astype(F32)
    db = scattered(dsmall[:, :3].reshape(SECTIONS, 3 * D), 1)
    dn = scattered(dsmall[:, 3:5], 2)
    return acts[None], grads[None], dw, db, dn


def solution(mesh):
    return jax.shard_map(
        shards,
        mesh=mesh,
        in_specs=(
            P("dp", None, None),
            P("dp", None, None),
            P("dp"),
            P("section", "dp", None),
            P("section", "dp"),
            P("section", None, "dp"),
        ),
        out_specs=(
            P("section", "dp", None, None),
            P("section", "dp", None, None),
            P("section", "dp", None),
            P("section", "dp"),
            P("section", None, "dp"),
        ),
        check_vma=False,
    )
```
